32 devices in a mesh: section: 2 (over core), ctx: 16 (over z, y, x).
Axes of the slice: x: 2, y: 2, z: 4, core: 2. Of those that a mesh axis runs over, the one named last changes fastest.
Arguments:
- tokens: bfloat16 [2, 2048, 1024], P(None, 'ctx'), may hold values from -6 to 6
- cotangent: bfloat16 [2, 2048, 1024], P(None, 'ctx'), may hold values from -6 to 6
- bounds: int32 [2, 8], replicated, may hold values from 0 to 2048, as said below
- norm_gain: bfloat16 [2, 1024], P('section'), may hold values from 0.5 to 1.5
- in_proj: bfloat16 [2, 1024, 4096], P('section'), may hold values from -0.1875 to 0.1875
- conv_kernel: bfloat16 [2, 4, 2048], P('section'), may hold values from -3 to 3
- conv_bias: bfloat16 [2, 2048], P('section'), may hold values from -3 to 3
- x_proj: bfloat16 [2, 2048, 96], P('section'), may hold values from -0.125 to 0.125
- dt_proj: bfloat16 [2, 64, 2048], P('section'), may hold values from -0.75 to 0.75
- dt_bias: bfloat16 [2, 2048], P('section'), may hold values from -9 to 1
- skip_gain: bfloat16 [2, 2048], P('section'), may hold values from 0.5 to 1.5
- out_proj: bfloat16 [2, 2048, 1024], P('section'), may hold values from -0.25 to 0.25
Outputs:
- block_out: bfloat16 [2, 2048, 1024], P('section', 'ctx')
- grad_tokens: bfloat16 [2, 2048, 1024], P('section', 'ctx')
- grad_norm_gain: float32 [2, 1024], P('section', 'ctx')
- grad_in_proj: float32 [2, 1024, 4096], P('section', 'ctx')
- grad_conv_kernel: float32 [2, 4, 2048], P('section', None, 'ctx')
- grad_conv_bias: float32 [2, 2048], P('section', 'ctx')
- grad_x_proj: float32 [2, 2048, 96], P('section', 'ctx')
- grad_dt_proj: float32 [2, 64, 2048], P('section', 'ctx')
- grad_dt_bias: float32 [2, 2048], P('section', 'ctx')
- grad_skip_gain: float32 [2, 2048], P('section', 'ctx')
- grad_out_proj: float32 [2, 2048, 1024], P('section', 'ctx')
The draws below stay inside these ranges and needn't reach their ends.
Inputs may be any that keep to these rules, and one draw needn't show every extreme that they name: Each row bounds[m] rises strictly from 0 to 2048: seven sequences. In one micro-batch, chosen by the draw, the first three sequences end within the first 128 tokens and the last three start within the last 128 tokens. In every other micro-batch the cuts lie anywhere, and the sequences are four of 128 tokens and three of 512 tokens in some order, with the first one longer and the last one shorter by the same amount, less than 64.
All inputs are finite; a program needn't handle non-finite values.
Results may differ from the reference program's by a relative error of at most 0.023.
Values may be sent and summed in bfloat16 or wider, within the bound.
A program may use at most 256 MiB of HBM per device.

```python
import jax
import jax.numpy as jnp
from jax import lax

D = 1024
E = 2048
STATE = 16
RANK = 64
TAPS = 4
TOK_CTX = 128
MICRO = 2
LAYERS = 2
MB_TOK = 2048


def spanning_row(key):
    key_head, key_tail = jax.random.split(key)
    head_cuts = jnp.sort(jax.random.permutation(key_head, TOK_CTX - 1)[:3] + 1)
    tail_cuts = jnp.sort(MB_TOK - 1 - jax.random.permutation(key_tail, TOK_CTX - 1)[:3])
    return jnp.concatenate([jnp.zeros((1,), jnp.int32), head_cuts.astype(jnp.int32), tail_cuts.astype(jnp.int32), jnp.full((1,), MB_TOK, jnp.int32)])


def packed_row(key):
    key_order, key_offset = jax.random.split(key)
    unit_len = MB_TOK // 16
    pattern = jax.random.permutation(key_order, jnp.array([1, 1, 1, 1, 4, 4, 4], jnp.int32))
    offset = jax.random.randint(key_offset, (), 1, unit_len // 2)
    cuts = jnp.cumsum(pattern)[:6] * unit_len + offset
    return jnp.concatenate([jnp.zeros((1,), jnp.int32), cuts.astype(jnp.int32), jnp.full((1,), MB_TOK, jnp.int32)])


def draw_bounds(key, part):
    key = jax.random.fold_in(key, 7)
    key_pick = jax.random.fold_in(key, 1000)
    chosen = jax.random.randint(key_pick, (), 0, MICRO)
    rows = []
    for micro_id in range(MICRO):
        row_key = jax.random.fold_in(key, micro_id)
        key_span, key_pack = jax.random.split(row_key)
        rows.append(jnp.where(chosen == micro_id, spanning_row(key_span), packed_row(key_pack)))
    return jnp.stack(rows).astype(jnp.int32)


def steps_of(stream_key, extent, cuts, low, high):
    def one(axis_at, shards_of):
        steps = jax.random.uniform(jax.random.fold_in(jax.random.fold_in(stream_key, 6), axis_at), (shards_of,), jnp.float32, low / len(cuts), high / len(cuts))
        return jnp.repeat(jnp.exp(steps), extent[axis_at] // shards_of).reshape((-1,) + (1,) * (len(extent) - axis_at - 1))

    loudness = one(*cuts[0])
    for cut in cuts[1:]:
        loudness = loudness * one(*cut)
    return loudness


def normal_values(own_key, shape, scale, reach, cuts=(), kind=jnp.bfloat16):
    values = jax.random.normal(own_key, shape, jnp.float32) * scale
    if len(cuts) > 0:
        values = steps_of(own_key, shape, cuts, -0.22, 0.18) * values
    return jnp.clip(values, min=-reach, max=reach).astype(kind)


def setup_inputs(seed: int = 0) -> dict:
    streams_of = jax.random.split(jax.random.key(seed), 13)
    return {
        "tokens": normal_values(streams_of[0], (MICRO, MB_TOK, D), 1.0, 6.0, ((1, 16),)),
        "cotangent": normal_values(streams_of[1], (MICRO, MB_TOK, D), 1.0, 6.0, ((1, 16),)),
        "bounds": draw_bounds(jax.random.fold_in(streams_of[12], 71), 0),
        "norm_gain": jnp.clip(1.0 + 0.1 * jax.random.normal(streams_of[3], (LAYERS, D), jnp.float32), 0.5, 1.5).astype(jnp.bfloat16),
        "in_proj": normal_values(streams_of[4], (LAYERS, D, 2 * E), D ** -0.5, 0.1875, ((0, 2),)),
        "conv_kernel": normal_values(streams_of[5], (LAYERS, TAPS, E), TAPS ** -0.5, 3.0, ((0, 2),)),
        "conv_bias": normal_values(streams_of[6], (LAYERS, E), 0.5, 3.0, ((0, 2),)),
        "x_proj": normal_values(streams_of[7], (LAYERS, E, RANK + 2 * STATE), E ** -0.5, 0.125, ((0, 2),)),
        "dt_proj": normal_values(streams_of[8], (LAYERS, RANK, E), RANK ** -0.5, 0.75, ((0, 2),)),
        "dt_bias": jnp.clip(-9.0 + 10.0 * jax.random.uniform(streams_of[9], (LAYERS, E), jnp.float32) ** steps_of(streams_of[9], (LAYERS, E), ((0, 2),), -0.2, 0.2), -9.0, 1.0).astype(jnp.bfloat16),
        "skip_gain": jnp.clip(0.5 + 1.0 * jax.random.uniform(streams_of[10], (LAYERS, E), jnp.float32) ** steps_of(streams_of[10], (LAYERS, E), ((0, 2),), -0.2, 0.2), 0.5, 1.5).astype(jnp.bfloat16),
        "out_proj": normal_values(streams_of[11], (LAYERS, E, D), (E // 4) ** -0.5, 0.25, ((0, 2),)),
    }


@jax.custom_vjp
def low(v):
    return lax.optimization_barrier(v.astype(jnp.bfloat16)).astype(jnp.float32)

@jax.custom_vjp
def low_back(v):
    return v

def low_keep(v):
    return (low(v), None)

def low_pass(kept, grad):
    return (grad,)

def back_keep(v):
    return (v, None)

def back_low(kept, grad):
    return (low(grad),)
low.defvjp(low_keep, low_pass)
low_back.defvjp(back_keep, back_low)

def matmul(left, right):
    return jnp.dot(left, right, precision=lax.Precision.HIGHEST, preferred_element_type=jnp.float32)

def state_run(step_size, key_vecs, query_vecs, conv_act, keep_flags):
    block_len = 64
    block_count = MB_TOK // block_len

    def token_step(carried, pieces):
        step_tok, key_tok, query_tok, act_tok, keep_tok = pieces
        decay = keep_tok * jnp.exp(-(key_tok * key_tok)[:, None] * step_tok[None, :])
        carried = decay * carried + (step_tok * act_tok)[None, :] * key_tok[:, None]
        return (carried, lax.optimization_barrier(jnp.sum(query_tok[:, None] * carried, axis=0)))

    def block_run(carried, pieces):
        return lax.scan(token_step, carried, pieces)

    def to_blocks(values):
        return values.reshape((block_count, block_len) + values.shape[1:])
    pieces = (to_blocks(step_size), to_blocks(key_vecs), to_blocks(query_vecs), to_blocks(conv_act), to_blocks(keep_flags))
    unused, outputs = lax.scan(jax.checkpoint(block_run), jnp.zeros((STATE, E), jnp.float32), pieces)
    return outputs.reshape(MB_TOK, E)

def starts_of(position, bounds_row):
    seq_start = jnp.zeros(position.shape, jnp.int32)
    for cut_index in range(1, 7):
        seq_start = jnp.where(position >= bounds_row[cut_index], bounds_row[cut_index], seq_start)
    return seq_start.astype(jnp.int32)

def mix_layer(hidden, params, bounds_row):
    norm_gain, in_proj, conv_kernel, conv_bias, x_proj, dt_proj, dt_bias, skip_gain, out_proj = params
    inv_rms = lax.rsqrt(lax.optimization_barrier(jnp.mean(hidden * hidden, axis=-1, keepdims=True)) + 1e-05)
    normed = low(hidden * inv_rms * norm_gain)
    mixed_in = low_back(matmul(normed, in_proj))
    x_in = mixed_in[:, :E]
    gate_in = mixed_in[:, E:]
    position = jnp.arange(MB_TOK, dtype=jnp.int32)
    seq_start = starts_of(position, bounds_row)
    padded = jnp.concatenate([jnp.zeros((TAPS - 1, E), jnp.float32), x_in], axis=0)
    conv_pre = conv_bias + jnp.zeros((MB_TOK, E), jnp.float32)
    for tap_index in range(TAPS):
        valid_tap = (position - (TAPS - 1 - tap_index) >= seq_start).astype(jnp.float32)[:, None]
        conv_pre = conv_pre + conv_kernel[tap_index] * padded[tap_index:tap_index + MB_TOK] * valid_tap
    conv_act = jax.nn.silu(conv_pre)
    projected = low(low_back(matmul(low(conv_act), x_proj)))
    dt_in = projected[:, :RANK]
    key_vecs = projected[:, RANK:RANK + STATE]
    query_vecs = projected[:, RANK + STATE:]
    beta_gate = jax.nn.sigmoid(low_back(matmul(dt_in, dt_proj) + dt_bias))
    step_size = beta_gate / (1.0 + beta_gate * lax.optimization_barrier(jnp.sum(key_vecs * key_vecs, axis=-1, keepdims=True)))
    keep_flags = (position != seq_start).astype(jnp.float32)
    output = state_run(step_size, key_vecs, query_vecs, conv_act, keep_flags) + skip_gain * conv_act
    gated = low(output * jax.nn.silu(gate_in))
    return hidden + low_back(matmul(gated, out_proj))

def reference(tokens, cotangent, bounds, norm_gain, in_proj, conv_kernel, conv_bias, x_proj, dt_proj, dt_bias, skip_gain, out_proj):
    weights = tuple((member.astype(jnp.float32) for member in (norm_gain, in_proj, conv_kernel, conv_bias, x_proj, dt_proj, dt_bias, skip_gain, out_proj)))
    outputs = []
    input_grads = []
    totals = [jnp.zeros(member.shape, jnp.float32) for member in weights]
    for micro_id in range(MICRO):
        bounds_row = bounds[micro_id]

        def stack_forward(entry_rows, *layer_weights):
            hidden = entry_rows
            for layer_id in range(LAYERS):
                hidden = mix_layer(hidden, tuple((member[layer_id] for member in layer_weights)), bounds_row)
                if layer_id + 1 < LAYERS:
                    hidden = low(low_back(hidden))
            return hidden
        result, pullback = jax.vjp(stack_forward, tokens[micro_id].astype(jnp.float32), *weights)
        grads = pullback(cotangent[micro_id].astype(jnp.float32))
        outputs.append(result.astype(jnp.bfloat16))
        input_grads.append(grads[0].astype(jnp.bfloat16))
        totals = [acc_sum + grad_part for acc_sum, grad_part in zip(totals, grads[1:])]
    return (jnp.stack(outputs), jnp.stack(input_grads), totals[0], totals[1], totals[2], totals[3], totals[4], totals[5], totals[6], totals[7], totals[8])
```

```python
import functools
import math

import jax
import jax.numpy as jnp
from jax import lax
from jax.experimental import pallas as pl
from jax.experimental.pallas import tpu as pltpu
from jax.sharding import PartitionSpec as P

NORM_EPS = 1e-05
LOG2E = math.log2(math.e)
BF = jnp.bfloat16
F32 = jnp.float32
MESH = pl.DeviceIdType.MESH
LANES = 128
BT = 16
N = 16
MIB = 2**20
VSPEC = pl.BlockSpec(memory_space=pltpu.VMEM)
ANYSPEC = pl.BlockSpec(memory_space=pl.ANY)


def params(**kw):
    return pltpu.CompilerParams(vmem_limit_bytes=56 * MIB, **kw)


def dot(a, b):
    return jnp.dot(a, b, preferred_element_type=F32)


def dot_nt(a, b):
    return lax.dot_general(a, b, (((1,), (1,)), ((), ())), preferred_element_type=F32)


def dot_tn(a, b):
    return lax.dot_general(a, b, (((0,), (0,)), ((), ())), preferred_element_type=F32)


def iota(shape, dim):
    return lax.broadcasted_iota(jnp.int32, shape, dim)


def chosen_copy(layer, own, other, dst, sem):
    sec = lax.axis_index("section")

    @pl.when(sec == layer)
    def _():
        pltpu.make_async_copy(own, dst, sem).start()

    @pl.when(sec != layer)
    def _():
        pltpu.make_async_copy(other, dst, sem).start()


def wait_copy(src, dst, sem):
    pltpu.make_async_copy(src, dst, sem).wait()


def silu_parts(v):
    s = jax.nn.sigmoid(v)
    return v * s, s * (1.0 + v * (1.0 - s))


def fwd_a_kernel(
    layer, rank, h_ref, rim_ref, gain_ref, ck_ref, cb_ref, xp_ref, dtp_ref, dtb_ref, mask_ref,
    in_own, in_oth,
    u_ref, xi_ref, z_ref, c_ref, proj_ref, beta_ref, ex_ref, us_ref, k2_ref, kb_ref, qb_ref, summ_ref,
    w_buf, sems,
):
    t_len, width = h_ref.shape
    inner = z_ref.shape[1]
    cb = 512
    n_chunk = 2 * inner // cb
    rim = rim_ref.shape[0]
    for k in range(n_chunk):
        at = pl.ds(k * cb, cb)
        chosen_copy(layer, in_own.at[:, at], in_oth.at[:, at], w_buf.at[:, at], sems.at[k])
    hf = jnp.concatenate([rim_ref[...], h_ref[...]], axis=0).astype(F32)
    inv = lax.rsqrt(jnp.mean(hf * hf, axis=-1, keepdims=True) + NORM_EPS)
    u_all = (hf * inv * gain_ref[...]).astype(BF)
    u_ref[...] = u_all[rim:]
    mask = mask_ref[...]
    proj = jnp.zeros((t_len, LANES), F32)
    for k in range(inner // cb):
        at = pl.ds(k * cb, cb)
        wait_copy(in_own.at[:, at], w_buf.at[:, at], sems.at[k])
        xi = dot(u_all, w_buf[:, at])
        xi_ref[:, at] = xi
        c = cb_ref[:, at] + ck_ref[3:4, at] * xi[rim:]
        for j in range(3):
            c = c + ck_ref[j : j + 1, at] * xi[rim - 3 + j : rim - 3 + j + t_len] * mask[:, j : j + 1]
        c_ref[:, at] = c
        xc = c * jax.nn.sigmoid(c)
        us_ref[:, at] = xc
        proj = proj + dot(xc.astype(BF), xp_ref[at, :])
    cols = iota((t_len, LANES), 1)
    keep = mask[:, 4:5]
    projb = jnp.where(cols == rank + 2 * N, keep, proj).astype(BF)
    proj_ref[...] = projb
    pf = projb.astype(F32)
    ksum = jnp.sum(jnp.where((cols >= rank) & (cols < rank + N), pf * pf, 0.0), axis=-1, keepdims=True)
    for k in range(inner // cb):
        at = pl.ds(k * cb, cb)
        beta = jax.nn.sigmoid(dot(projb, dtp_ref[:, at]) + dtb_ref[:, at])
        eps = beta / (1.0 + beta * ksum)
        beta_ref[:, at] = beta
        us_ref[:, at] = us_ref[:, at] * eps
        ex_ref[:, at] = jnp.where(keep > 0.0, eps, 1.0)
    rows = t_len * N
    sel = (iota((rows, t_len), 0) // N == iota((rows, t_len), 1)).astype(F32).astype(BF)
    spread = dot(sel, projb).astype(BF)
    rn = iota((rows, LANES), 0) % N
    cl = iota((rows, LANES), 1)
    ones = jnp.ones((LANES, LANES), BF)
    zero = jnp.zeros((rows, LANES), BF)
    kb = dot(jnp.where(cl == rank + rn, spread, zero), ones)
    qb = dot(jnp.where(cl == rank + N + rn, spread, zero), ones)
    keepb = dot(jnp.where(cl == rank + 2 * N, spread, zero), ones)
    kb_ref[...] = kb
    qb_ref[...] = qb
    k2_ref[...] = jnp.where(keepb > 0.5, -LOG2E * kb * kb, -1e30)
    ec = 512
    nt = ec // LANES
    un = 8

    def chunk(ci, carry):
        e0 = pl.multiple_of(ci * ec, ec)

        def body(i, sd):
            s, d = [list(v) for v in sd]
            g0 = pl.multiple_of(i * un, un)
            for t in range(un):
                r = pl.multiple_of(g0 * N + t * N, N)
                k2 = k2_ref[pl.ds(r, N), :]
                kv = kb_ref[pl.ds(r, N), :]
                for j in range(nt):
                    lane = pl.ds(e0 + LANES * j, LANES)
                    a = jnp.exp2(k2 * ex_ref.at[pl.ds(g0, un), lane][t : t + 1, :])
                    s[j] = a * s[j] + kv * us_ref.at[pl.ds(g0, un), lane][t : t + 1, :]
                    d[j] = a * d[j]
            return tuple(s), tuple(d)

        zeros = tuple(jnp.zeros((N, LANES), F32) for _ in range(nt))
        one = tuple(jnp.ones((N, LANES), F32) for _ in range(nt))
        s, d = lax.fori_loop(0, t_len // un, body, (zeros, one))
        for j in range(nt):
            lane = pl.ds(e0 + LANES * j, LANES)
            summ_ref[0:N, lane] = d[j].astype(BF)
            summ_ref[N : 2 * N, lane] = s[j].astype(BF)
        return carry

    lax.fori_loop(0, inner // ec, chunk, 0)
    for k in range(inner // cb, n_chunk):
        at = pl.ds(k * cb, cb)
        wait_copy(in_own.at[:, at], w_buf.at[:, at], sems.at[k])
        z_ref[:, pl.ds(k * cb - inner, cb)] = dot(u_all[rim:], w_buf[:, at])


def fwd_a(layer, rank, h, rim, w, mask, in_own, in_oth):
    t_len, width = h.shape
    inner = w["cb"].shape[1]
    rows = t_len * N

    def f32(*s):
        return jax.ShapeDtypeStruct(s, F32)

    def b16(*s):
        return jax.ShapeDtypeStruct(s, BF)

    return pl.pallas_call(
        functools.partial(fwd_a_kernel, layer, rank),
        out_shape=[
            b16(t_len, width), f32(t_len + rim.shape[0], inner), f32(t_len, inner), f32(t_len, inner),
            b16(t_len, LANES), f32(t_len, inner), f32(t_len, inner), f32(t_len, inner),
            f32(rows, LANES), f32(rows, LANES), f32(rows, LANES), b16(2 * N, inner),
        ],
        in_specs=[VSPEC] * 9 + [ANYSPEC] * 2,
        out_specs=[VSPEC] * 12,
        scratch_shapes=[pltpu.VMEM((width, 2 * inner), BF), pltpu.SemaphoreType.DMA((2 * inner // 512,))],
        compiler_params=params(),
        name=f"fwd_in_{layer}",
    )(h, rim, w["gain"], w["ck"], w["cb"], w["xp"], w["dtp"], w["dtb"], mask, in_own, in_oth)


def carry_kernel(n, reverse, *refs):
    if reverse:
        s_ref, d_ref, in_ref, recv, pre, send1, recv1, send2, recv2 = refs
        parts = 1
    else:
        s_ref, in_ref, d_ref, recv, pre, send1, recv1, send2, recv2 = refs
        parts = 2
    inner = s_ref.shape[1]
    blocks = min(n, inner // LANES)
    stride = n // blocks
    sec = lax.axis_index("section")
    me = lax.axis_index("ctx")
    mine = me // stride
    owner = lax.rem(me, stride) == 0

    def when(cond, fn):
        if stride == 1:
            fn()
        else:
            pl.when(cond)(fn)

    def peers(k):
        to = lax.rem(me + k, n)
        frm = lax.rem(me - k + n, n)
        return to, frm

    def first(k):
        to, frm = peers(k)
        lane = pl.ds(pl.multiple_of((to // stride) * LANES, LANES), LANES)
        return pltpu.make_async_remote_copy(
            src_ref=s_ref.at[:, lane], dst_ref=recv.at[me],
            send_sem=send1.at[k], recv_sem=recv1.at[me],
            device_id=(sec, to), device_id_type=MESH)

    def second(k):
        to, frm = peers(k)
        lane = pl.ds(pl.multiple_of(mine * LANES, LANES), LANES)
        return pltpu.make_async_remote_copy(
            src_ref=pre.at[to], dst_ref=in_ref.at[:, lane],
            send_sem=send2.at[k], recv_sem=recv2.at[me],
            device_id=(sec, to), device_id_type=MESH)

    barrier = pltpu.get_barrier_semaphore()
    for k in range(1, n):
        pl.semaphore_signal(barrier, inc=1, device_id=(sec, peers(k)[0]), device_id_type=MESH)
    pl.semaphore_wait(barrier, n - 1)
    for k in range(1, n):
        when(lax.rem(peers(k)[0], stride) == 0, lambda k=k: first(k).start())

    def own_part():
        lane = pl.ds(pl.multiple_of(mine * LANES, LANES), LANES)
        recv[me] = s_ref[:, lane]
        for k in range(1, n):
            frm = peers(k)[1]
            pltpu.make_async_remote_copy(
                src_ref=s_ref.at[:, pl.ds(0, LANES)], dst_ref=recv.at[frm],
                send_sem=send1.at[k], recv_sem=recv1.at[frm],
                device_id=(sec, frm), device_id_type=MESH).wait_recv()
        run = jnp.zeros((N, LANES), F32)
        for i in range(n):
            d = n - 1 - i if reverse else i
            pre[d] = run.astype(BF)
            if reverse:
                dec, st = d_ref[d], recv[d]
            else:
                dec, st = recv[d, 0:N, :], recv[d, N : 2 * N, :]
                d_ref[d] = dec
            run = dec.astype(F32) * run + st.astype(F32)
        for k in range(1, n):
            second(k).start()
        in_ref[:, lane] = pre[me]

    when(owner, own_part)
    for k in range(1, n):
        frm = peers(k)[1]

        def get(frm=frm, k=k):
            lane = pl.ds(pl.multiple_of((frm // stride) * LANES, LANES), LANES)
            pltpu.make_async_remote_copy(
                src_ref=pre.at[0], dst_ref=in_ref.at[:, lane],
                send_sem=send2.at[k], recv_sem=recv2.at[frm],
                device_id=(sec, frm), device_id_type=MESH).wait_recv()

        when(lax.rem(frm, stride) == 0, get)
    for k in range(1, n):
        when(lax.rem(peers(k)[0], stride) == 0, lambda k=k: first(k).wait_send())

    def sent():
        for k in range(1, n):
            second(k).wait_send()

    when(owner, sent)


def carry(n, reverse, cid, summ, decay=None):
    inner = summ.shape[1]
    got = jax.ShapeDtypeStruct((N, inner), BF)
    dec = jax.ShapeDtypeStruct((n, N, LANES), BF)
    rows = N if reverse else 2 * N
    sems = [pltpu.SemaphoreType.DMA((n,))] * 4
    return pl.pallas_call(
        functools.partial(carry_kernel, n, reverse),
        out_shape=[got] if reverse else [got, dec],
        in_specs=[VSPEC] * (2 if reverse else 1),
        out_specs=[VSPEC] * (1 if reverse else 2),
        scratch_shapes=[pltpu.VMEM((n, rows, LANES), BF), pltpu.VMEM((n, N, LANES), BF)] + sems,
        compiler_params=params(collective_id=cid, has_side_effects=True),
        name=f"carry_{cid}",
    )(*((summ, decay) if reverse else (summ,)))


def block_diag(projb, first_col):
    pick = (iota((LANES, BT * N), 0) == first_col + iota((LANES, BT * N), 1) % N).astype(F32).astype(BF)
    vals = dot(projb, pick)
    same = iota((BT, BT * N), 0) == iota((BT, BT * N), 1) // N
    return jnp.where(same, vals, 0.0)


def fwd_b_kernel(
    layer, rank, k2_ref, kb_ref, proj_ref, ex_ref, us_ref, c_ref, z_ref, skip_ref, sin_ref, h_ref, out_own, out_oth,
    s_ref, sb_ref, y_ref, o_ref, hout_ref,
    st, o_all, w_buf, sem,
):
    i = pl.program_id(0)
    inner = z_ref.shape[1]
    ec = 512
    nt = ec // LANES

    @pl.when(i == 0)
    def _():
        chosen_copy(layer, out_own, out_oth, w_buf, sem)
        st[...] = sin_ref[...].astype(F32)

    sb_ref[...] = st[...].astype(BF)
    qbd = block_diag(proj_ref[...], rank + N).astype(BF)
    for ci in range(inner // ec):
        e0 = ci * ec
        s = [st[:, pl.ds(e0 + LANES * j, LANES)] for j in range(nt)]
        for t in range(BT):
            k2 = k2_ref[t * N : (t + 1) * N, :]
            kv = kb_ref[t * N : (t + 1) * N, :]
            for j in range(nt):
                lane = pl.ds(e0 + LANES * j, LANES)
                a = jnp.exp2(k2 * ex_ref[t : t + 1, lane])
                s[j] = a * s[j] + kv * us_ref[t : t + 1, lane]
                s_ref[t * N : (t + 1) * N, lane] = s[j].astype(BF)
        for j in range(nt):
            st[:, pl.ds(e0 + LANES * j, LANES)] = s[j]
        at = pl.ds(e0, ec)
        c = c_ref[:, at]
        y = dot(qbd, s_ref[:, at]) + skip_ref[:, at] * (c * jax.nn.sigmoid(c))
        y_ref[:, at] = y
        z = z_ref[:, at]
        o = (y * (z * jax.nn.sigmoid(z))).astype(BF)
        o_ref[:, at] = o
        o_all[pl.ds(pl.multiple_of(i * BT, BT), BT), at] = o

    @pl.when(i == pl.num_programs(0) - 1)
    def _():
        wait_copy(out_own, w_buf, sem)
        hout_ref[...] = (h_ref[...].astype(F32) + dot(o_all[...], w_buf[...])).astype(BF)


def fwd_b(layer, rank, h, fa, sin, w, out_own, out_oth):
    t_len, width = h.shape
    inner = w["cb"].shape[1]

    def blk(r, c):
        return pl.BlockSpec((r, c), lambda i: (i, 0))

    def whole(r, c):
        return pl.BlockSpec((r, c), lambda i: (0, 0))

    return pl.pallas_call(
        functools.partial(fwd_b_kernel, layer, rank),
        grid=(t_len // BT,),
        in_specs=[
            blk(BT * N, LANES), blk(BT * N, LANES), blk(BT, LANES), blk(BT, inner), blk(BT, inner), blk(BT, inner),
            blk(BT, inner), whole(1, inner), whole(N, inner), whole(t_len, width), ANYSPEC, ANYSPEC,
        ],
        out_specs=[blk(BT * N, inner), blk(BT, inner), blk(BT, inner), blk(BT, inner), whole(t_len, width)],
        out_shape=[
            jax.ShapeDtypeStruct((t_len * N, inner), BF), jax.ShapeDtypeStruct((t_len, inner), BF),
            jax.ShapeDtypeStruct((t_len, inner), F32), jax.ShapeDtypeStruct((t_len, inner), BF),
            jax.ShapeDtypeStruct((t_len, width), BF),
        ],
        scratch_shapes=[
            pltpu.VMEM((N, inner), F32), pltpu.VMEM((t_len, inner), BF), pltpu.VMEM((inner, width), BF),
            pltpu.SemaphoreType.DMA(()),
        ],
        compiler_params=params(),
        name=f"fwd_out_{layer}",
    )(fa["k2"], fa["kb"], fa["proj"], fa["ex"], fa["us"], fa["c"], fa["z"], w["skip"], sin, h, out_own, out_oth)


def bwd_a_kernel(
    layer, gout_ref, z_ref, y_ref, c_ref, o_ref, u_ref, skip_ref, k2_ref, qb_ref, ex_ref, out_own, out_oth,
    dy_ref, dz_ref, go_ref, gz_ref, gskip_ref, from_ref,
    w_buf, sems,
):
    t_len, width = gout_ref.shape
    inner = z_ref.shape[1]
    cb = 512
    for k in range(inner // cb):
        at = pl.ds(k * cb, cb)
        chosen_copy(layer, out_own.at[at, :], out_oth.at[at, :], w_buf.at[at, :], sems.at[k])
    dr = gout_ref[...]
    u = u_ref[...]
    for k in range(inner // cb):
        at = pl.ds(k * cb, cb)
        wait_copy(out_own.at[at, :], w_buf.at[at, :], sems.at[k])
        do = dot_nt(dr, w_buf[at, :])
        act, der = silu_parts(z_ref[:, at])
        dy = do * act
        dy_ref[:, at] = dy
        dz = (do * y_ref[:, at] * der).astype(BF)
        dz_ref[:, at] = dz
        c = c_ref[:, at]
        gskip_ref[:, at] = jnp.sum(dy * (c * jax.nn.sigmoid(c)), axis=0, keepdims=True)
        go_ref[at, :] = dot_tn(o_ref[:, at], dr).astype(BF)
        gz_ref[:, at] = dot_tn(u, dz).astype(BF)
    ec = 512
    nt = ec // LANES
    un = 8

    def chunk(ci, carry):
        e0 = pl.multiple_of(ci * ec, ec)

        def body(i, b):
            b = list(b)
            g0 = pl.multiple_of((t_len // un - 1 - i) * un, un)
            for t in range(un - 1, -1, -1):
                r = pl.multiple_of(g0 * N + t * N, N)
                k2 = k2_ref[pl.ds(r, N), :]
                qv = qb_ref[pl.ds(r, N), :]
                for j in range(nt):
                    lane = pl.ds(e0 + LANES * j, LANES)
                    a = jnp.exp2(k2 * ex_ref.at[pl.ds(g0, un), lane][t : t + 1, :])
                    b[j] = a * (qv * dy_ref.at[pl.ds(g0, un), lane][t : t + 1, :] + b[j])
            return tuple(b)

        b = lax.fori_loop(0, t_len // un, body, tuple(jnp.zeros((N, LANES), F32) for _ in range(nt)))
        for j in range(nt):
            from_ref[:, pl.ds(e0 + LANES * j, LANES)] = b[j].astype(BF)
        return carry

    lax.fori_loop(0, inner // ec, chunk, 0)


def bwd_a(layer, gout, fa, fb, w, out_own, out_oth):
    t_len, width = gout.shape
    inner = w["cb"].shape[1]

    def sd(t, *s):
        return jax.ShapeDtypeStruct(s, t)

    return pl.pallas_call(
        functools.partial(bwd_a_kernel, layer),
        out_shape=[
            sd(F32, t_len, inner), sd(BF, t_len, inner), sd(BF, inner, width), sd(BF, width, inner), sd(F32, 1, inner),
            sd(BF, N, inner),
        ],
        in_specs=[VSPEC] * 10 + [ANYSPEC] * 2,
        out_specs=[VSPEC] * 6,
        scratch_shapes=[pltpu.VMEM((inner, width), BF), pltpu.SemaphoreType.DMA((inner // 512,))],
        compiler_params=params(),
        name=f"back_out_{layer}",
    )(gout, fa["z"], fb["y"], fa["c"], fb["o"], fa["u"], w["skip"], fa["k2"], fa["qb"], fa["ex"], out_own, out_oth)


def bwd_b_kernel(
    rank, k2_ref, qb_ref, proj_blk, ex_ref, us_ref, dy_ref, beta_ref, c_ref, s_ref, sb_ref,
    bin_ref, proj_ref, skip_ref, beta_all, c_all, xi_ref, ck_ref, xp_ref, dtp_ref, mask_ref,
    dxi_ref, rim_ref, gdt_ref, gdtb_ref, gxp_ref, gcb_ref, gck_ref,
    bst, qs, ws, deps_ref, dxc_ref, dkq_ref, dp_ref,
):
    i = pl.program_id(0)
    steps = pl.num_programs(0)
    blk = steps - 1 - i
    t_len = proj_ref.shape[0]
    inner = skip_ref.shape[1]
    ec = 512
    nt = ec // LANES

    @pl.when(i == 0)
    def _():
        bst[...] = bin_ref[...].astype(F32)

    projb = proj_blk[...]
    pf = projb.astype(F32)
    cols = iota((BT, LANES), 1)
    is_k = (cols >= rank) & (cols < rank + N)
    ksum = jnp.sum(jnp.where(is_k, pf * pf, 0.0), axis=-1, keepdims=True)
    kbd = block_diag(projb, rank)
    k2bd = (kbd * kbd).astype(BF)
    kbd = kbd.astype(BF)
    r1 = jnp.zeros((BT, BT * N), F32)
    r2 = jnp.zeros((BT, BT * N), F32)
    r3 = jnp.zeros((BT, BT * N), F32)
    base = pl.multiple_of(blk * BT, BT)
    for ci in range(inner // ec):
        e0 = ci * ec
        b = [bst[:, pl.ds(e0 + LANES * j, LANES)] for j in range(nt)]
        for t in range(BT - 1, -1, -1):
            row = slice(t * N, (t + 1) * N)
            k2 = k2_ref[row, :]
            qv = qb_ref[row, :]
            for j in range(nt):
                lane = pl.ds(e0 + LANES * j, LANES)
                a = jnp.exp2(k2 * ex_ref[t : t + 1, lane])
                q = qv * dy_ref[t : t + 1, lane] + b[j]
                b[j] = a * q
                prev = (s_ref[(t - 1) * N : t * N, lane] if t > 0 else sb_ref[:, lane]).astype(F32)
                qs[row, lane] = q.astype(BF)
                ws[row, lane] = (b[j] * prev).astype(BF)
        for j in range(nt):
            bst[:, pl.ds(e0 + LANES * j, LANES)] = b[j]
        at = pl.ds(e0, ec)
        p1 = dot(kbd, qs[:, at])
        p2 = dot(k2bd, ws[:, at])
        c = c_ref[:, at]
        beta = beta_ref[:, at]
        eps = beta / (1.0 + beta * ksum)
        dy = dy_ref[:, at]
        deps_ref[pl.ds(base, BT), at] = (c * jax.nn.sigmoid(c)) * p1 - p2
        dxc_ref[pl.ds(base, BT), at] = dy * skip_ref[:, at] + eps * p1
        r1 = r1 + dot_nt(us_ref[:, at].astype(BF), qs[:, at])
        r2 = r2 + dot_nt(eps.astype(BF), ws[:, at])
        r3 = r3 + dot_nt(dy.astype(BF), s_ref[:, at])
    same = iota((BT, BT * N), 0) == iota((BT, BT * N), 1) // N
    gather_k = (iota((BT * N, LANES), 1) == rank + iota((BT * N, LANES), 0) % N).astype(F32)
    gather_q = (iota((BT * N, LANES), 1) == rank + N + iota((BT * N, LANES), 0) % N).astype(F32)

    def pick(r, g):
        return jnp.dot(jnp.where(same, r, 0.0), g, precision=lax.Precision.HIGHEST, preferred_element_type=F32)

    dkq_ref[pl.ds(base, BT), :] = pick(r1, gather_k) - 2.0 * pf * pick(r2, gather_k) + pick(r3, gather_q)

    @pl.when(i == steps - 1)
    def _():
        projw = proj_ref[...]
        pw = projw.astype(F32)
        colw = iota((t_len, LANES), 1)
        isk = (colw >= rank) & (colw < rank + N)
        kall = jnp.where(isk, pw, 0.0)
        ks = jnp.sum(kall * kall, axis=-1, keepdims=True)
        tc = 256

        def first(k, carry):
            dkc, ddt = carry
            at = pl.ds(pl.multiple_of(k * tc, tc), tc)
            beta = beta_all[:, at]
            inv = 1.0 / (1.0 + beta * ks)
            dq = deps_ref[:, at] * (inv * inv)
            dkc = dkc + jnp.sum(dq * beta * beta, axis=-1, keepdims=True)
            dp = (dq * beta * (1.0 - beta)).astype(BF)
            gdtb_ref[:, at] = jnp.sum(dp.astype(F32), axis=0, keepdims=True)
            gdt_ref[:, at] = dot_tn(projw, dp)
            ddt = ddt + dot_nt(dp, dtp_ref[:, at])
            return dkc, ddt

        dkc, ddt = lax.fori_loop(
            0, inner // tc, first, (jnp.zeros((t_len, 1), F32), jnp.zeros((t_len, LANES), F32)))
        dproj = (jnp.where(colw < rank, ddt, dkq_ref[...]) - 2.0 * kall * dkc).astype(BF)
        mask = mask_ref[...]
        lead = xi_ref.shape[0] - t_len

        def second(k, carry):
            at = pl.ds(pl.multiple_of(k * tc, tc), tc)
            c = c_all[:, at]
            act, der = silu_parts(c)
            gxp_ref[at, :] = dot_tn(act.astype(BF), dproj)
            dc = (dxc_ref[:, at] + dot_nt(dproj, xp_ref[at, :])) * der
            gcb_ref[:, at] = jnp.sum(dc, axis=0, keepdims=True)
            xi = xi_ref[:, at]
            pad = jnp.zeros((8, tc), F32)
            dxi = ck_ref[3:4, at] * dc
            rim = jnp.zeros((8, tc), F32)
            gck_ref[3:4, at] = jnp.sum(dc * xi[lead:], axis=0, keepdims=True)
            for j in range(3):
                m = dc * mask[:, j : j + 1]
                gck_ref[j : j + 1, at] = jnp.sum(m * xi[lead - 3 + j : lead - 3 + j + t_len], axis=0, keepdims=True)
                m = m * ck_ref[j : j + 1, at]
                ext = jnp.concatenate([pad, m, pad], axis=0)
                dxi = dxi + ext[8 + 3 - j : 8 + 3 - j + t_len]
                rim = rim + ext[8 - j : 16 - j]
            dxi_ref[:, at] = dxi
            rim_ref[:, at] = jnp.where(iota((8, tc), 0) < 3, rim, 0.0)
            return carry

        lax.fori_loop(0, inner // tc, second, 0)


def bwd_b(rank, fa, fb, dy, bin_, w, mask):
    t_len = dy.shape[0]
    inner = w["cb"].shape[1]
    steps = t_len // BT

    def blk(r, c):
        return pl.BlockSpec((r, c), lambda i: (steps - 1 - i, 0))

    def whole(r, c):
        return pl.BlockSpec((r, c), lambda i: (0, 0))

    def sd(*s):
        return jax.ShapeDtypeStruct(s, F32)

    ext = fa["xi"].shape[0]
    return pl.pallas_call(
        functools.partial(bwd_b_kernel, rank),
        grid=(steps,),
        in_specs=[
            blk(BT * N, LANES), blk(BT * N, LANES), blk(BT, LANES), blk(BT, inner), blk(BT, inner), blk(BT, inner),
            blk(BT, inner), blk(BT, inner), blk(BT * N, inner), blk(BT, inner),
            whole(N, inner), whole(t_len, LANES), whole(1, inner), whole(t_len, inner), whole(t_len, inner),
            whole(ext, inner), whole(8, inner), whole(inner, LANES), whole(LANES, inner), whole(t_len, LANES),
        ],
        out_specs=[
            whole(t_len, inner), whole(8, inner), whole(LANES, inner), whole(1, inner), whole(inner, LANES),
            whole(1, inner), whole(8, inner),
        ],
        out_shape=[
            sd(t_len, inner), sd(8, inner), sd(LANES, inner), sd(1, inner), sd(inner, LANES), sd(1, inner), sd(8, inner),
        ],
        scratch_shapes=[
            pltpu.VMEM((N, inner), F32), pltpu.VMEM((BT * N, inner), BF), pltpu.VMEM((BT * N, inner), BF),
            pltpu.VMEM((t_len, inner), F32), pltpu.VMEM((t_len, inner), F32), pltpu.VMEM((t_len, LANES), F32),
            pltpu.VMEM((8, LANES), BF),
        ],
        compiler_params=params(),
        name="back_scan",
    )(
        fa["k2"], fa["qb"], fa["proj"], fa["ex"], fa["us"], dy, fa["beta"], fa["c"], fb["s"], fb["sb"],
        bin_, fa["proj"], w["skip"], fa["beta"], fa["c"], fa["xi"], w["ck"], w["xp"], w["dtp"], mask,
    )


def bwd_c_kernel(
    layer, dxi_ref, rim_ref, dz_ref, u_ref, h_ref, gout_ref, gain_ref, in_own, in_oth,
    gx_ref, dh_ref, ggain_ref,
    w_buf, sems,
):
    t_len, width = h_ref.shape
    inner = dz_ref.shape[1]
    cb = 512
    n_chunk = 2 * inner // cb
    for k in range(n_chunk):
        at = pl.ds(k * cb, cb)
        chosen_copy(layer, in_own.at[:, at], in_oth.at[:, at], w_buf.at[:, at], sems.at[k])
    u = u_ref[...]
    du = jnp.zeros((t_len, width), F32)
    for k in range(n_chunk):
        at = pl.ds(k * cb, cb)
        if k < inner // cb:
            dxi = dxi_ref[:, at]
            rim = jnp.concatenate([jnp.zeros((5, cb), F32), rim_ref[0:3, at]], axis=0)
            g = jnp.concatenate([dxi[: t_len - 8], dxi[t_len - 8 :] + rim], axis=0).astype(BF)
            gx_ref[:, at] = dot_tn(u, g).astype(BF)
        else:
            g = dz_ref[:, pl.ds(k * cb - inner, cb)]
        wait_copy(in_own.at[:, at], w_buf.at[:, at], sems.at[k])
        du = du + dot_nt(g, w_buf[:, at])
    hf = h_ref[...].astype(F32)
    inv = lax.rsqrt(jnp.mean(hf * hf, axis=-1, keepdims=True) + NORM_EPS)
    unit = hf * inv
    ggain_ref[...] = jnp.sum(du * unit, axis=0, keepdims=True)
    dn = du * gain_ref[...]
    dh = gout_ref[...].astype(F32) + inv * (dn - unit * jnp.mean(dn * unit, axis=-1, keepdims=True))
    dh_ref[...] = dh.astype(BF)


def bwd_c(layer, dxi, rim, dz, fa, h, gout, w, in_own, in_oth):
    t_len, width = h.shape
    inner = dz.shape[1]
    return pl.pallas_call(
        functools.partial(bwd_c_kernel, layer),
        out_shape=[
            jax.ShapeDtypeStruct((width, inner), BF), jax.ShapeDtypeStruct((t_len, width), BF),
            jax.ShapeDtypeStruct((1, width), F32),
        ],
        in_specs=[VSPEC] * 7 + [ANYSPEC] * 2,
        out_specs=[VSPEC] * 3,
        scratch_shapes=[pltpu.VMEM((width, 2 * inner), BF), pltpu.SemaphoreType.DMA((2 * inner // 512,))],
        compiler_params=params(),
        name=f"back_in_{layer}",
    )(dxi, rim, dz, fa["u"], h, gout, w["gain"], in_own, in_oth)


def bit_orders(bits):
    low = list(range(bits))
    return [low, [1, 0] + low[2:], [2, 0, 1] + low[3:], low]


def sum_kernel(layer, bits, orders, *refs):
    cnt = len(orders)
    srcs = refs[:cnt]
    outs = refs[cnt : 2 * cnt]
    accs = refs[2 * cnt : 3 * cnt]
    sib = refs[3 * cnt : 4 * cnt]
    rest = refs[4 * cnt :]
    recvs = [rest[p * bits : (p + 1) * bits] for p in range(cnt)]
    res = rest[cnt * bits : cnt * bits + cnt]
    load_sem, ssem, rsem, fsem, frsem = rest[cnt * bits + cnt :]
    sec = lax.axis_index("section")
    me = lax.axis_index("ctx")
    my_bit = [lax.rem(me // 2**b, 2) for b in range(bits)]
    barrier = pltpu.get_barrier_semaphore()
    pl.semaphore_signal(barrier, inc=1, device_id=(1 - sec, me), device_id_type=MESH)
    for b in range(bits):
        to = me + 2**b * (1 - 2 * my_bit[b])
        pl.semaphore_signal(barrier, inc=1, device_id=(sec, to), device_id_type=MESH)
    pl.semaphore_wait(barrier, bits + 1)

    def half(p, which):
        lanes = srcs[p].shape[-1] // 2
        return srcs[p].at[(slice(None),) * (bits + 1) + (pl.ds(pl.multiple_of(which * lanes, LANES), lanes),)]

    def across(p):
        return pltpu.make_async_remote_copy(
            src_ref=half(p, 1 - sec), dst_ref=sib[p], send_sem=ssem.at[p, 0], recv_sem=rsem.at[p, 0],
            device_id=(1 - sec, me), device_id_type=MESH)

    def load(p):
        return pltpu.make_async_copy(half(p, sec), accs[p], load_sem.at[p])

    def index(p, r, last):
        idx = [slice(None)] * bits
        for q in range(r):
            b = orders[p][q]
            idx[bits - 1 - b] = my_bit[b]
        b = orders[p][r]
        idx[bits - 1 - b] = last if last is not None else my_bit[b]
        return tuple(idx)

    def step(p, r):
        b = orders[p][r]
        to = me + 2**b * (1 - 2 * my_bit[b])
        return pltpu.make_async_remote_copy(
            src_ref=accs[p].at[index(p, r, 1 - my_bit[b])], dst_ref=recvs[p][r],
            send_sem=ssem.at[p, r + 1], recv_sem=rsem.at[p, r + 1],
            device_id=(sec, to), device_id_type=MESH)

    for p in range(cnt):
        across(p).start()
        load(p).start()

    def add(p, r):
        if r == 0:
            across(p).wait_recv()
            load(p).wait()
            rows = accs[p].shape[-2]
            lead = accs[p].shape[:bits]
            total = math.prod(lead)

            def body(k, carry):
                idx = tuple(lax.rem(k // 2 ** (bits - 1 - d), 2) for d in range(bits))
                accs[p][idx] = (accs[p][idx].astype(F32) + sib[p][idx].astype(F32)).astype(BF)
                return carry

            lax.fori_loop(0, total, body, 0)
            return
        step(p, r - 1).wait_recv()
        shape = recvs[p][r - 1].shape[:-2]
        total = math.prod(shape)
        fixed = index(p, r - 1, None)

        def body(k, carry):
            sub = []
            left = len(shape)
            for d in range(len(shape)):
                left -= 1
                sub.append(lax.rem(k // 2**left, 2))
            full, pos = [], 0
            for f in fixed:
                if isinstance(f, slice):
                    full.append(sub[pos])
                    pos += 1
                else:
                    full.append(f)
            val = accs[p][tuple(full)].astype(F32) + recvs[p][r - 1][tuple(sub)].astype(F32)
            if r == bits:
                res[p][...] = val
            else:
                accs[p][tuple(full)] = val.astype(BF)
            return carry

        lax.fori_loop(0, total, body, 0)

    for r in range(bits + 1):
        for p in range(cnt):
            add(p, r)
            if r < bits:
                step(p, r).start()

    def final(p):
        lanes = res[p].shape[-1]
        return pltpu.make_async_remote_copy(
            src_ref=res[p], dst_ref=outs[p].at[:, pl.ds(pl.multiple_of((1 - layer) * lanes, LANES), lanes)],
            send_sem=fsem.at[p], recv_sem=frsem.at[p], device_id=(1 - sec, me), device_id_type=MESH)

    @pl.when(sec != layer)
    def _():
        for p in range(cnt):
            final(p).start()
        for p in range(cnt):
            final(p).wait_send()

    @pl.when(sec == layer)
    def _():
        for p in range(cnt):
            lanes = res[p].shape[-1]
            outs[p][:, pl.ds(layer * lanes, lanes)] = res[p][...]
        for p in range(cnt):
            final(p).wait_recv()

    for p in range(cnt):
        across(p).wait_send()
        for r in range(bits):
            step(p, r).wait_send()


def summed(layer, n, cid, arrays):
    bits = n.bit_length() - 1
    orders = bit_orders(bits)[: len(arrays)]
    srcs, outs, accs, sibs, recvs, res = [], [], [], [], [], []
    for order, a in zip(orders, arrays):
        rows, lanes = a.shape[0] // n, a.shape[1]
        srcs.append(a.reshape((2,) * bits + (rows, lanes)))
        outs.append(jax.ShapeDtypeStruct((rows, lanes), F32))
        accs.append(pltpu.VMEM((2,) * bits + (rows, lanes // 2), BF))
        sibs.append(pltpu.VMEM((2,) * bits + (rows, lanes // 2), BF))
        for r in range(bits):
            recvs.append(pltpu.VMEM((2,) * (bits - 1 - r) + (rows, lanes // 2), BF))
        res.append(pltpu.VMEM((rows, lanes // 2), F32))
    cnt = len(arrays)
    return pl.pallas_call(
        functools.partial(sum_kernel, layer, bits, orders),
        out_shape=outs,
        in_specs=[ANYSPEC] * cnt,
        out_specs=[VSPEC] * cnt,
        scratch_shapes=accs + sibs + recvs + res + [
            pltpu.SemaphoreType.DMA((cnt,)), pltpu.SemaphoreType.DMA((cnt, bits + 1)),
            pltpu.SemaphoreType.DMA((cnt, bits + 1)), pltpu.SemaphoreType.DMA((cnt,)), pltpu.SemaphoreType.DMA((cnt,)),
        ],
        compiler_params=params(collective_id=cid, has_side_effects=True),
        name=f"sums_{layer}",
    )(*srcs)


def shift(value, axis, by):
    size = lax.axis_size(axis)
    return lax.ppermute(value, axis, [(i, i + by) for i in range(size) if 0 <= i + by < size])


def starts_of(position, bounds_row):
    start = jnp.zeros(position.shape, jnp.int32)
    for cut in range(1, 7):
        start = jnp.where(position >= bounds_row[cut], bounds_row[cut], start)
    return start


def pack_small(n, gain, ck, cb, xp, dt, dtb, skip):
    flat = [
        gain.reshape(n, -1),
        ck.reshape(ck.shape[0], n, -1).transpose(1, 0, 2).reshape(n, -1),
        cb.reshape(n, -1), dtb.reshape(n, -1), skip.reshape(n, -1),
        xp.reshape(n, -1), dt.reshape(n, -1),
    ]
    sizes = [f.shape[1] for f in flat]
    total = sum(sizes)
    unit = 16 * 2 * LANES
    padded = -(-total // unit) * unit
    flat.append(jnp.zeros((n, padded - total), F32))
    return jnp.concatenate(flat, axis=1).astype(BF).reshape(n * (padded // (2 * LANES)), 2 * LANES), sizes


def on_device(
    tokens, cotangent, bounds, norm_gain, in_proj, conv_kernel, conv_bias, x_proj, dt_proj, dt_bias, skip_gain, out_proj
):
    sec = lax.axis_index("section")
    n = lax.axis_size("ctx")
    me = lax.axis_index("ctx")
    t_len = tokens.shape[1]
    rank = dt_proj.shape[1]
    inner = in_proj.shape[2] // 2
    used = x_proj.shape[2]

    def swap(v):
        return lax.ppermute(v, "section", [(0, 1), (1, 0)])

    small = jnp.concatenate(
        [
            norm_gain[0].reshape(-1), conv_kernel[0].reshape(-1), conv_bias[0].reshape(-1), dt_bias[0].reshape(-1),
            skip_gain[0].reshape(-1), x_proj[0].reshape(-1), dt_proj[0].reshape(-1),
        ]
    )
    in_own, out_own = in_proj[0], out_proj[0]
    in_oth, small_oth, out_oth = swap(in_own), swap(small), swap(out_own)
    weights = []
    for layer in range(2):
        v = jnp.where(sec == layer, small, small_oth)
        at = 0

        def take(shape):
            nonlocal at
            size = math.prod(shape)
            piece = v[at : at + size].reshape(shape)
            at += size
            return piece

        w = {"gain": take((1, tokens.shape[2])).astype(F32)}
        w["ck"] = jnp.pad(take((4, inner)).astype(F32), ((0, 4), (0, 0)))
        w["cb"] = take((1, inner)).astype(F32)
        w["dtb"] = take((1, inner)).astype(F32)
        w["skip"] = take((1, inner)).astype(F32)
        w["xp"] = jnp.pad(take((inner, used)), ((0, 0), (0, LANES - used)))
        w["dtp"] = jnp.pad(take((rank, inner)), ((0, LANES - rank), (0, 0)))
        weights.append(w)
    tok = lax.dynamic_index_in_dim(tokens, sec, 0, keepdims=False)
    cot = lax.dynamic_index_in_dim(cotangent, sec, 0, keepdims=False)
    row = lax.dynamic_index_in_dim(bounds, sec, 0, keepdims=False)
    position = me * t_len + jnp.arange(t_len, dtype=jnp.int32)
    start = starts_of(position, row)
    marks = [(position - 3 + j >= start).astype(F32) for j in range(4)] + [(position != start).astype(F32)]
    mask = jnp.pad(jnp.stack(marks, axis=1), ((0, 0), (0, LANES - 5)))

    names_a = ("u", "xi", "z", "c", "proj", "beta", "ex", "us", "k2", "kb", "qb", "summ")
    names_b = ("s", "sb", "y", "o", "h")
    h = tok
    saved = []
    for layer in range(2):
        w = weights[layer]
        rim = shift(h[t_len - 16 :], "ctx", 1)
        fa = dict(zip(names_a, fwd_a(layer, rank, h, rim, w, mask, in_own, in_oth)))
        sin, dec = carry(n, False, 1 + layer, fa["summ"])
        fb = dict(zip(names_b, fwd_b(layer, rank, h, fa, sin, w, out_own, out_oth)))
        saved.append((h, fa, fb, dec))
        h = fb["h"]
    block_out = h
    gout = cot
    sums = [None, None]
    for layer in (1, 0):
        w = weights[layer]
        hin, fa, fb, dec = saved[layer]
        dy, dz, go, gz, gskip, frm = bwd_a(layer, gout, fa, fb, w, out_own, out_oth)
        (bin_,) = carry(n, True, 3 + layer, frm, dec)
        dxi, rim, gdt, gdtb, gxp, gcb, gck = bwd_b(rank, fa, fb, dy, bin_, w, mask)
        rim = shift(rim, "ctx", -1)
        gx, dh, ggain = bwd_c(layer, dxi, rim, dz, fa, hin, gout, w, in_own, in_oth)
        packed, sizes = pack_small(n, ggain, gck[:4], gcb, gxp, gdt[:rank], gdtb, gskip)
        sums[layer] = summed(layer, n, 5 + layer, (gx, gz, go, packed))
        gout = dh

    def mine(k):
        return jnp.where(sec == 0, sums[0][k], sums[1][k])

    s_small = mine(3).reshape(-1)
    parts, at = [], 0
    for size in sizes:
        parts.append(s_small[at : at + size])
        at += size
    g_gain, g_ck, g_cb, g_dtb, g_skip, g_xp, g_dt = parts
    return (
        block_out[None],
        gout[None],
        g_gain[None],
        jnp.concatenate([mine(0), mine(1)], axis=1)[None],
        g_ck.reshape(1, 4, -1),
        g_cb[None],
        g_xp.reshape(1, -1, LANES)[:, :, :used],
        g_dt.reshape(1, -1, inner),
        g_dtb[None],
        g_skip[None],
        mine(2)[None],
    )


def solution(mesh):
    placed = (
        P(None, "ctx", None), P(None, "ctx", None), P(), P("section", None), P("section", None, None),
        P("section", None, None), P("section", None), P("section", None, None), P("section", None, None),
        P("section", None), P("section", None), P("section", None, None),
    )
    return jax.shard_map(
        on_device,
        mesh=mesh,
        in_specs=placed,
        out_specs=(
            P("section", "ctx", None), P("section", "ctx", None), P("section", "ctx"), P("section", "ctx", None),
            P("section", None, "ctx"), P("section", "ctx"), P("section", "ctx", None), P("section", "ctx", None),
            P("section", "ctx"), P("section", "ctx"), P("section", "ctx", None),
        ),
        check_vma=False,
    )
```

```python
import functools
import math

import jax
import jax.numpy as jnp
from jax import lax
from jax.experimental import pallas as pl
from jax.experimental.pallas import tpu as pltpu
from jax.sharding import PartitionSpec as P

NORM_EPS = 1e-05
LOG2E = math.log2(math.e)
BF = jnp.bfloat16
F32 = jnp.float32
MESH = pl.DeviceIdType.MESH
LANES = 128
BT = 16
N = 16
MIB = 2**20
VSPEC = pl.BlockSpec(memory_space=pltpu.VMEM)
ANYSPEC = pl.BlockSpec(memory_space=pl.ANY)


def params(**kw):
    return pltpu.CompilerParams(vmem_limit_bytes=56 * MIB, **kw)


def dot(a, b):
    return jnp.dot(a, b, preferred_element_type=F32)


def dot_nt(a, b):
    return lax.dot_general(a, b, (((1,), (1,)), ((), ())), preferred_element_type=F32)


def dot_tn(a, b):
    return lax.dot_general(a, b, (((0,), (0,)), ((), ())), preferred_element_type=F32)


def iota(shape, dim):
    return lax.broadcasted_iota(jnp.int32, shape, dim)


def chosen_copy(layer, own, other, dst, sem):
    sec = lax.axis_index("section")

    @pl.when(sec == layer)
    def _():
        pltpu.make_async_copy(own, dst, sem).start()

    @pl.when(sec != layer)
    def _():
        pltpu.make_async_copy(other, dst, sem).start()


def wait_copy(src, dst, sem):
    pltpu.make_async_copy(src, dst, sem).wait()


def silu_parts(v):
    s = jax.nn.sigmoid(v)
    return v * s, s * (1.0 + v * (1.0 - s))


def fwd_a_kernel(
    layer, rank, h_ref, rim_ref, gain_ref, ck_ref, cb_ref, xp_ref, dtp_ref, dtb_ref, mask_ref,
    in_own, in_oth,
    u_ref, xi_ref, z_ref, c_ref, proj_ref, beta_ref, ex_ref, us_ref, k2_ref, kb_ref, qb_ref, summ_ref,
    w_buf, sems,
):
    t_len, width = h_ref.shape
    inner = z_ref.shape[1]
    cb = 512
    n_chunk = 2 * inner // cb
    rim = rim_ref.shape[0]
    for k in range(n_chunk):
        at = pl.ds(k * cb, cb)
        chosen_copy(layer, in_own.at[:, at], in_oth.at[:, at], w_buf.at[:, at], sems.at[k])
    hf = jnp.concatenate([rim_ref[...], h_ref[...]], axis=0).astype(F32)
    inv = lax.rsqrt(jnp.mean(hf * hf, axis=-1, keepdims=True) + NORM_EPS)
    u_all = (hf * inv * gain_ref[...]).astype(BF)
    u_ref[...] = u_all[rim:]
    mask = mask_ref[...]
    proj = jnp.zeros((t_len, LANES), F32)
    for k in range(inner // cb):
        at = pl.ds(k * cb, cb)
        wait_copy(in_own.at[:, at], w_buf.at[:, at], sems.at[k])
        xi = dot(u_all, w_buf[:, at])
        xi_ref[:, at] = xi
        c = cb_ref[:, at] + ck_ref[3:4, at] * xi[rim:]
        for j in range(3):
            c = c + ck_ref[j : j + 1, at] * xi[rim - 3 + j : rim - 3 + j + t_len] * mask[:, j : j + 1]
        c_ref[:, at] = c
        xc = c * jax.nn.sigmoid(c)
        us_ref[:, at] = xc
        proj = proj + dot(xc.astype(BF), xp_ref[at, :])
    cols = iota((t_len, LANES), 1)
    keep = mask[:, 4:5]
    projb = jnp.where(cols == rank + 2 * N, keep, proj).astype(BF)
    proj_ref[...] = projb
    pf = projb.astype(F32)
    ksum = jnp.sum(jnp.where((cols >= rank) & (cols < rank + N), pf * pf, 0.0), axis=-1, keepdims=True)
    for k in range(inner // cb):
        at = pl.ds(k * cb, cb)
        beta = jax.nn.sigmoid(dot(projb, dtp_ref[:, at]) + dtb_ref[:, at])
        eps = beta / (1.0 + beta * ksum)
        beta_ref[:, at] = beta
        us_ref[:, at] = us_ref[:, at] * eps
        ex_ref[:, at] = jnp.where(keep > 0.0, eps, 1.0)
    rows = t_len * N
    sel = (iota((rows, t_len), 0) // N == iota((rows, t_len), 1)).astype(F32).astype(BF)
    spread = dot(sel, projb).astype(BF)
    rn = iota((rows, LANES), 0) % N
    cl = iota((rows, LANES), 1)
    ones = jnp.ones((LANES, LANES), BF)
    zero = jnp.zeros((rows, LANES), BF)
    kb = dot(jnp.where(cl == rank + rn, spread, zero), ones)
    qb = dot(jnp.where(cl == rank + N + rn, spread, zero), ones)
    keepb = dot(jnp.where(cl == rank + 2 * N, spread, zero), ones)
    kb_ref[...] = kb
    qb_ref[...] = qb
    k2_ref[...] = jnp.where(keepb > 0.5, -LOG2E * kb * kb, -1e30)
    ec = 512
    nt = ec // LANES
    un = 8

    def chunk(ci, carry):
        e0 = pl.multiple_of(ci * ec, ec)

        def body(i, sd):
            s, d = [list(v) for v in sd]
            g0 = pl.multiple_of(i * un, un)
            for t in range(un):
                r = pl.multiple_of(g0 * N + t * N, N)
                k2 = k2_ref[pl.ds(r, N), :]
                kv = kb_ref[pl.ds(r, N), :]
                for j in range(nt):
                    lane = pl.ds(e0 + LANES * j, LANES)
                    a = jnp.exp2(k2 * ex_ref.at[pl.ds(g0, un), lane][t : t + 1, :])
                    s[j] = a * s[j] + kv * us_ref.at[pl.ds(g0, un), lane][t : t + 1, :]
                    d[j] = a * d[j]
            return tuple(s), tuple(d)

        zeros = tuple(jnp.zeros((N, LANES), F32) for _ in range(nt))
        one = tuple(jnp.ones((N, LANES), F32) for _ in range(nt))
        s, d = lax.fori_loop(0, t_len // un, body, (zeros, one))
        for j in range(nt):
            lane = pl.ds(e0 + LANES * j, LANES)
            summ_ref[0:N, lane] = d[j].astype(BF)
            summ_ref[N : 2 * N, lane] = s[j].astype(BF)
        return carry

    lax.fori_loop(0, inner // ec, chunk, 0)
    for k in range(inner // cb, n_chunk):
        at = pl.ds(k * cb, cb)
        wait_copy(in_own.at[:, at], w_buf.at[:, at], sems.at[k])
        z_ref[:, pl.ds(k * cb - inner, cb)] = dot(u_all[rim:], w_buf[:, at])


def fwd_a(layer, rank, h, rim, w, mask, in_own, in_oth):
    t_len, width = h.shape
    inner = w["cb"].shape[1]
    rows = t_len * N

    def f32(*s):
        return jax.ShapeDtypeStruct(s, F32)

    def b16(*s):
        return jax.ShapeDtypeStruct(s, BF)

    return pl.pallas_call(
        functools.partial(fwd_a_kernel, layer, rank),
        out_shape=[
            b16(t_len, width), f32(t_len + rim.shape[0], inner), f32(t_len, inner), f32(t_len, inner),
            b16(t_len, LANES), f32(t_len, inner), f32(t_len, inner), f32(t_len, inner),
            f32(rows, LANES), f32(rows, LANES), f32(rows, LANES), b16(2 * N, inner),
        ],
        in_specs=[VSPEC] * 9 + [ANYSPEC] * 2,
        out_specs=[VSPEC] * 12,
        scratch_shapes=[pltpu.VMEM((width, 2 * inner), BF), pltpu.SemaphoreType.DMA((2 * inner // 512,))],
        compiler_params=params(),
        name=f"fwd_in_{layer}",
    )(h, rim, w["gain"], w["ck"], w["cb"], w["xp"], w["dtp"], w["dtb"], mask, in_own, in_oth)


def carry_kernel(n, reverse, *refs):
    if reverse:
        s_ref, d_ref, in_ref, recv, pre, send1, recv1, send2, recv2 = refs
        parts = 1
    else:
        s_ref, in_ref, d_ref, recv, pre, send1, recv1, send2, recv2 = refs
        parts = 2
    inner = s_ref.shape[1]
    blocks = min(n, inner // LANES)
    stride = n // blocks
    sec = lax.axis_index("section")
    me = lax.axis_index("ctx")
    mine = me // stride
    owner = lax.rem(me, stride) == 0

    def when(cond, fn):
        if stride == 1:
            fn()
        else:
            pl.when(cond)(fn)

    def peers(k):
        to = lax.rem(me + k, n)
        frm = lax.rem(me - k + n, n)
        return to, frm

    def first(k):
        to, frm = peers(k)
        lane = pl.ds(pl.multiple_of((to // stride) * LANES, LANES), LANES)
        return pltpu.make_async_remote_copy(
            src_ref=s_ref.at[:, lane], dst_ref=recv.at[me],
            send_sem=send1.at[k], recv_sem=recv1.at[me],
            device_id=(sec, to), device_id_type=MESH)

    def second(k):
        to, frm = peers(k)
        lane = pl.ds(pl.multiple_of(mine * LANES, LANES), LANES)
        return pltpu.make_async_remote_copy(
            src_ref=pre.at[to], dst_ref=in_ref.at[:, lane],
            send_sem=send2.at[k], recv_sem=recv2.at[me],
            device_id=(sec, to), device_id_type=MESH)

    barrier = pltpu.get_barrier_semaphore()
    for k in range(1, n):
        pl.semaphore_signal(barrier, inc=1, device_id=(sec, peers(k)[0]), device_id_type=MESH)
    pl.semaphore_wait(barrier, n - 1)
    for k in range(1, n):
        when(lax.rem(peers(k)[0], stride) == 0, lambda k=k: first(k).start())

    def own_part():
        lane = pl.ds(pl.multiple_of(mine * LANES, LANES), LANES)
        recv[me] = s_ref[:, lane]
        for k in range(1, n):
            frm = peers(k)[1]
            pltpu.make_async_remote_copy(
                src_ref=s_ref.at[:, pl.ds(0, LANES)], dst_ref=recv.at[frm],
                send_sem=send1.at[k], recv_sem=recv1.at[frm],
                device_id=(sec, frm), device_id_type=MESH).wait_recv()
        run = jnp.zeros((N, LANES), F32)
        for i in range(n):
            d = n - 1 - i if reverse else i
            pre[d] = run.astype(BF)
            if reverse:
                dec, st = d_ref[d], recv[d]
            else:
                dec, st = recv[d, 0:N, :], recv[d, N : 2 * N, :]
                d_ref[d] = dec
            run = dec.astype(F32) * run + st.astype(F32)
        for k in range(1, n):
            second(k).start()
        in_ref[:, lane] = pre[me]

    when(owner, own_part)
    for k in range(1, n):
        frm = peers(k)[1]

        def get(frm=frm, k=k):
            lane = pl.ds(pl.multiple_of((frm // stride) * LANES, LANES), LANES)
            pltpu.make_async_remote_copy(
                src_ref=pre.at[0], dst_ref=in_ref.at[:, lane],
                send_sem=send2.at[k], recv_sem=recv2.at[frm],
                device_id=(sec, frm), device_id_type=MESH).wait_recv()

        when(lax.rem(frm, stride) == 0, get)
    for k in range(1, n):
        when(lax.rem(peers(k)[0], stride) == 0, lambda k=k: first(k).wait_send())

    def sent():
        for k in range(1, n):
            second(k).wait_send()

    when(owner, sent)


def carry(n, reverse, cid, summ, decay=None):
    inner = summ.shape[1]
    got = jax.ShapeDtypeStruct((N, inner), BF)
    dec = jax.ShapeDtypeStruct((n, N, LANES), BF)
    rows = N if reverse else 2 * N
    sems = [pltpu.SemaphoreType.DMA((n,))] * 4
    return pl.pallas_call(
        functools.partial(carry_kernel, n, reverse),
        out_shape=[got] if reverse else [got, dec],
        in_specs=[VSPEC] * (2 if reverse else 1),
        out_specs=[VSPEC] * (1 if reverse else 2),
        scratch_shapes=[pltpu.VMEM((n, rows, LANES), BF), pltpu.VMEM((n, N, LANES), BF)] + sems,
        compiler_params=params(collective_id=cid, has_side_effects=True),
        name=f"carry_{cid}",
    )(*((summ, decay) if reverse else (summ,)))


def block_diag(projb, first_col):
    pick = (iota((LANES, BT * N), 0) == first_col + iota((LANES, BT * N), 1) % N).astype(F32).astype(BF)
    vals = dot(projb, pick)
    same = iota((BT, BT * N), 0) == iota((BT, BT * N), 1) // N
    return jnp.where(same, vals, 0.0)


def fwd_b_kernel(
    layer, rank, k2_ref, kb_ref, proj_ref, ex_ref, us_ref, c_ref, z_ref, skip_ref, sin_ref, h_ref, out_own, out_oth,
    s_ref, sb_ref, y_ref, o_ref, hout_ref,
    st, o_all, w_buf, sem,
):
    i = pl.program_id(0)
    inner = z_ref.shape[1]
    ec = 512
    nt = ec // LANES

    @pl.when(i == 0)
    def _():
        chosen_copy(layer, out_own, out_oth, w_buf, sem)
        st[...] = sin_ref[...].astype(F32)

    sb_ref[...] = st[...].astype(BF)
    qbd = block_diag(proj_ref[...], rank + N).astype(BF)
    for ci in range(inner // ec):
        e0 = ci * ec
        s = [st[:, pl.ds(e0 + LANES * j, LANES)] for j in range(nt)]
        for t in range(BT):
            k2 = k2_ref[t * N : (t + 1) * N, :]
            kv = kb_ref[t * N : (t + 1) * N, :]
            for j in range(nt):
                lane = pl.ds(e0 + LANES * j, LANES)
                a = jnp.exp2(k2 * ex_ref[t : t + 1, lane])
                s[j] = a * s[j] + kv * us_ref[t : t + 1, lane]
                s_ref[t * N : (t + 1) * N, lane] = s[j].astype(BF)
        for j in range(nt):
            st[:, pl.ds(e0 + LANES * j, LANES)] = s[j]
        at = pl.ds(e0, ec)
        c = c_ref[:, at]
        y = dot(qbd, s_ref[:, at]) + skip_ref[:, at] * (c * jax.nn.sigmoid(c))
        y_ref[:, at] = y
        z = z_ref[:, at]
        o = (y * (z * jax.nn.sigmoid(z))).astype(BF)
        o_ref[:, at] = o
        o_all[pl.ds(pl.multiple_of(i * BT, BT), BT), at] = o

    @pl.when(i == pl.num_programs(0) - 1)
    def _():
        wait_copy(out_own, w_buf, sem)
        hout_ref[...] = (h_ref[...].astype(F32) + dot(o_all[...], w_buf[...])).astype(BF)


def fwd_b(layer, rank, h, fa, sin, w, out_own, out_oth):
    t_len, width = h.shape
    inner = w["cb"].shape[1]

    def blk(r, c):
        return pl.BlockSpec((r, c), lambda i: (i, 0))

    def whole(r, c):
        return pl.BlockSpec((r, c), lambda i: (0, 0))

    return pl.pallas_call(
        functools.partial(fwd_b_kernel, layer, rank),
        grid=(t_len // BT,),
        in_specs=[
            blk(BT * N, LANES), blk(BT * N, LANES), blk(BT, LANES), blk(BT, inner), blk(BT, inner), blk(BT, inner),
            blk(BT, inner), whole(1, inner), whole(N, inner), whole(t_len, width), ANYSPEC, ANYSPEC,
        ],
        out_specs=[blk(BT * N, inner), blk(BT, inner), blk(BT, inner), blk(BT, inner), whole(t_len, width)],
        out_shape=[
            jax.ShapeDtypeStruct((t_len * N, inner), BF), jax.ShapeDtypeStruct((t_len, inner), BF),
            jax.ShapeDtypeStruct((t_len, inner), F32), jax.ShapeDtypeStruct((t_len, inner), BF),
            jax.ShapeDtypeStruct((t_len, width), BF),
        ],
        scratch_shapes=[
            pltpu.VMEM((N, inner), F32), pltpu.VMEM((t_len, inner), BF), pltpu.VMEM((inner, width), BF),
            pltpu.SemaphoreType.DMA(()),
        ],
        compiler_params=params(),
        name=f"fwd_out_{layer}",
    )(fa["k2"], fa["kb"], fa["proj"], fa["ex"], fa["us"], fa["c"], fa["z"], w["skip"], sin, h, out_own, out_oth)


def coords(n):
    bits = n.bit_length() - 1
    me = lax.axis_index("ctx")
    return bits, me, [lax.rem(me // 2**b, 2) for b in range(bits)]


def unpack_index(k, dims):
    return tuple(lax.rem(k // 2 ** (dims - 1 - d), 2) for d in range(dims))


def bit_orders(bits):
    low = list(range(bits))
    return [low, [1, 0] + low[2:], [2, 0, 1] + low[3:]]


class Sub:
    def __init__(self, kit, num, buf, sib, recvs, out, lane0, lanes, order):
        self.kit, self.num, self.order = kit, num, order
        self.at = pl.ds(lane0, lanes)
        self.buf, self.sib, self.recvs, self.out = buf, sib, recvs, out
        self.layer = 1
        self.stage = 0

    def lead(self, dims):
        return (slice(None),) * dims

    def partner(self, r):
        kit = self.kit
        b = self.order[r]
        return (kit.sec, kit.me + 2**b * (1 - 2 * kit.mybit[b]))

    def index(self, r, last):
        idx = [slice(None)] * self.kit.bits
        for q in range(r):
            b = self.order[q]
            idx[self.kit.bits - 1 - b] = self.kit.mybit[b]
        b = self.order[r]
        idx[self.kit.bits - 1 - b] = (1 - self.kit.mybit[b]) if last else self.kit.mybit[b]
        return tuple(idx)

    def copy(self, stage):
        kit = self.kit
        bits = kit.bits
        if stage == 0:
            src = self.buf.at[(1 - kit.sec,) + self.lead(bits + 1) + (self.at,)]
            dst = self.sib.at[self.lead(bits + 1) + (self.at,)]
            to = (1 - kit.sec, kit.me)
        else:
            r = stage - 1
            src = self.buf.at[(kit.sec,) + self.index(r, True) + (slice(None), self.at)]
            dst = self.recvs[r].at[self.lead(bits - r) + (self.at,)]
            to = self.partner(r)
        return pltpu.make_async_remote_copy(
            src_ref=src, dst_ref=dst, send_sem=kit.ssem.at[self.num, stage], recv_sem=kit.rsem.at[self.num, stage],
            device_id=to, device_id_type=MESH)

    def start(self, stage):
        if self.layer == 0:
            pl.semaphore_wait(self.kit.cred.at[self.num, stage], 1)
        self.copy(stage).start()

    def begin(self, layer):
        self.layer = layer
        self.stage = 0
        self.start(0)

    def final(self):
        kit = self.kit
        return pltpu.make_async_remote_copy(
            src_ref=kit.res[self.out].at[:, self.at], dst_ref=self.place(1 - self.layer),
            send_sem=kit.fsem.at[self.layer, self.num], recv_sem=kit.frsem.at[self.layer, self.num],
            device_id=(1 - kit.sec, kit.me), device_id_type=MESH)

    def place(self, half):
        return self.kit.place[self.out](half, self.at)

    def advance(self):
        kit = self.kit
        bits, s = kit.bits, self.stage
        if s > bits:
            return
        self.copy(s).wait_recv()
        if s == 0:
            dims = bits

            def body(k, carry):
                idx = unpack_index(k, dims) + (slice(None), self.at)
                dst = (kit.sec,) + idx
                self.buf[dst] = self.buf[dst] + self.sib[idx]
                return carry

            lax.fori_loop(0, 2**dims, body, 0)
        else:
            r = s - 1
            dims = bits - 1 - r
            fixed = self.index(r, False)
            res = kit.res[self.out]

            def body(k, carry):
                sub = list(unpack_index(k, dims))
                src = tuple(sub) + (slice(None), self.at)
                full = tuple(sub.pop(0) if isinstance(f, slice) else f for f in fixed)
                dst = (kit.sec,) + full + (slice(None), self.at)
                if s == bits:
                    val = self.buf[dst].astype(F32) + self.recvs[r][src].astype(F32)

                    @pl.when(kit.sec == self.layer)
                    def _():
                        self.place(self.layer)[...] = val

                    @pl.when(kit.sec != self.layer)
                    def _():
                        res[:, self.at] = val
                else:
                    self.buf[dst] = self.buf[dst] + self.recvs[r][src]
                return carry

            if dims:
                lax.fori_loop(0, 2**dims, body, 0)
            else:
                body(0, 0)
        if self.layer == 1:
            to = (1 - kit.sec, kit.me) if s == 0 else self.partner(s - 1)
            pl.semaphore_signal(kit.cred.at[self.num, s], inc=1, device_id=to, device_id_type=MESH)
        self.stage = s + 1
        if s < bits:
            self.start(s + 1)
        else:
            @pl.when(kit.sec != self.layer)
            def _():
                self.final().start()

    def drain(self):
        while self.stage <= self.kit.bits:
            self.advance()
        for s in range(self.kit.bits + 1):
            self.copy(s).wait_send()

    def finish(self, layer):
        self.layer = layer

        @pl.when(self.kit.sec != layer)
        def _():
            self.final().wait_send()

        @pl.when(self.kit.sec == layer)
        def _():
            self.final().wait_recv()


class VecSum:
    def __init__(self, kit, layer, acc, send, recv):
        self.kit, self.layer, self.acc, self.send, self.recv = kit, layer, acc, send, recv
        self.stage = 0

    def copy(self, s):
        kit = self.kit
        if s == 0:
            to = (1 - kit.sec, kit.me)
        else:
            to = (kit.sec, kit.me + 2 ** (s - 1) * (1 - 2 * kit.mybit[s - 1]))
        return pltpu.make_async_remote_copy(
            src_ref=self.send.at[self.layer, s], dst_ref=self.recv.at[self.layer, s],
            send_sem=kit.vsem.at[self.layer, s], recv_sem=kit.vrsem.at[self.layer, s],
            device_id=to, device_id_type=MESH)

    def start(self, s):
        self.send[self.layer, s] = self.acc[self.layer].astype(BF)
        self.copy(s).start()

    def begin(self):
        self.start(0)

    def advance(self):
        s = self.stage
        if s > self.kit.bits:
            return
        self.copy(s).wait_recv()
        self.acc[self.layer] = self.send[self.layer, s].astype(F32) + self.recv[self.layer, s].astype(F32)
        self.stage = s + 1
        if s < self.kit.bits:
            self.start(s + 1)

    def drain(self):
        while self.stage <= self.kit.bits:
            self.advance()
        for s in range(self.kit.bits + 1):
            self.copy(s).wait_send()


class Kit:
    pass


class Carry:
    def __init__(self, sec, me, n, src, recv, pre, dst, sems, decay, inner):
        self.sec, self.me, self.n = sec, me, n
        self.src, self.recv, self.pre, self.dst, self.decay = src, recv, pre, dst, decay
        self.send1, self.recv1, self.send2, self.recv2 = sems
        self.blocks = min(n, inner // LANES)
        self.stride = n // self.blocks
        self.mine = me // self.stride
        self.reverse = decay is not None

    def when(self, cond, fn):
        if self.stride == 1:
            fn()
        else:
            pl.when(cond)(fn)

    def to(self, k):
        return lax.rem(self.me + k, self.n)

    def frm(self, k):
        return lax.rem(self.me - k + self.n, self.n)

    def lane(self, dev):
        return pl.ds(pl.multiple_of((dev // self.stride) * LANES, LANES), LANES)

    def owns(self, dev):
        return lax.rem(dev, self.stride) == 0

    def first(self, k, dev, slot):
        return pltpu.make_async_remote_copy(
            src_ref=self.src.at[:, self.lane(dev)], dst_ref=self.recv.at[slot],
            send_sem=self.send1.at[k], recv_sem=self.recv1.at[slot],
            device_id=(self.sec, dev), device_id_type=MESH)

    def second(self, k, dev, frm):
        return pltpu.make_async_remote_copy(
            src_ref=self.pre.at[dev], dst_ref=self.dst.at[:, self.lane(frm)],
            send_sem=self.send2.at[k], recv_sem=self.recv2.at[frm],
            device_id=(self.sec, dev), device_id_type=MESH)

    def send(self):
        for k in range(1, self.n):
            self.when(self.owns(self.to(k)), lambda k=k: self.first(k, self.to(k), self.me).start())

    def combine(self):
        def own():
            self.recv[self.me] = self.src[:, self.lane(self.me)]
            for k in range(1, self.n):
                self.first(k, self.frm(k), self.frm(k)).wait_recv()
            run = jnp.zeros((N, LANES), F32)
            for i in range(self.n):
                d = self.n - 1 - i if self.reverse else i
                self.pre[d] = run.astype(BF)
                if self.reverse:
                    dec, st = self.decay[d], self.recv[d]
                else:
                    dec, st = self.recv[d, 0:N, :], self.recv[d, N : 2 * N, :]
                run = dec.astype(F32) * run + st.astype(F32)
            for k in range(1, self.n):
                self.second(k, self.to(k), self.me).start()
            self.dst[:, self.lane(self.me)] = self.pre[self.me]

        self.when(self.owns(self.me), own)

    def get(self):
        for k in range(1, self.n):
            self.when(
                self.owns(self.frm(k)),
                lambda k=k: pltpu.make_async_remote_copy(
                    src_ref=self.pre.at[0], dst_ref=self.dst.at[:, self.lane(self.frm(k))],
                    send_sem=self.send2.at[k], recv_sem=self.recv2.at[self.frm(k)],
                    device_id=(self.sec, self.frm(k)), device_id_type=MESH).wait_recv())

    def sent(self):
        for k in range(1, self.n):
            self.when(self.owns(self.to(k)), lambda k=k: self.first(k, self.to(k), self.me).wait_send())

        def own():
            for k in range(1, self.n):
                self.second(k, self.to(k), self.me).wait_send()

        self.when(self.owns(self.me), own)


LOADS = ("h", "u", "xi", "z", "c", "proj", "beta", "ex", "us", "k2", "qb", "sb", "y", "o", "dec")
BOTH = ("h", "u", "proj", "dec", "sb")
WSMALL = ("gain", "ck", "skip", "xp", "dtp")


def lane_parts(lanes):
    unit = lanes // LANES
    if unit < 3:
        return [(0, lanes)]
    a = -(-3 * unit // 8)
    b = min(a, unit - a - 1)
    return [(0, a * LANES), (a * LANES, b * LANES), ((a + b) * LANES, (unit - a - b) * LANES)]


def back_kernel(n, rank, shapes, *refs):
    refs = list(refs)

    def take(k):
        out = refs[:k]
        del refs[:k]
        return out

    cot_hbm, mask_ref, in_own, in_oth, out_own, out_oth = take(6)
    hbm = [dict(zip(LOADS + ("s",), take(len(LOADS) + 1))) for _ in range(2)]
    wts = [dict(zip(WSMALL, take(len(WSMALL)))) for _ in range(2)]
    dh_out, gin_out, gout_out, gsm_out, vec_out = take(5)
    loc = {name: (take(2) if name in BOTH else take(1) * 2) for name in LOADS}
    (g_ref, w_out, w_in, sbuf, qs2, ws2, bst, deps, dkq, dy_ref, dz_ref, gdt_ref, gtmp, rims, rimr) = take(15)
    dxc = loc["y"][0]
    bufs = dict(zip(("go", "gz", "gx", "sm"), take(4)))
    sibs = dict(zip(("go", "gz", "gx", "sm"), take(4)))
    kit = Kit()
    bits, me, mybit = coords(n)
    recvs = {name: take(bits) for name in ("go", "gz", "gx", "sm")}
    kit.res = dict(zip(("go", "gz", "gx", "sm"), take(4)))
    vacc, vsend, vrecv = take(3)
    c_src, c_recv, c_pre, c_dst = take(4)
    (ld_sem, g_sem, wo_sem, wi_sem, s_sem, rim_sem, rimr_sem, kit.ssem, kit.rsem, kit.cred, kit.fsem, kit.frsem,
     kit.vsem, kit.vrsem, c1, c2, c3, c4) = take(18)
    assert not refs
    sec = lax.axis_index("section")
    kit.sec, kit.me, kit.bits, kit.mybit = sec, me, bits, mybit
    t_len, width = dh_out.shape
    inner = w_out.shape[0]
    cb = 512
    lead = shapes["lead"]

    barrier = pltpu.get_barrier_semaphore()
    for k in range(1, n):
        pl.semaphore_signal(barrier, inc=1, device_id=(sec, lax.rem(me + k, n)), device_id_type=MESH)
    pl.semaphore_signal(barrier, inc=1, device_id=(1 - sec, me), device_id_type=MESH)

    pos = {name: i for i, name in enumerate(LOADS)}

    def load(name, layer):
        return pltpu.make_async_copy(hbm[layer][name], loc[name][layer], ld_sem.at[pos[name], layer])

    def out_chunk(k, src):
        at = pl.ds(k * cb, cb)
        return src.at[at, :], w_out.at[at, :], wo_sem.at[k]

    def in_chunk(k, slot, src):
        return src.at[:, pl.ds(k * cb, cb)], w_in.at[slot], wi_sem.at[slot]

    def fetch(layer, chunk, own, oth):
        a, b, s = chunk(own)
        a2 = chunk(oth)[0]

        @pl.when(sec == layer)
        def _():
            pltpu.make_async_copy(a, b, s).start()

        @pl.when(sec != layer)
        def _():
            pltpu.make_async_copy(a2, b, s).start()

    def arrive(chunk, own):
        a, b, s = chunk(own)
        pltpu.make_async_copy(a, b, s).wait()

    n_out = inner // cb
    n_in = 2 * inner // cb
    in_order = list(range(n_in // 2, n_in)) + list(range(n_in // 2))
    slots = w_in.shape[0]

    pltpu.make_async_copy(cot_hbm, g_ref, g_sem).start()
    for k in range(n_out):
        fetch(1, lambda src, k=k: out_chunk(k, src), out_own, out_oth)
    for name in ("z", "y", "c", "ex", "k2", "qb", "o", "u", "dec", "proj", "beta", "us", "sb", "xi", "h"):
        load(name, 1).start()
    for name in BOTH:
        load(name, 0).start()
    for i in range(slots):
        fetch(1, lambda src, i=i: in_chunk(in_order[i], i, src), in_own, in_oth)

    half_go = width // 2
    half_in = inner // 2
    kit.place = {
        "go": lambda hf, at: gout_out.at[:, pl.ds(hf * half_go + at.start, at.size)],
        "gz": lambda hf, at: gin_out.at[:, pl.ds(inner + hf * half_in + at.start, at.size)],
        "gx": lambda hf, at: gin_out.at[:, pl.ds(hf * half_in + at.start, at.size)],
        "sm": lambda hf, at: gsm_out.at[hf, :, at],
    }
    order3 = bit_orders(bits)[:3]
    subs = {}
    num = 0
    for name, lanes in (("go", half_go), ("gz", half_in), ("gx", half_in), ("sm", LANES)):
        parts = lane_parts(lanes)
        subs[name] = []
        for i, (l0, ln) in enumerate(parts):
            subs[name].append(Sub(kit, num, bufs[name], sibs[name], recvs[name], name, l0, ln, order3[i]))
            num += 1

    def begin(name, layer):
        for s in subs[name]:
            s.begin(layer)

    def advance(*names):
        for name in names:
            if isinstance(name, VecSum):
                name.advance()
                continue
            for s in subs[name]:
                s.advance()

    def drain(*names):
        for name in names:
            for s in subs[name]:
                s.drain()

    rows_go = inner // n
    rows_in = width // n
    rows_sm = inner // n

    def owner(j):
        return tuple((j >> (bits - 1 - d)) & 1 for d in range(bits))

    pl.semaphore_wait(barrier, n)
    vecs = [VecSum(kit, layer, vacc, vsend, vrecv) for layer in range(2)]
    pltpu.make_async_copy(cot_hbm, g_ref, g_sem).wait()

    carries = []
    for layer in (1, 0):
        late = vecs[1] if layer == 0 else None
        L = {name: loc[name][layer] for name in LOADS}
        w = wts[layer]
        vacc[layer] = jnp.zeros(vacc.shape[1:], F32)
        if layer == 0:
            advance("gx", "sm", late)
        for name in ("z", "y", "c"):
            load(name, layer).wait()
        dr = g_ref[...]
        for k in range(n_out):
            at = pl.ds(k * cb, cb)
            arrive(lambda src, k=k: out_chunk(k, src), out_own)
            do = dot_nt(dr, w_out[at, :])
            act, der = silu_parts(L["z"][:, at])
            dy = do * act
            dy_ref[:, at] = dy
            dz_ref[:, at] = (do * L["y"][:, at] * der).astype(BF)
            c = L["c"][:, at]
            vacc[layer, 6:7, at] = jnp.sum(dy * (c * jax.nn.sigmoid(c)), axis=0, keepdims=True)
        if layer == 1:
            for k in range(n_out):
                fetch(0, lambda src, k=k: out_chunk(k, src), out_own, out_oth)
            load("z", 0).start()
        for name in ("ex", "k2", "qb"):
            load(name, layer).wait()
        k2_ref, qb_ref, ex_ref = L["k2"], L["qb"], L["ex"]
        ec = 512
        nt = ec // LANES
        un = 8

        def chunk(ci, carry, k2_ref=k2_ref, qb_ref=qb_ref, ex_ref=ex_ref, layer=layer):
            e0 = pl.multiple_of(ci * ec, ec)

            def body(i, b):
                b = list(b)
                g0 = pl.multiple_of((t_len // un - 1 - i) * un, un)
                for t in range(un - 1, -1, -1):
                    r = pl.multiple_of(g0 * N + t * N, N)
                    k2 = k2_ref[pl.ds(r, N), :]
                    qv = qb_ref[pl.ds(r, N), :]
                    for j in range(nt):
                        lane = pl.ds(e0 + LANES * j, LANES)
                        a = jnp.exp2(k2 * ex_ref.at[pl.ds(g0, un), lane][t : t + 1, :])
                        b[j] = a * (qv * dy_ref.at[pl.ds(g0, un), lane][t : t + 1, :] + b[j])
                return tuple(b)

            b = lax.fori_loop(0, t_len // un, body, tuple(jnp.zeros((N, LANES), F32) for _ in range(nt)))
            for j in range(nt):
                c_src[layer, :, pl.ds(e0 + LANES * j, LANES)] = b[j].astype(BF)
            return carry

        lax.fori_loop(0, inner // ec, chunk, 0)
        load("dec", layer).wait()
        cr = Carry(sec, me, n, c_src.at[layer], c_recv.at[layer], c_pre.at[layer], c_dst.at[layer],
                   [s.at[layer] for s in (c1, c2, c3, c4)], L["dec"], inner)
        carries.append(cr)
        cr.send()
        for name in ("o", "u"):
            load(name, layer).wait()
        if layer == 0:
            drain("go", "gz")
            advance("gx", "sm", late)
        u = L["u"][...]
        per = cb // rows_go
        for k in range(n_out):
            at = pl.ds(k * cb, cb)
            go = dot_tn(L["o"][:, at], dr).astype(BF)
            for i in range(per):
                piece = go[i * rows_go : (i + 1) * rows_go]
                for hf in range(2):
                    bufs["go"][(hf,) + owner(k * per + i)] = piece[:, hf * half_go : (hf + 1) * half_go]
        def in_grad(name, grad_at):
            for k in range(n_out):
                g = dot_tn(u, grad_at(pl.ds(k * cb, cb))).astype(BF)
                hf = (k * cb) // half_in
                l0 = k * cb - hf * half_in
                for j in range(n):
                    bufs[name][(hf,) + owner(j) + (slice(None), pl.ds(l0, cb))] = g[j * rows_in : (j + 1) * rows_in]

        in_grad("gz", lambda at: dz_ref[:, at])
        begin("go", layer)
        begin("gz", layer)
        cr.combine()
        if layer == 1:
            load("o", 0).start()
        advance("go", "gz")
        if layer == 0:
            advance("gx", "sm", late)
        steps = t_len // BT

        def s_copy(blk, slot, layer=layer):
            return pltpu.make_async_copy(
                hbm[layer]["s"].at[pl.ds(pl.multiple_of(blk * BT * N, BT * N), BT * N), :], sbuf.at[slot],
                s_sem.at[slot])

        s_copy(steps - 1, 0).start()
        for name in ("proj", "beta", "us", "sb"):
            load(name, layer).wait()
        cr.get()
        bst[...] = c_dst[layer].astype(F32)

        def block(i, carry, L=L, w=w, s_copy=s_copy):
            blk = steps - 1 - i
            slot = lax.rem(i, 2)
            base = pl.multiple_of(blk * BT, BT)
            rows = pl.ds(base, BT)
            rbase = pl.multiple_of(blk * BT * N, BT * N)

            @pl.when(i + 1 < steps)
            def _():
                s_copy(blk - 1, 1 - slot).start()

            s_copy(blk, slot).wait()
            projb = L["proj"][rows, :]
            pf = projb.astype(F32)
            cols = iota((BT, LANES), 1)
            is_k = (cols >= rank) & (cols < rank + N)
            ksum = jnp.sum(jnp.where(is_k, pf * pf, 0.0), axis=-1, keepdims=True)
            kbd = block_diag(projb, rank)
            k2bd = (kbd * kbd).astype(BF)
            kbd = kbd.astype(BF)
            r1 = jnp.zeros((BT, BT * N), F32)
            r2 = jnp.zeros((BT, BT * N), F32)
            r3 = jnp.zeros((BT, BT * N), F32)
            s_blk = sbuf.at[slot]
            for ci in range(inner // ec):
                e0 = ci * ec
                qs, ws = qs2.at[ci % 2], ws2.at[ci % 2]
                b = [bst[:, pl.ds(e0 + LANES * j, LANES)] for j in range(nt)]
                for t in range(BT - 1, -1, -1):
                    row = slice(t * N, (t + 1) * N)
                    krow = pl.ds(pl.multiple_of(rbase + t * N, N), N)
                    k2 = L["k2"][krow, :]
                    qv = L["qb"][krow, :]
                    for j in range(nt):
                        lane = pl.ds(e0 + LANES * j, LANES)
                        a = jnp.exp2(k2 * L["ex"].at[rows, lane][t : t + 1, :])
                        q = qv * dy_ref.at[rows, lane][t : t + 1, :] + b[j]
                        b[j] = a * q
                        prev = s_blk[(t - 1) * N : t * N, lane] if t > 0 else L["sb"][rows, lane]
                        qs[row, LANES * j : LANES * (j + 1)] = q.astype(BF)
                        ws[row, LANES * j : LANES * (j + 1)] = (b[j] * prev.astype(F32)).astype(BF)
                for j in range(nt):
                    bst[:, pl.ds(e0 + LANES * j, LANES)] = b[j]
                at = pl.ds(e0, ec)
                p1 = dot(kbd, qs[...])
                p2 = dot(k2bd, ws[...])
                c = L["c"][rows, at]
                beta = L["beta"][rows, at]
                eps = beta / (1.0 + beta * ksum)
                dy = dy_ref[rows, at]
                deps[rows, at] = (c * jax.nn.sigmoid(c)) * p1 - p2
                dxc[rows, at] = dy * w["skip"][:, at] + eps * p1
                r1 = r1 + dot_nt(L["us"][rows, at].astype(BF), qs[...])
                r2 = r2 + dot_nt(eps.astype(BF), ws[...])
                r3 = r3 + dot_nt(dy.astype(BF), s_blk[:, at])
            same = iota((BT, BT * N), 0) == iota((BT, BT * N), 1) // N
            gather_k = (iota((BT * N, LANES), 1) == rank + iota((BT * N, LANES), 0) % N).astype(F32)
            gather_q = (iota((BT * N, LANES), 1) == rank + N + iota((BT * N, LANES), 0) % N).astype(F32)

            def pick(r, g):
                return jnp.dot(
                    jnp.where(same, r, 0.0), g, precision=lax.Precision.HIGHEST, preferred_element_type=F32)

            dkq[rows, :] = pick(r1, gather_k) - 2.0 * pf * pick(r2, gather_k) + pick(r3, gather_q)
            return carry

        def ticks(first_half):
            if first_half:
                advance("go", "gz")
                if layer == 0:
                    advance("gx", "sm", late)
            else:
                advance("go", "gz")
                if layer == 0:
                    advance("gx", "sm", late)

        state = {}

        def block_and_tick(i, carry):
            block(i, carry)

            @pl.when(i == steps // 2 - 1)
            def _():
                ticks(True)

            @pl.when(i == steps - 1)
            def _():
                ticks(False)

            return carry

        lax.fori_loop(0, steps, block_and_tick, 0)
        if layer == 1:
            for name in ("k2", "qb", "ex", "us"):
                load(name, 0).start()
        load("xi", layer).wait()
        projw = L["proj"][...]
        pw = projw.astype(F32)
        colw = iota((t_len, LANES), 1)
        kall = jnp.where((colw >= rank) & (colw < rank + N), pw, 0.0)
        ks = jnp.sum(kall * kall, axis=-1, keepdims=True)
        tc = 256
        if layer == 0:
            drain("sm", "gx")

        def first(k, carry, L=L, w=w, layer=layer, projw=projw, ks=ks):
            dkc, ddt = carry
            at = pl.ds(pl.multiple_of(k * tc, tc), tc)
            beta = L["beta"][:, at]
            inv = 1.0 / (1.0 + beta * ks)
            dq = deps[:, at] * (inv * inv)
            dkc = dkc + jnp.sum(dq * beta * beta, axis=-1, keepdims=True)
            dp = (dq * beta * (1.0 - beta)).astype(BF)
            vacc[layer, 5:6, at] = jnp.sum(dp.astype(F32), axis=0, keepdims=True)
            gdt_ref[:, at] = dot_tn(projw, dp)[:rank]
            ddt = ddt + dot_nt(dp, w["dtp"][:, at])
            return dkc, ddt

        dkc, ddt = lax.fori_loop(
            0, inner // tc, first, (jnp.zeros((t_len, 1), F32), jnp.zeros((t_len, LANES), F32)))
        dproj = (jnp.where(colw < rank, ddt, dkq[...]) - 2.0 * kall * dkc).astype(BF)
        mask = mask_ref[...]
        ck_ref = w["ck"]

        def second(k, carry, L=L, w=w, layer=layer, dproj=dproj, ck_ref=ck_ref):
            at = pl.ds(pl.multiple_of(k * tc, tc), tc)
            c = L["c"][:, at]
            act, der = silu_parts(c)
            gxp = dot_tn(act.astype(BF), dproj).astype(BF)
            for i in range(tc // rows_sm):
                j = k * (tc // rows_sm) + i
                bufs["sm"][(0,) + unpack_index(j, bits)] = gxp[i * rows_sm : (i + 1) * rows_sm]
            dc = (dxc[:, at] + dot_nt(dproj, w["xp"][at, :])) * der
            vacc[layer, 4:5, at] = jnp.sum(dc, axis=0, keepdims=True)
            xi = L["xi"][:, at]
            pad = jnp.zeros((8, tc), F32)
            dxi = ck_ref[3:4, at] * dc
            rim = jnp.zeros((8, tc), F32)
            vacc[layer, 3:4, at] = jnp.sum(dc * xi[lead:], axis=0, keepdims=True)
            for j in range(3):
                m = dc * mask[:, j : j + 1]
                vacc[layer, j : j + 1, at] = jnp.sum(m * xi[lead - 3 + j : lead - 3 + j + t_len], axis=0, keepdims=True)
                m = m * ck_ref[j : j + 1, at]
                ext = jnp.concatenate([pad, m, pad], axis=0)
                dxi = dxi + ext[8 + 3 - j : 8 + 3 - j + t_len]
                rim = rim + ext[8 - j : 16 - j]
            deps[:, at] = dxi
            rims[layer, :, at] = jnp.where(iota((8, tc), 0) < 3, rim, 0.0)
            return carry

        lax.fori_loop(0, inner // tc, second, 0)

        def rim_copy(to, layer=layer):
            return pltpu.make_async_remote_copy(
                src_ref=rims.at[layer], dst_ref=rimr.at[layer], send_sem=rim_sem.at[layer], recv_sem=rimr_sem.at[layer],
                device_id=(sec, to), device_id_type=MESH)

        @pl.when(me > 0)
        def _():
            rim_copy(me - 1).start()

        @pl.when(me == n - 1)
        def _():
            rimr[layer] = jnp.zeros(rimr.shape[1:], F32)

        if layer == 1:
            for name in ("c", "beta", "xi", "y"):
                load(name, 0).start()
        prow = rank // n
        for j in range(n):
            for t in range(inner // LANES):
                gtmp[j, t * prow : (t + 1) * prow, :] = gdt_ref[j * prow : (j + 1) * prow, t * LANES : (t + 1) * LANES]
        drow = prow * (inner // LANES)
        for j in range(n):
            bufs["sm"][(1,) + owner(j) + (slice(0, drow),)] = gtmp[j, 0:drow].astype(BF)
        advance("go", "gz")
        du = jnp.zeros((t_len, width), F32)

        def project(du, i, g, layer=layer):
            slot = i % slots
            arrive(lambda src: in_chunk(in_order[i], slot, src), in_own)
            du = du + dot_nt(g, w_in[slot])
            if i + slots < n_in:
                fetch(layer, lambda src: in_chunk(in_order[i + slots], slot, src), in_own, in_oth)
            elif layer == 1:
                fetch(0, lambda src: in_chunk(in_order[i + slots - n_in], slot, src), in_own, in_oth)
            return du

        for i in range(n_in // 2):
            du = project(du, i, dz_ref[:, pl.ds(i * cb, cb)])

        @pl.when(me < n - 1)
        def _():
            rim_copy(me).wait_recv()

        tail = jnp.concatenate([jnp.zeros((5, inner), F32), rimr[layer][0:3]], axis=0)
        deps[pl.ds(t_len - 8, 8), :] = deps[pl.ds(t_len - 8, 8), :] + tail
        in_grad("gx", lambda at: deps[:, at].astype(BF))
        begin("gx", layer)
        begin("sm", layer)
        for i in range(n_in // 2, n_in):
            du = project(du, i, deps[:, pl.ds((i - n_in // 2) * cb, cb)].astype(BF))
        load("h", layer).wait()
        hf = L["h"][...].astype(F32)
        inv = lax.rsqrt(jnp.mean(hf * hf, axis=-1, keepdims=True) + NORM_EPS)
        unit = hf * inv
        vacc[layer, 7:8, pl.ds(0, width)] = jnp.sum(du * unit, axis=0, keepdims=True)
        dn = du * w["gain"][...]
        dh = g_ref[...].astype(F32) + inv * (dn - unit * jnp.mean(dn * unit, axis=-1, keepdims=True))
        if layer == 1:
            g_ref[...] = dh.astype(BF)
        else:
            dh_out[...] = dh.astype(BF)
        vecs[layer].begin()
        advance("go", "gz")

    drain("go", "gz")
    while any(s.stage <= bits for s in subs["gx"] + subs["sm"]) or vecs[0].stage <= bits:
        advance("gx", "sm", vecs[0])
    drain("gx", "sm")
    for v in vecs:
        v.drain()
    for layer in range(2):
        vec_out[layer] = vacc[layer]
        for name in ("go", "gz", "gx", "sm"):
            for s in subs[name]:
                s.finish(layer)

    @pl.when(me > 0)
    def _():
        for layer in range(2):
            pltpu.make_async_remote_copy(
                src_ref=rims.at[layer], dst_ref=rimr.at[layer], send_sem=rim_sem.at[layer], recv_sem=rimr_sem.at[layer],
                device_id=(sec, me - 1), device_id_type=MESH).wait_send()

    for cr in carries:
        cr.sent()


def backward(n, rank, cid, cot, mask, in_own, in_oth, out_own, out_oth, saved, weights):
    t_len, width = cot.shape
    inner = weights[0]["cb"].shape[1]
    bits = n.bit_length() - 1
    lead = saved[0]["xi"].shape[0] - t_len
    args = [cot, mask, in_own, in_oth, out_own, out_oth]
    specs = [ANYSPEC, VSPEC] + [ANYSPEC] * 4
    for layer in range(2):
        args += [saved[layer][name] for name in LOADS + ("s",)]
        specs += [ANYSPEC] * (len(LOADS) + 1)
    for layer in range(2):
        args += [weights[layer][name] for name in WSMALL]
        specs += [VSPEC] * len(WSMALL)
    rows_go, rows_in, rows_sm = inner // n, width // n, inner // n

    def sd(t, *s):
        return jax.ShapeDtypeStruct(s, t)

    outs = [
        sd(BF, t_len, width), sd(F32, rows_in, 2 * inner), sd(F32, rows_go, width), sd(F32, 2, rows_sm, LANES),
        sd(F32, 2, 16, inner),
    ]
    scratch = []
    for name in LOADS:
        a = saved[0][name]
        scratch += [pltpu.VMEM(a.shape, a.dtype)] * (2 if name in BOTH else 1)
    slots = 4
    scratch += [
        pltpu.VMEM((t_len, width), BF), pltpu.VMEM((inner, width), BF), pltpu.VMEM((slots, width, 512), BF),
        pltpu.VMEM((2, BT * N, inner), BF), pltpu.VMEM((2, BT * N, 512), BF), pltpu.VMEM((2, BT * N, 512), BF),
        pltpu.VMEM((N, inner), F32), pltpu.VMEM((t_len, inner), F32),
        pltpu.VMEM((t_len, LANES), F32), pltpu.VMEM((t_len, inner), F32), pltpu.VMEM((t_len, inner), BF),
        pltpu.VMEM((rank, inner), F32), pltpu.VMEM((n, max(8, rank * inner // (LANES * n)), LANES), F32),
        pltpu.VMEM((2, 8, inner), F32), pltpu.VMEM((2, 8, inner), F32),
    ]
    dims = (("go", rows_go, width // 2), ("gz", rows_in, inner // 2), ("gx", rows_in, inner // 2), ("sm", rows_sm, LANES))
    two = (2,) * bits
    scratch += [pltpu.VMEM((2,) + two + (r, ln), BF) for _, r, ln in dims]
    scratch += [pltpu.VMEM(two + (r, ln), BF) for _, r, ln in dims]
    for _, r, ln in dims:
        scratch += [pltpu.VMEM((2,) * (bits - 1 - q) + (r, ln), BF) for q in range(bits)]
    scratch += [pltpu.VMEM((r, ln), F32) for _, r, ln in dims]
    scratch += [pltpu.VMEM((2, 16, inner), F32)] + [pltpu.VMEM((2, bits + 1, 16, inner), BF)] * 2
    scratch += [
        pltpu.VMEM((2, N, inner), BF), pltpu.VMEM((2, n, N, LANES), BF), pltpu.VMEM((2, n, N, LANES), BF),
        pltpu.VMEM((2, N, inner), BF),
    ]
    nsub = sum(len(lane_parts(ln)) for _, _, ln in dims)
    dma = pltpu.SemaphoreType.DMA
    scratch += [
        dma((len(LOADS), 2)), dma(()), dma((inner // 512,)), dma((slots,)), dma((2,)), dma((2,)), dma((2,)),
        dma((nsub, bits + 1)), dma((nsub, bits + 1)), pltpu.SemaphoreType.REGULAR((nsub, bits + 1)),
        dma((2, nsub)), dma((2, nsub)), dma((2, bits + 1)), dma((2, bits + 1)),
        dma((2, n)), dma((2, n)), dma((2, n)), dma((2, n)),
    ]
    return pl.pallas_call(
        functools.partial(back_kernel, n, rank, {"lead": lead}),
        out_shape=outs,
        in_specs=specs,
        out_specs=[VSPEC] * len(outs),
        scratch_shapes=scratch,
        compiler_params=pltpu.CompilerParams(
            vmem_limit_bytes=63 * MIB, collective_id=cid, has_side_effects=True),
        name="backward",
    )(*args)


def shift(value, axis, by):
    size = lax.axis_size(axis)
    return lax.ppermute(value, axis, [(i, i + by) for i in range(size) if 0 <= i + by < size])


def starts_of(position, bounds_row):
    start = jnp.zeros(position.shape, jnp.int32)
    for cut in range(1, 7):
        start = jnp.where(position >= bounds_row[cut], bounds_row[cut], start)
    return start


def on_device(
    tokens, cotangent, bounds, norm_gain, in_proj, conv_kernel, conv_bias, x_proj, dt_proj, dt_bias, skip_gain, out_proj
):
    sec = lax.axis_index("section")
    n = lax.axis_size("ctx")
    me = lax.axis_index("ctx")
    t_len = tokens.shape[1]
    rank = dt_proj.shape[1]
    inner = in_proj.shape[2] // 2
    used = x_proj.shape[2]

    def swap(v):
        return lax.ppermute(v, "section", [(0, 1), (1, 0)])

    small = jnp.concatenate(
        [
            norm_gain[0].reshape(-1), conv_kernel[0].reshape(-1), conv_bias[0].reshape(-1), dt_bias[0].reshape(-1),
            skip_gain[0].reshape(-1), x_proj[0].reshape(-1), dt_proj[0].reshape(-1),
        ]
    )
    in_own, out_own = in_proj[0], out_proj[0]
    in_oth, small_oth, out_oth = swap(in_own), swap(small), swap(out_own)
    weights = []
    for layer in range(2):
        v = jnp.where(sec == layer, small, small_oth)
        at = 0

        def take(shape):
            nonlocal at
            size = math.prod(shape)
            piece = v[at : at + size].reshape(shape)
            at += size
            return piece

        w = {"gain": take((1, tokens.shape[2])).astype(F32)}
        w["ck"] = jnp.pad(take((4, inner)).astype(F32), ((0, 4), (0, 0)))
        w["cb"] = take((1, inner)).astype(F32)
        w["dtb"] = take((1, inner)).astype(F32)
        w["skip"] = take((1, inner)).astype(F32)
        w["xp"] = jnp.pad(take((inner, used)), ((0, 0), (0, LANES - used)))
        w["dtp"] = jnp.pad(take((rank, inner)), ((0, LANES - rank), (0, 0)))
        weights.append(w)
    tok = lax.dynamic_index_in_dim(tokens, sec, 0, keepdims=False)
    cot = lax.dynamic_index_in_dim(cotangent, sec, 0, keepdims=False)
    row = lax.dynamic_index_in_dim(bounds, sec, 0, keepdims=False)
    position = me * t_len + jnp.arange(t_len, dtype=jnp.int32)
    start = starts_of(position, row)
    marks = [(position - 3 + j >= start).astype(F32) for j in range(4)] + [(position != start).astype(F32)]
    mask = jnp.pad(jnp.stack(marks, axis=1), ((0, 0), (0, LANES - 5)))

    names_a = ("u", "xi", "z", "c", "proj", "beta", "ex", "us", "k2", "kb", "qb", "summ")
    names_b = ("s", "sb", "y", "o", "h")
    h = tok
    saved = []
    for layer in range(2):
        w = weights[layer]
        rim = shift(h[t_len - 16 :], "ctx", 1)
        fa = dict(zip(names_a, fwd_a(layer, rank, h, rim, w, mask, in_own, in_oth)))
        sin, dec = carry(n, False, 1 + layer, fa["summ"])
        fb = dict(zip(names_b, fwd_b(layer, rank, h, fa, sin, w, out_own, out_oth)))
        nxt = fb.pop("h")
        saved.append({**fa, **fb, "h": h, "dec": dec})
        h = nxt
    dh, g_in, g_out, g_sm, g_vec = backward(
        n, rank, 3, cot, mask, in_own, in_oth, out_own, out_oth, saved, weights)
    vec = lax.dynamic_index_in_dim(g_vec, sec, 0, keepdims=False)

    def share(rows, length):
        size = length // n
        return lax.dynamic_slice_in_dim(vec[rows, :length], me * size, size, axis=1)

    every = share(slice(0, 7), inner)
    tiles = inner // LANES
    prow = rank // n
    g_dt = g_sm[1, : prow * tiles].reshape(tiles, prow, LANES).transpose(1, 0, 2).reshape(prow, inner)
    return (
        h[None],
        dh[None],
        share(slice(7, 8), tokens.shape[2]),
        g_in[None],
        every[None, 0:4],
        every[4:5],
        g_sm[0][None, :, :used],
        g_dt[None],
        every[5:6],
        every[6:7],
        g_out[None],
    )


def solution(mesh):
    placed = (
        P(None, "ctx", None), P(None, "ctx", None), P(), P("section", None), P("section", None, None),
        P("section", None, None), P("section", None), P("section", None, None), P("section", None, None),
        P("section", None), P("section", None), P("section", None, None),
    )
    return jax.shard_map(
        on_device,
        mesh=mesh,
        in_specs=placed,
        out_specs=(
            P("section", "ctx", None), P("section", "ctx", None), P("section", "ctx"), P("section", "ctx", None),
            P("section", None, "ctx"), P("section", "ctx"), P("section", "ctx", None), P("section", "ctx", None),
            P("section", "ctx"), P("section", "ctx"), P("section", "ctx", None),
        ),
        check_vma=False,
    )
```

```python
import functools
import math

import jax
import jax.numpy as jnp
from jax import lax
from jax.experimental import pallas as pl
from jax.experimental.pallas import tpu as pltpu
from jax.sharding import PartitionSpec as P

NORM_EPS = 1e-05
LOG2E = math.log2(math.e)
BF = jnp.bfloat16
F32 = jnp.float32
MESH = pl.DeviceIdType.MESH
LANES = 128
BT = 16
N = 16
MIB = 2**20
VSPEC = pl.BlockSpec(memory_space=pltpu.VMEM)
ANYSPEC = pl.BlockSpec(memory_space=pl.ANY)


def dot(a, b):
    return jnp.dot(a, b, preferred_element_type=F32)


def dot_nt(a, b):
    return lax.dot_general(a, b, (((1,), (1,)), ((), ())), preferred_element_type=F32)


def dot_tn(a, b):
    return lax.dot_general(a, b, (((0,), (0,)), ((), ())), preferred_element_type=F32)


def iota(shape, dim):
    return lax.broadcasted_iota(jnp.int32, shape, dim)


def silu_parts(v):
    s = jax.nn.sigmoid(v)
    return v * s, s * (1.0 + v * (1.0 - s))


def coords(n):
    bits = n.bit_length() - 1
    me = lax.axis_index("ctx")
    return bits, me, [lax.rem(me // 2**b, 2) for b in range(bits)]


def unpack_index(k, dims):
    return tuple(lax.rem(k // 2 ** (dims - 1 - d), 2) for d in range(dims))


class Carry:
    def __init__(self, sec, me, n, src, recv, pre, dst, sems, decay, inner):
        self.sec, self.me, self.n = sec, me, n
        self.src, self.recv, self.pre, self.dst, self.decay = src, recv, pre, dst, decay
        self.send1, self.recv1, self.send2, self.recv2 = sems
        self.blocks = min(n, inner // LANES)
        self.stride = n // self.blocks
        self.mine = me // self.stride
        self.reverse = decay is not None

    def when(self, cond, fn):
        if self.stride == 1:
            fn()
        else:
            pl.when(cond)(fn)

    def to(self, k):
        return lax.rem(self.me + k, self.n)

    def frm(self, k):
        return lax.rem(self.me - k + self.n, self.n)

    def lane(self, dev):
        return pl.ds(pl.multiple_of((dev // self.stride) * LANES, LANES), LANES)

    def owns(self, dev):
        return lax.rem(dev, self.stride) == 0

    def first(self, k, dev, slot):
        return pltpu.make_async_remote_copy(
            src_ref=self.src.at[:, self.lane(dev)], dst_ref=self.recv.at[slot],
            send_sem=self.send1.at[k], recv_sem=self.recv1.at[slot],
            device_id=(self.sec, dev), device_id_type=MESH)

    def second(self, k, dev, frm):
        return pltpu.make_async_remote_copy(
            src_ref=self.pre.at[dev], dst_ref=self.dst.at[:, self.lane(frm)],
            send_sem=self.send2.at[k], recv_sem=self.recv2.at[frm],
            device_id=(self.sec, dev), device_id_type=MESH)

    def send(self):
        for k in range(1, self.n):
            self.when(self.owns(self.to(k)), lambda k=k: self.first(k, self.to(k), self.me).start())

    def combine(self):
        def own():
            self.recv[self.me] = self.src[:, self.lane(self.me)]
            for k in range(1, self.n):
                self.first(k, self.frm(k), self.frm(k)).wait_recv()
            run = jnp.zeros((N, LANES), F32)
            for i in range(self.n):
                d = self.n - 1 - i if self.reverse else i
                self.pre[d] = run.astype(BF)
                if self.reverse:
                    dec, st = self.decay[d], self.recv[d]
                else:
                    dec, st = self.recv[d, 0:N, :], self.recv[d, N : 2 * N, :]
                    self.decay_out[d] = dec
                run = dec.astype(F32) * run + st.astype(F32)
            for k in range(1, self.n):
                self.second(k, self.to(k), self.me).start()
            self.dst[:, self.lane(self.me)] = self.pre[self.me]

        self.when(self.owns(self.me), own)

    def get(self):
        for k in range(1, self.n):
            self.when(
                self.owns(self.frm(k)),
                lambda k=k: pltpu.make_async_remote_copy(
                    src_ref=self.pre.at[0], dst_ref=self.dst.at[:, self.lane(self.frm(k))],
                    send_sem=self.send2.at[k], recv_sem=self.recv2.at[self.frm(k)],
                    device_id=(self.sec, self.frm(k)), device_id_type=MESH).wait_recv())

    def sent(self):
        for k in range(1, self.n):
            self.when(self.owns(self.to(k)), lambda k=k: self.first(k, self.to(k), self.me).wait_send())

        def own():
            for k in range(1, self.n):
                self.second(k, self.to(k), self.me).wait_send()

        self.when(self.owns(self.me), own)


SAVED = ("xi", "z", "c", "beta", "ex", "us", "k2", "qb", "y", "proj", "dec", "sb")


def block_diag(projb, first_col):
    pick = (iota((LANES, BT * N), 0) == first_col + iota((LANES, BT * N), 1) % N).astype(F32).astype(BF)
    vals = dot(projb, pick)
    same = iota((BT, BT * N), 0) == iota((BT, BT * N), 1) // N
    return jnp.where(same, vals, 0.0)


def forward_kernel(n, rank, *refs):
    refs = list(refs)

    def take(k):
        out = refs[:k]
        del refs[:k]
        return out

    bounds_ref, tok_ref, gain_ref, ck_ref, cb_ref, dtb_ref, skip_ref, xproj_ref, dtproj_ref, in_own, out_own = take(11)
    in_oth, out_oth, mask_ref, xp2, dtp2, vec2, hmid_ref, hout_ref = take(8)
    hbm = [dict(zip(SAVED + ("s", "ut4", "ot4"), take(len(SAVED) + 3))) for _ in range(2)]
    loc = dict(zip(SAVED, take(len(SAVED))))
    kb_ref, w_in, w_out, stage, rim_ref, hrow, st, sbuf, o_all, ut_s, ot_s = take(11)
    c_src, c_recv, c_pre, c_dst = take(4)
    (sv_sem, wi_sem, wo_sem, sm_s, sm_r, xz_s, xz_r, oth_s, oth_r, rim_s, rim_r, s_sem, op_s, op_r, own_sem,
     c1, c2, c3, c4) = take(19)
    assert not refs
    sec = lax.axis_index("section")
    bits, me, mybit = coords(n)
    x = mybit[0]
    neigh = me + 1 - 2 * x
    t_len, width = hout_ref.shape
    inner = w_out.shape[0]
    used = xproj_ref.shape[1]
    cb = 512
    n_half = inner // cb
    rim = rim_ref.shape[2]
    barrier = pltpu.get_barrier_semaphore()
    for k in range(1, n):
        pl.semaphore_signal(barrier, inc=1, device_id=(sec, lax.rem(me + k, n)), device_id_type=MESH)
    pl.semaphore_signal(barrier, inc=1, device_id=(1 - sec, me), device_id_type=MESH)

    in_order = list(range(n_half, 2 * n_half)) + list(range(n_half))

    def in_copy(k, src):
        at = pl.ds(k * cb, cb)
        return pltpu.make_async_copy(src.at[:, at], w_in.at[:, at], wi_sem.at[k])

    def out_copy(src):
        return pltpu.make_async_copy(src, w_out, wo_sem)

    @pl.when(sec == 0)
    def _():
        for k in in_order:
            in_copy(k, in_own).start()
        out_copy(out_own).start()

    @pl.when(sec == 1)
    def _():
        for k in in_order:
            in_copy(k, in_own).start()

    vec2[sec, 0:4, :] = ck_ref[...].astype(F32)
    vec2[sec, 4:5, :] = cb_ref[...].astype(F32)
    vec2[sec, 5:6, :] = dtb_ref[...].astype(F32)
    vec2[sec, 6:7, :] = skip_ref[...].astype(F32)
    vec2[sec, 7:8, 0:width] = gain_ref[...].astype(F32)
    vec2[sec, 7:8, width:inner] = jnp.zeros((1, inner - width), F32)
    xp2[sec, :, :] = jnp.concatenate([xproj_ref[...], jnp.zeros((inner, LANES - used), BF)], axis=1)
    dtp2[sec, 0:rank, :] = dtproj_ref[...]
    dtp2[sec, rank:LANES, :] = jnp.zeros((LANES - rank, inner), BF)
    row = me * t_len + iota((t_len, LANES), 0)
    col = iota((t_len, LANES), 1)
    start = jnp.zeros((t_len, LANES), jnp.int32)
    for cut in range(1, 7):
        bound = bounds_ref[sec, cut]
        start = jnp.where(row >= bound, bound, start)
    tap = jnp.where(row - 3 + col >= start, 1.0, 0.0)
    keeps = jnp.where(row != start, 1.0, 0.0)
    mask_ref[...] = jnp.where(col < 4, tap, jnp.where(col == 4, keeps, 0.0))

    pl.semaphore_wait(barrier, n)

    def sibling(src, dst, a, b):
        return pltpu.make_async_remote_copy(
            src_ref=src, dst_ref=dst, send_sem=a, recv_sem=b, device_id=(1 - sec, me), device_id_type=MESH)

    small = [sibling(r.at[sec], r.at[sec], sm_s.at[i], sm_r.at[i]) for i, r in enumerate((vec2, xp2, dtp2))]
    for cp in small:
        cp.start()

    def rim_copy(layer, to):
        src = tok_ref.at[:, pl.ds(t_len - rim, rim), :] if layer == 0 else hrow.at[pl.ds(t_len - rim, rim), :]
        dst = rim_ref.at[0] if layer == 0 else rim_ref.at[1, 0]
        return pltpu.make_async_remote_copy(
            src_ref=src, dst_ref=dst, send_sem=rim_s.at[layer], recv_sem=rim_r.at[layer],
            device_id=(sec, to), device_id_type=MESH)

    def has_rim(layer, cond):
        return cond & (sec == 0) if layer == 0 else cond

    def send_rim(layer):
        @pl.when(has_rim(layer, me < n - 1))
        def _():
            rim_copy(layer, me + 1).start()

        @pl.when(me == 0)
        def _():
            if layer == 0:
                rim_ref[0] = jnp.zeros(rim_ref.shape[1:], BF)
            else:
                rim_ref[1, 0] = jnp.zeros(rim_ref.shape[2:], BF)

    def get_rim(layer):
        @pl.when(has_rim(layer, me > 0))
        def _():
            rim_copy(layer, me).wait_recv()

    send_rim(0)

    def xz_copy(k, rows):
        at = pl.ds((k % n_half) * cb, cb)
        dst = loc["z"] if k >= n_half else loc["xi"]
        return sibling(stage.at[k, pl.ds(0, rows), :], dst.at[:, at], xz_s.at[k], xz_r.at[k])

    def oth(k):
        if k == 0:
            return sibling(out_own, out_oth, oth_s.at[0], oth_r.at[0])
        return sibling(in_own, in_oth, oth_s.at[1], oth_r.at[1])

    def normed(h, layer):
        hf = h.astype(F32)
        inv = lax.rsqrt(jnp.mean(hf * hf, axis=-1, keepdims=True) + NORM_EPS)
        return (hf * inv * vec2[layer, 7:8, 0:width]).astype(BF)

    @pl.when(sec == 0)
    def _():
        both = normed(jnp.concatenate([tok_ref[0], tok_ref[1]], axis=0), 0)
        for k in in_order[:n_half]:
            in_copy(k, in_own).wait()
            r = dot(both, w_in[:, k * cb : (k + 1) * cb])
            loc["z"][:, pl.ds((k - n_half) * cb, cb)] = r[:t_len]
            stage[k, 0:t_len, :] = r[t_len:]
            xz_copy(k, t_len).start()
        get_rim(0)
        edge = normed(jnp.concatenate([rim_ref[0, 0], rim_ref[0, 1]], axis=0), 0)
        rows = jnp.concatenate([edge[:rim], both[:t_len], edge[rim:], both[t_len:]], axis=0)
        for k in in_order[n_half:]:
            in_copy(k, in_own).wait()
            r = dot(rows, w_in[:, k * cb : (k + 1) * cb])
            loc["xi"][:, pl.ds(k * cb, cb)] = r[: rim + t_len]
            stage[k] = r[rim + t_len :]
            xz_copy(k, rim + t_len).start()

    hrow[...] = tok_ref[sec]
    for cp in small:
        cp.wait_recv()

    @pl.when(sec == 1)
    def _():
        for k in in_order:
            xz_copy(k, t_len if k >= n_half else rim + t_len).wait_recv()

    oth(0).start()
    oth(1).start()

    carries = []
    saved = []

    def keep(name, layer):
        cp = pltpu.make_async_copy(loc[name], hbm[layer][name], sv_sem.at[layer, SAVED.index(name)])
        cp.start()
        saved.append((layer, name))

    def kept(name, layer):
        pltpu.make_async_copy(loc[name], hbm[layer][name], sv_sem.at[layer, SAVED.index(name)]).wait()

    def part_copy(kind, layer, k, where_from, where_to):
        src = (ut_s, ot_s)[kind].at[layer]
        dst = hbm[layer][("ut4", "ot4")[kind]]

        def slot(i):
            return pl.ds(pl.multiple_of(i * t_len, LANES), t_len)

        mine = 2 * sec + x
        if k == 0:
            s, i, to = src.at[:, x], mine, (1 - sec, me)
        elif k == 1:
            s, i, to = src.at[:, 1 - x], mine, (sec, neigh)
        else:
            i, to = 2 * sec + 1 - x, (1 - sec, me)
            s = dst.at[:, :, slot(i)]
        return pltpu.make_async_remote_copy(
            src_ref=s, dst_ref=dst.at[:, :, slot(i)], send_sem=op_s.at[layer, kind, k], recv_sem=op_r.at[layer, kind, i],
            device_id=to, device_id_type=MESH)

    def part_arrived(kind, layer, i):
        dst = hbm[layer][("ut4", "ot4")[kind]]
        at = pl.ds(pl.multiple_of(i * t_len, LANES), t_len)
        pltpu.make_async_remote_copy(
            src_ref=(ut_s, ot_s)[kind].at[layer, :, 0], dst_ref=dst.at[:, :, at], send_sem=op_s.at[layer, kind, 0],
            recv_sem=op_r.at[layer, kind, i], device_id=(1 - sec, me), device_id_type=MESH).wait_recv()

    def part_own(kind, layer):
        at = pl.ds(pl.multiple_of((2 * sec + x) * t_len, LANES), t_len)
        return pltpu.make_async_copy(
            (ut_s, ot_s)[kind].at[layer, :, x], hbm[layer][("ut4", "ot4")[kind]].at[:, :, at], own_sem.at[layer, kind])

    def part_send(kind, layer):
        part_copy(kind, layer, 0, None, None).start()
        part_copy(kind, layer, 1, None, None).start()
        part_own(kind, layer).start()

    def part_forward(kind, layer):
        part_arrived(kind, layer, 2 * sec + 1 - x)
        part_copy(kind, layer, 2, None, None).start()

    mask = mask_ref[...]
    cols = iota((t_len, LANES), 1)
    keepc = mask[:, 4:5]
    for layer in range(2):
        vec, xp, dtp = vec2.at[layer], xp2.at[layer], dtp2.at[layer]
        u = normed(hrow[...], layer)
        if layer == 1:
            for k in in_order[:n_half]:
                in_copy(k, in_own).wait()
                loc["z"][:, pl.ds((k - n_half) * cb, cb)] = dot(u, w_in[:, k * cb : (k + 1) * cb])
            get_rim(1)
            rows = jnp.concatenate([normed(rim_ref[1, 0], 1), u], axis=0)
            for k in in_order[n_half:]:
                in_copy(k, in_own).wait()
                loc["xi"][:, pl.ds(k * cb, cb)] = dot(rows, w_in[:, k * cb : (k + 1) * cb])
        keep("z", layer)
        keep("xi", layer)
        proj = jnp.zeros((t_len, LANES), F32)
        for k in range(n_half):
            at = pl.ds(k * cb, cb)
            xi = loc["xi"][:, at]
            c = vec[4:5, at] + vec[3:4, at] * xi[rim:]
            for j in range(3):
                c = c + vec[j : j + 1, at] * xi[rim - 3 + j : rim - 3 + j + t_len] * mask[:, j : j + 1]
            loc["c"][:, at] = c
            xc = c * jax.nn.sigmoid(c)
            loc["us"][:, at] = xc
            proj = proj + dot(xc.astype(BF), xp[at, :])
        keep("c", layer)
        projb = jnp.where(cols == rank + 2 * N, keepc, proj).astype(BF)
        loc["proj"][...] = projb
        keep("proj", layer)
        pf = projb.astype(F32)
        ksum = jnp.sum(jnp.where((cols >= rank) & (cols < rank + N), pf * pf, 0.0), axis=-1, keepdims=True)
        for k in range(n_half):
            at = pl.ds(k * cb, cb)
            beta = jax.nn.sigmoid(dot(projb, dtp[:, at]) + vec[5:6, at])
            eps = beta / (1.0 + beta * ksum)
            loc["beta"][:, at] = beta
            loc["us"][:, at] = loc["us"][:, at] * eps
            loc["ex"][:, at] = jnp.where(keepc > 0.0, eps, 1.0)
        for name in ("beta", "us", "ex"):
            keep(name, layer)
        nrow = t_len * N
        sel = (iota((nrow, t_len), 0) // N == iota((nrow, t_len), 1)).astype(F32).astype(BF)
        spread = dot(sel, projb).astype(BF)
        rn = iota((nrow, LANES), 0) % N
        cl = iota((nrow, LANES), 1)
        ones = jnp.ones((LANES, LANES), BF)
        zero = jnp.zeros((nrow, LANES), BF)
        kb = dot(jnp.where(cl == rank + rn, spread, zero), ones)
        kb_ref[...] = kb
        loc["qb"][...] = dot(jnp.where(cl == rank + N + rn, spread, zero), ones)
        keepb = dot(jnp.where(cl == rank + 2 * N, spread, zero), ones)
        loc["k2"][...] = jnp.where(keepb > 0.5, -LOG2E * kb * kb, -1e30)
        keep("qb", layer)
        keep("k2", layer)
        ec = 512
        nt = ec // LANES
        un = 8
        k2_ref, ex_ref, us_ref = loc["k2"], loc["ex"], loc["us"]

        def chunk(ci, carry, layer=layer):
            e0 = pl.multiple_of(ci * ec, ec)

            def body(i, sd):
                s, d = [list(v) for v in sd]
                g0 = pl.multiple_of(i * un, un)
                for t in range(un):
                    r = pl.multiple_of(g0 * N + t * N, N)
                    k2 = k2_ref[pl.ds(r, N), :]
                    kv = kb_ref[pl.ds(r, N), :]
                    for j in range(nt):
                        lane = pl.ds(e0 + LANES * j, LANES)
                        a = jnp.exp2(k2 * ex_ref.at[pl.ds(g0, un), lane][t : t + 1, :])
                        s[j] = a * s[j] + kv * us_ref.at[pl.ds(g0, un), lane][t : t + 1, :]
                        d[j] = a * d[j]
                return tuple(s), tuple(d)

            zeros = tuple(jnp.zeros((N, LANES), F32) for _ in range(nt))
            one = tuple(jnp.ones((N, LANES), F32) for _ in range(nt))
            s, d = lax.fori_loop(0, t_len // un, body, (zeros, one))
            for j in range(nt):
                lane = pl.ds(e0 + LANES * j, LANES)
                c_src[layer, 0:N, lane] = d[j].astype(BF)
                c_src[layer, N : 2 * N, lane] = s[j].astype(BF)
            return carry

        lax.fori_loop(0, inner // ec, chunk, 0)
        cr = Carry(sec, me, n, c_src.at[layer], c_recv.at[layer], c_pre.at[layer], c_dst.at[layer],
                   [s.at[layer] for s in (c1, c2, c3, c4)], None, inner)
        cr.decay_out = loc["dec"]
        carries.append(cr)
        if layer == 1:
            for name in ("dec", "sb", "y"):
                kept(name, 0)
        cr.send()
        ut_s[layer] = u.T.reshape(ut_s.shape[1:])
        cr.combine()
        keep("dec", layer)
        cr.get()
        st[...] = c_dst[layer].astype(F32)
        part_send(0, layer)

        def s_copy(blk, slot, layer=layer):
            return pltpu.make_async_copy(
                sbuf.at[slot], hbm[layer]["s"].at[pl.ds(pl.multiple_of(blk * BT * N, BT * N), BT * N), :], s_sem.at[slot])

        steps = t_len // BT

        def block(i, carry, s_copy=s_copy, vec=vec):
            slot = lax.rem(i, 2)
            rows = pl.ds(pl.multiple_of(i * BT, BT), BT)
            rbase = pl.multiple_of(i * BT * N, BT * N)

            @pl.when(i >= 2)
            def _():
                s_copy(i - 2, slot).wait()

            loc["sb"][rows, :] = st[...].astype(BF)
            qbd = block_diag(loc["proj"][rows, :], rank + N).astype(BF)
            s_ref = sbuf.at[slot]
            for ci in range(inner // ec):
                e0 = ci * ec
                s = [st[:, pl.ds(e0 + LANES * j, LANES)] for j in range(nt)]
                for t in range(BT):
                    krow = pl.ds(pl.multiple_of(rbase + t * N, N), N)
                    k2 = k2_ref[krow, :]
                    kv = kb_ref[krow, :]
                    for j in range(nt):
                        lane = pl.ds(e0 + LANES * j, LANES)
                        a = jnp.exp2(k2 * ex_ref.at[rows, lane][t : t + 1, :])
                        s[j] = a * s[j] + kv * us_ref.at[rows, lane][t : t + 1, :]
                        s_ref[t * N : (t + 1) * N, lane] = s[j].astype(BF)
                for j in range(nt):
                    st[:, pl.ds(e0 + LANES * j, LANES)] = s[j]
                at = pl.ds(e0, ec)
                c = loc["c"][rows, at]
                y = dot(qbd, s_ref[:, at]) + vec[6:7, at] * (c * jax.nn.sigmoid(c))
                loc["y"][rows, at] = y
                z = loc["z"][rows, at]
                o_all[rows, at] = (y * (z * jax.nn.sigmoid(z))).astype(BF)
            s_copy(i, slot).start()
            return carry

        lax.fori_loop(0, steps, block, 0)
        keep("sb", layer)
        keep("y", layer)
        part_forward(0, layer)
        if layer == 0:
            @pl.when(sec == 1)
            def _():
                oth(0).wait_recv()
                out_copy(out_oth).start()

            @pl.when(sec == 0)
            def _():
                oth(1).wait_recv()
                for k in in_order:
                    in_copy(k, in_oth).start()

        out_copy(out_own).wait()
        o = o_all[...]
        hn = (hrow[...].astype(F32) + dot(o, w_out[...])).astype(BF)
        if layer == 0:
            hrow[...] = hn
            hmid_ref[...] = hn
            send_rim(1)

            @pl.when(sec == 0)
            def _():
                oth(0).wait_recv()
                out_copy(out_oth).start()

            @pl.when(sec == 1)
            def _():
                oth(1).wait_recv()
                out_copy(out_own).start()
        else:
            hout_ref[...] = hn
        ot_s[layer] = o.T.reshape(ot_s.shape[1:])
        part_send(1, layer)
        for slot in range(2):
            s_copy(steps - 2 + slot, slot).wait()
        if layer == 0:
            for name in SAVED:
                if name not in ("dec", "sb", "y"):
                    kept(name, 0)

    for name in SAVED:
        kept(name, 1)
    for layer in range(2):
        part_forward(1, layer)
    for layer in range(2):
        for kind in range(2):
            part_own(kind, layer).wait()
            for i in range(2):
                part_arrived(kind, layer, 2 * (1 - sec) + (x if i == 0 else 1 - x))
            for k in range(3):
                part_copy(kind, layer, k, None, None).wait_send()
    for cp in small:
        cp.wait_send()
    for k in range(2):
        oth(k).wait_send()

    @pl.when(sec == 0)
    def _():
        for k in in_order:
            xz_copy(k, t_len if k >= n_half else rim + t_len).wait_send()

    for layer in range(2):
        @pl.when(has_rim(layer, me < n - 1))
        def _(layer=layer):
            rim_copy(layer, me + 1).wait_send()

    for cr in carries:
        cr.sent()


def forward(n, rank, cid, bounds, tokens, smalls, in_own, out_own):
    t_len, width = tokens.shape[1:]
    inner = out_own.shape[0]
    rim = 16
    rows = t_len * N

    def f32(*s):
        return jax.ShapeDtypeStruct(s, F32)

    def b16(*s):
        return jax.ShapeDtypeStruct(s, BF)

    shapes = {
        "xi": f32(t_len + rim, inner), "z": f32(t_len, inner), "c": f32(t_len, inner), "beta": f32(t_len, inner),
        "ex": f32(t_len, inner), "us": f32(t_len, inner), "k2": f32(rows, LANES), "qb": f32(rows, LANES),
        "y": f32(t_len, inner), "proj": b16(t_len, LANES), "dec": b16(n, N, LANES), "sb": b16(t_len, inner),
    }
    outs = [
        b16(width, 2 * inner), b16(inner, width), f32(t_len, LANES), b16(2, inner, LANES), b16(2, LANES, inner),
        f32(2, 8, inner), b16(t_len, width), b16(t_len, width),
    ]
    specs = [ANYSPEC, ANYSPEC] + [VSPEC] * 6
    for _ in range(2):
        outs += [shapes[name] for name in SAVED]
        outs += [b16(rows, inner), b16(n // 2, width // n, 4 * t_len), b16(n // 2, inner // n, 4 * t_len)]
        specs += [ANYSPEC] * (len(SAVED) + 3)
    scratch = [pltpu.VMEM(shapes[name].shape, shapes[name].dtype) for name in SAVED]
    scratch += [
        pltpu.VMEM((rows, LANES), F32), pltpu.VMEM((width, 2 * inner), BF), pltpu.VMEM((inner, width), BF),
        pltpu.VMEM((2 * inner // 512, rim + t_len, 512), F32), pltpu.VMEM((2, 2, rim, width), BF),
        pltpu.VMEM((t_len, width), BF), pltpu.VMEM((N, inner), F32), pltpu.VMEM((2, BT * N, inner), BF),
        pltpu.VMEM((t_len, inner), BF), pltpu.VMEM((2, n // 2, 2, width // n, t_len), BF),
        pltpu.VMEM((2, n // 2, 2, inner // n, t_len), BF),
        pltpu.VMEM((2, 2 * N, inner), BF), pltpu.VMEM((2, n, 2 * N, LANES), BF), pltpu.VMEM((2, n, N, LANES), BF),
        pltpu.VMEM((2, N, inner), BF),
    ]
    dma = pltpu.SemaphoreType.DMA
    n_in = 2 * inner // 512
    scratch += [
        dma((2, len(SAVED))), dma((n_in,)), dma(()), dma((3,)), dma((3,)), dma((n_in,)), dma((n_in,)), dma((2,)), dma((2,)),
        dma((2,)), dma((2,)), dma((2,)), dma((2, 2, 3)), dma((2, 2, 4)), dma((2, 2)),
        dma((2, n)), dma((2, n)), dma((2, n)), dma((2, n)),
    ]
    res = pl.pallas_call(
        functools.partial(forward_kernel, n, rank),
        out_shape=outs,
        in_specs=[pl.BlockSpec(memory_space=pltpu.SMEM)] + [VSPEC] * 8 + [ANYSPEC] * 2,
        out_specs=specs,
        scratch_shapes=scratch,
        compiler_params=pltpu.CompilerParams(vmem_limit_bytes=60 * MIB, collective_id=cid, has_side_effects=True),
        name="forward",
    )(bounds, tokens, *smalls, in_own, out_own)
    first, rest = res[:8], res[8:]
    per = len(SAVED) + 3
    saved = [dict(zip(SAVED + ("s", "ut4", "ot4"), rest[i * per : (i + 1) * per])) for i in range(2)]
    return first, saved


class Sub:
    def __init__(self, kit, num, layer, buf, recvs, out, lane0, lanes, steps, held):
        self.kit, self.num, self.layer = kit, num, layer
        self.at = pl.ds(lane0, lanes)
        self.buf, self.recvs, self.out = buf, recvs, out
        self.steps, self.held = steps, held
        self.last = len(steps) - 1
        self.stage = 0

    def bit(self, what):
        return self.kit.sec if what == "s" else self.kit.mybit[what]

    def partner(self, i):
        kit, what = self.kit, self.steps[i]
        if what == "s":
            return (1 - kit.sec, kit.me)
        return (kit.sec, kit.me + 2**what * (1 - 2 * kit.mybit[what]))

    def index(self, i, away):
        done = {w: self.bit(w) for w in self.steps[:i]}
        what = self.steps[i]
        done[what] = 1 - self.bit(what) if away else self.bit(what)
        return tuple(done.get(w, slice(None)) for w in self.held)

    def copy(self, i):
        free = len(self.held) - 1 - i
        return pltpu.make_async_remote_copy(
            src_ref=self.buf.at[self.index(i, True) + (slice(None), self.at)],
            dst_ref=self.recvs[i].at[(slice(None),) * (free + 1) + (self.at,)],
            send_sem=self.kit.ssem.at[self.layer, self.num, i], recv_sem=self.kit.rsem.at[self.layer, self.num, i],
            device_id=self.partner(i), device_id_type=MESH)

    def begin(self):
        self.copy(0).start()

    def place(self, half):
        return self.kit.place[self.out](half, self.at)

    def final(self):
        kit = self.kit
        return pltpu.make_async_remote_copy(
            src_ref=kit.res[self.out].at[:, self.at], dst_ref=self.place(1 - self.layer),
            send_sem=kit.fsem.at[self.layer, self.num], recv_sem=kit.frsem.at[self.layer, self.num],
            device_id=(1 - kit.sec, kit.me), device_id_type=MESH)

    def advance(self):
        i = self.stage
        if i > self.last:
            return
        kit = self.kit
        self.copy(i).wait_recv()
        free = len(self.held) - 1 - i
        fixed = self.index(i, False)
        res = kit.res[self.out]

        def body(k, carry):
            sub = list(unpack_index(k, free))
            src = tuple(sub) + (slice(None), self.at)
            dst = tuple(sub.pop(0) if isinstance(f, slice) else f for f in fixed) + (slice(None), self.at)
            if i == self.last:
                val = self.buf[dst].astype(F32) + self.recvs[i][src].astype(F32)

                @pl.when(kit.sec == self.layer)
                def _():
                    self.place(self.layer)[...] = val

                @pl.when(kit.sec != self.layer)
                def _():
                    res[:, self.at] = val
            else:
                self.buf[dst] = self.buf[dst] + self.recvs[i][src]
            return carry

        if free:
            lax.fori_loop(0, 2**free, body, 0)
        else:
            body(0, 0)
        self.stage = i + 1
        if i < self.last:
            self.copy(i + 1).start()
        else:
            @pl.when(kit.sec != self.layer)
            def _():
                self.final().start()

    def finish(self):
        assert self.stage > self.last
        for i in range(self.last + 1):
            self.copy(i).wait_send()

        @pl.when(self.kit.sec != self.layer)
        def _():
            self.final().wait_send()

        @pl.when(self.kit.sec == self.layer)
        def _():
            self.final().wait_recv()


class VecSum:
    def __init__(self, kit, layer, acc, send, recv):
        self.kit, self.layer, self.acc, self.send, self.recv = kit, layer, acc, send, recv
        self.stage = 0

    def copy(self, s):
        kit = self.kit
        if s == 0:
            to = (1 - kit.sec, kit.me)
        else:
            to = (kit.sec, kit.me + 2 ** (s - 1) * (1 - 2 * kit.mybit[s - 1]))
        return pltpu.make_async_remote_copy(
            src_ref=self.send.at[self.layer, s], dst_ref=self.recv.at[self.layer, s],
            send_sem=kit.vsem.at[self.layer, s], recv_sem=kit.vrsem.at[self.layer, s],
            device_id=to, device_id_type=MESH)

    def start(self, s):
        self.send[self.layer, s] = self.acc[self.layer].astype(BF)
        self.copy(s).start()

    def begin(self):
        self.start(0)

    def advance(self):
        s = self.stage
        if s > self.kit.bits:
            return
        self.copy(s).wait_recv()
        self.acc[self.layer] = self.send[self.layer, s].astype(F32) + self.recv[self.layer, s].astype(F32)
        self.stage = s + 1
        if s < self.kit.bits:
            self.start(s + 1)

    def drain(self):
        while self.stage <= self.kit.bits:
            self.advance()
        for s in range(self.kit.bits + 1):
            self.copy(s).wait_send()


class Kit:
    pass


class Gather:
    def __init__(self, kit, kind, layer, src, dst):
        self.kit, self.kind, self.layer = kit, kind, layer
        self.src, self.dst = src, dst

    def peers(self):
        kit = self.kit
        x = kit.mybit[0]
        other = kit.me + 1 - 2 * x
        return [(1 - kit.sec, kit.me, x), (kit.sec, other, 1 - x), (1 - kit.sec, other, 1 - x)]

    def copy(self, k, slot):
        kit = self.kit
        sec, dev, bit = self.peers()[k]
        return pltpu.make_async_remote_copy(
            src_ref=self.src(sec, bit), dst_ref=self.dst(slot),
            send_sem=kit.osem.at[self.layer, self.kind, k], recv_sem=kit.orsem.at[self.layer, self.kind, slot],
            device_id=(sec, dev), device_id_type=MESH)

    def slot(self, sec, bit):
        return 2 * sec + bit

    def send(self, order=(1, 2, 0)):
        mine = self.slot(self.kit.sec, self.kit.mybit[0])
        for k in order:
            self.copy(k, mine).start()

    def wait(self):
        for k in range(3):
            sec, dev, bit = self.peers()[k]
            self.copy(k, self.slot(sec, bit)).wait_recv()

    def sent(self):
        mine = self.slot(self.kit.sec, self.kit.mybit[0])
        for k in range(3):
            self.copy(k, mine).wait_send()


LOADS = ("h", "xi", "z", "c", "proj", "beta", "ex", "us", "k2", "qb", "sb", "y", "dec")
BOTH = ("h", "proj", "dec", "sb")
BIG = ("go", "gz", "gx")


def lane_parts(lanes):
    unit = lanes // LANES
    a = max(1, (3 * unit) // 4)
    return [(0, a * LANES), (a * LANES, lanes - a * LANES)]


def bit_orders(bits):
    low = list(range(1, bits))
    return [low, [2, 1] + low[2:]]


def back_kernel(n, rank, shapes, *refs):
    refs = list(refs)

    def take(k):
        out = refs[:k]
        del refs[:k]
        return out

    cots, mask_ref, in_own, in_oth, out_own, out_oth = take(6)
    hbm = [dict(zip(LOADS + ("s", "ut4", "ot4"), take(len(LOADS) + 3))) for _ in range(2)]
    vec2, xp2, dtp2 = take(3)
    dh_out, gin_out, gout_out, gsm_out, vec_out = take(5)
    loc = {name: (take(2) if name in BOTH else take(1) * 2) for name in LOADS}
    (g_both, w_out, w_in, sbuf, qs2, ws2, bst, deps, dkq, dy_ref, dz_both, dx_both, gdt_ref, gtmp, rims, rimr) = take(16)
    dxc = loc["y"][0]
    ut4, ot4, dr4, dz4, dx4 = take(5)
    kit = Kit()
    bits, me, mybit = coords(n)
    bufs = [dict(zip(BIG + ("sm",), take(4))) for _ in range(2)]
    recvs = []
    for _ in range(2):
        got = {name: take(bits - 1) for name in BIG}
        got["sm"] = take(bits + 1)
        recvs.append(got)
    kit.res = dict(zip(BIG + ("sm",), take(4)))
    vacc, vsend, vrecv = take(3)
    c_src, c_recv, c_pre, c_dst = take(4)
    (ld_sem, g_sem, wo_sem, wi_sem, s_sem, rim_sem, rimr_sem, own_sem, kit.osem, kit.orsem, kit.ssem, kit.rsem,
     kit.fsem, kit.frsem, kit.vsem, kit.vrsem, c1, c2, c3, c4) = take(20)
    assert not refs
    sec = lax.axis_index("section")
    kit.sec, kit.me, kit.bits, kit.mybit = sec, me, bits, mybit
    t_len, width = dh_out.shape
    inner = w_out.shape[0]
    cb = 512
    lead = shapes["lead"]

    barrier = pltpu.get_barrier_semaphore()
    for k in range(1, n):
        pl.semaphore_signal(barrier, inc=1, device_id=(sec, lax.rem(me + k, n)), device_id_type=MESH)
    for to in (me, me + 1 - 2 * mybit[0]):
        pl.semaphore_signal(barrier, inc=1, device_id=(1 - sec, to), device_id_type=MESH)

    pos = {name: i for i, name in enumerate(LOADS)}

    def load(name, layer):
        return pltpu.make_async_copy(hbm[layer][name], loc[name][layer], ld_sem.at[pos[name], layer])

    def out_chunk(k, src):
        at = pl.ds(k * cb, cb)
        return src.at[at, :], w_out.at[at, :], wo_sem.at[k]

    def in_chunk(k, slot, src):
        return src.at[:, pl.ds(k * cb, cb)], w_in.at[slot], wi_sem.at[slot]

    def fetch(layer, chunk, own, oth):
        a, b, s = chunk(own)
        a2 = chunk(oth)[0]

        @pl.when(sec == layer)
        def _():
            pltpu.make_async_copy(a, b, s).start()

        @pl.when(sec != layer)
        def _():
            pltpu.make_async_copy(a2, b, s).start()

    def arrive(chunk, own):
        a, b, s = chunk(own)
        pltpu.make_async_copy(a, b, s).wait()

    n_out = inner // cb
    n_in = 2 * inner // cb
    in_order = list(range(n_in // 2, n_in)) + list(range(n_in // 2))
    slots = w_in.shape[0]

    cot_hbm = cots.at[sec]
    pltpu.make_async_copy(cot_hbm, g_both.at[1], g_sem).start()
    for k in range(n_out):
        fetch(1, lambda src, k=k: out_chunk(k, src), out_own, out_oth)
    for name in ("z", "y", "c", "ex", "k2", "qb", "dec", "proj", "beta", "us", "sb", "xi", "h"):
        load(name, 1).start()
    for name in BOTH:
        load(name, 0).start()
    for i in range(slots):
        fetch(1, lambda src, i=i: in_chunk(in_order[i], i, src), in_own, in_oth)

    half_go = width // 2
    half_in = inner // 2
    kit.place = {
        "go": lambda hf, at: gout_out.at[:, pl.ds(hf * half_go + at.start, at.size)],
        "gz": lambda hf, at: gin_out.at[:, pl.ds(inner + hf * half_in + at.start, at.size)],
        "gx": lambda hf, at: gin_out.at[:, pl.ds(hf * half_in + at.start, at.size)],
        "sm": lambda hf, at: gsm_out.at[hf, :, at],
    }
    halves = [2] * (bits - 1)
    subs = []
    for layer in range(2):
        mine = {}
        num = 0
        for name, lanes in (("go", half_go), ("gz", half_in), ("gx", half_in)):
            mine[name] = []
            for (l0, ln), order in zip(lane_parts(lanes), bit_orders(bits)):
                mine[name].append(
                    Sub(kit, num, layer, bufs[layer][name], recvs[layer][name], name, l0, ln, order,
                        list(range(bits - 1, 0, -1))))
                num += 1
        mine["sm"] = [Sub(kit, num, layer, bufs[layer]["sm"], recvs[layer]["sm"], "sm", 0, LANES,
                          ["s", 2, 1, 0] + list(range(3, bits)), ["s"] + list(range(bits - 1, -1, -1)))]
        subs.append(mine)

    def begin(name, layer):
        for s in subs[layer][name]:
            s.begin()

    def advance(layer, *names):
        for name in names:
            for s in subs[layer][name]:
                s.advance()

    rows_go = inner // n
    rows_in = width // n
    rows_sm = inner // n
    x = mybit[0]

    def owner(j, count):
        return tuple((j >> (count - 1 - d)) & 1 for d in range(count))

    my_slot = 2 * sec + x

    def operands(layer):
        half = n // 2

        def lanes_of(ref, size):
            return lambda sc, b: ref.at[:, pl.ds(pl.multiple_of(sc * size, LANES), size)]

        def rows_of(ref):
            return lambda slot: ref.at[layer, slot]

        return {
            "dr": Gather(kit, 0, layer, lanes_of(g_both.at[layer], half_go), rows_of(dr4)),
            "dz": Gather(kit, 1, layer, lanes_of(dz_both.at[layer], half_in), rows_of(dz4)),
            "dx": Gather(kit, 2, layer, lanes_of(dx_both.at[layer], half_in), rows_of(dx4)),
        }

    ops = [operands(layer) for layer in range(2)]

    def part_load(layer, k):
        src, dst = (("ut4", ut4), ("ot4", ot4))[k]
        return pltpu.make_async_copy(hbm[layer][src], dst.at[layer], own_sem.at[layer, k])

    def own_half(ref, layer, size):
        return ref[layer, :, pl.ds(pl.multiple_of(sec * size, LANES), size)]

    pl.semaphore_wait(barrier, n + 1)
    vecs = [VecSum(kit, layer, vacc, vsend, vrecv) for layer in range(2)]
    pltpu.make_async_copy(cot_hbm, g_both.at[1], g_sem).wait()
    ops[1]["dr"].send()
    for layer in (1, 0):
        for k in range(2):
            part_load(layer, k).start()

    def grad_go(layer):
        ops[layer]["dr"].wait()
        part_load(layer, 1).wait()
        dr4[layer, my_slot] = own_half(g_both, layer, half_go)
        rhs = dr4[layer].reshape(4 * t_len, half_go)
        for j in range(n // 2):
            bufs[layer]["go"][owner(j, bits - 1)] = dot(ot4[layer, j], rhs).astype(BF)
        begin("go", layer)

    def grad_in(name, layer, key, both, four):
        ops[layer][key].wait()
        if name == "gz":
            part_load(layer, 0).wait()
        four[layer, my_slot] = own_half(both, layer, half_in)
        lhs = ut4[layer].reshape(n // 2 * rows_in, 4 * t_len)
        step = 512
        for l0 in range(0, half_in, step):
            at = pl.ds(l0, step)
            g = dot(lhs, four[layer, :, :, at].reshape(4 * t_len, step)).astype(BF)
            for j in range(n // 2):
                bufs[layer][name][owner(j, bits - 1) + (slice(None), at)] = g[j * rows_in : (j + 1) * rows_in]
        begin(name, layer)


    carries = []
    for layer in (1, 0):
        g_ref = g_both.at[layer]
        dz_ref = dz_both.at[layer]
        L = {name: loc[name][layer] for name in LOADS}
        vec, xp, dtp = vec2.at[layer], xp2.at[layer], dtp2.at[layer]
        vacc[layer] = jnp.zeros(vacc.shape[1:], F32)
        for name in ("z", "y", "c"):
            load(name, layer).wait()
        dr = g_ref[...]
        for k in range(n_out):
            at = pl.ds(k * cb, cb)
            arrive(lambda src, k=k: out_chunk(k, src), out_own)
            do = dot_nt(dr, w_out[at, :])
            act, der = silu_parts(L["z"][:, at])
            dy = do * act
            dy_ref[:, at] = dy
            dz_ref[:, at] = (do * L["y"][:, at] * der).astype(BF)
            c = L["c"][:, at]
            vacc[layer, 6:7, at] = jnp.sum(dy * (c * jax.nn.sigmoid(c)), axis=0, keepdims=True)
        if layer == 1:
            for k in range(n_out):
                fetch(0, lambda src, k=k: out_chunk(k, src), out_own, out_oth)
            load("z", 0).start()
        for name in ("ex", "k2", "qb"):
            load(name, layer).wait()
        k2_ref, qb_ref, ex_ref = L["k2"], L["qb"], L["ex"]
        ec = 512
        nt = ec // LANES
        un = 8

        def chunk(ci, carry, k2_ref=k2_ref, qb_ref=qb_ref, ex_ref=ex_ref, layer=layer):
            e0 = pl.multiple_of(ci * ec, ec)

            def body(i, b):
                b = list(b)
                g0 = pl.multiple_of((t_len // un - 1 - i) * un, un)
                for t in range(un - 1, -1, -1):
                    r = pl.multiple_of(g0 * N + t * N, N)
                    k2 = k2_ref[pl.ds(r, N), :]
                    qv = qb_ref[pl.ds(r, N), :]
                    for j in range(nt):
                        lane = pl.ds(e0 + LANES * j, LANES)
                        a = jnp.exp2(k2 * ex_ref.at[pl.ds(g0, un), lane][t : t + 1, :])
                        b[j] = a * (qv * dy_ref.at[pl.ds(g0, un), lane][t : t + 1, :] + b[j])
                return tuple(b)

            b = lax.fori_loop(0, t_len // un, body, tuple(jnp.zeros((N, LANES), F32) for _ in range(nt)))
            for j in range(nt):
                c_src[layer, :, pl.ds(e0 + LANES * j, LANES)] = b[j].astype(BF)
            return carry

        lax.fori_loop(0, inner // ec, chunk, 0)
        load("dec", layer).wait()
        cr = Carry(sec, me, n, c_src.at[layer], c_recv.at[layer], c_pre.at[layer], c_dst.at[layer],
                   [s.at[layer] for s in (c1, c2, c3, c4)], L["dec"], inner)
        carries.append(cr)
        cr.send()
        if layer == 0:
            advance(1, "sm")
            vecs[1].advance()
        cr.combine()
        steps = t_len // BT

        def s_copy(blk, slot, layer=layer):
            return pltpu.make_async_copy(
                hbm[layer]["s"].at[pl.ds(pl.multiple_of(blk * BT * N, BT * N), BT * N), :], sbuf.at[slot],
                s_sem.at[slot])

        s_copy(steps - 1, 0).start()
        for name in ("proj", "beta", "us", "sb"):
            load(name, layer).wait()
        cr.get()
        bst[...] = c_dst[layer].astype(F32)
        ops[layer]["dz"].send()
        if layer == 0:
            grad_in("gx", 1, "dx", dx_both, dx4)

        def block(i, carry, L=L, vec=vec, s_copy=s_copy, dy_ref=dy_ref):
            blk = steps - 1 - i
            slot = lax.rem(i, 2)
            base = pl.multiple_of(blk * BT, BT)
            rows = pl.ds(base, BT)
            rbase = pl.multiple_of(blk * BT * N, BT * N)

            @pl.when(i + 1 < steps)
            def _():
                s_copy(blk - 1, 1 - slot).start()

            s_copy(blk, slot).wait()
            projb = L["proj"][rows, :]
            pf = projb.astype(F32)
            cols = iota((BT, LANES), 1)
            is_k = (cols >= rank) & (cols < rank + N)
            ksum = jnp.sum(jnp.where(is_k, pf * pf, 0.0), axis=-1, keepdims=True)
            kbd = block_diag(projb, rank)
            k2bd = (kbd * kbd).astype(BF)
            kbd = kbd.astype(BF)
            r1 = jnp.zeros((BT, BT * N), F32)
            r2 = jnp.zeros((BT, BT * N), F32)
            r3 = jnp.zeros((BT, BT * N), F32)
            s_blk = sbuf.at[slot]
            for ci in range(inner // ec):
                e0 = ci * ec
                qs, ws = qs2.at[ci % 2], ws2.at[ci % 2]
                b = [bst[:, pl.ds(e0 + LANES * j, LANES)] for j in range(nt)]
                for t in range(BT - 1, -1, -1):
                    row = slice(t * N, (t + 1) * N)
                    krow = pl.ds(pl.multiple_of(rbase + t * N, N), N)
                    k2 = L["k2"][krow, :]
                    qv = L["qb"][krow, :]
                    for j in range(nt):
                        lane = pl.ds(e0 + LANES * j, LANES)
                        a = jnp.exp2(k2 * L["ex"].at[rows, lane][t : t + 1, :])
                        q = qv * dy_ref.at[rows, lane][t : t + 1, :] + b[j]
                        b[j] = a * q
                        prev = s_blk[(t - 1) * N : t * N, lane] if t > 0 else L["sb"][rows, lane]
                        qs[row, LANES * j : LANES * (j + 1)] = q.astype(BF)
                        ws[row, LANES * j : LANES * (j + 1)] = (b[j] * prev.astype(F32)).astype(BF)
                for j in range(nt):
                    bst[:, pl.ds(e0 + LANES * j, LANES)] = b[j]
                at = pl.ds(e0, ec)
                p1 = dot(kbd, qs[...])
                p2 = dot(k2bd, ws[...])
                c = L["c"][rows, at]
                beta = L["beta"][rows, at]
                eps = beta / (1.0 + beta * ksum)
                dy = dy_ref[rows, at]
                deps[rows, at] = (c * jax.nn.sigmoid(c)) * p1 - p2
                dxc[rows, at] = dy * vec[6:7, at] + eps * p1
                r1 = r1 + dot_nt(L["us"][rows, at].astype(BF), qs[...])
                r2 = r2 + dot_nt(eps.astype(BF), ws[...])
                r3 = r3 + dot_nt(dy.astype(BF), s_blk[:, at])
            same = iota((BT, BT * N), 0) == iota((BT, BT * N), 1) // N
            gather_k = (iota((BT * N, LANES), 1) == rank + iota((BT * N, LANES), 0) % N).astype(F32)
            gather_q = (iota((BT * N, LANES), 1) == rank + N + iota((BT * N, LANES), 0) % N).astype(F32)

            def pick(r, g):
                return jnp.dot(
                    jnp.where(same, r, 0.0), g, precision=lax.Precision.HIGHEST, preferred_element_type=F32)

            dkq[rows, :] = pick(r1, gather_k) - 2.0 * pf * pick(r2, gather_k) + pick(r3, gather_q)
            return carry

        def tick(k, layer=layer):
            if layer == 0:
                advance(1, "sm")
                vecs[1].advance()
            if k == 1:
                if layer == 0:
                    advance(1, "gx")
                grad_go(layer)
                grad_in("gz", layer, "dz", dz_both, dz4)
            if k == 3:
                if layer == 0:
                    advance(1, "gx")
                advance(layer, "go", "gz")

        def block_and_tick(i, carry):
            block(i, carry)
            for k in range(4):
                @pl.when(i == (k + 1) * steps // 4 - 1)
                def _(k=k):
                    tick(k)

            return carry

        lax.fori_loop(0, steps, block_and_tick, 0)
        if layer == 1:
            for name in ("k2", "qb", "ex", "us"):
                load(name, 0).start()
        load("xi", layer).wait()
        projw = L["proj"][...]
        pw = projw.astype(F32)
        colw = iota((t_len, LANES), 1)
        kall = jnp.where((colw >= rank) & (colw < rank + N), pw, 0.0)
        ks = jnp.sum(kall * kall, axis=-1, keepdims=True)
        tc = 256
        def first(k, carry, L=L, dtp=dtp, layer=layer, projw=projw, ks=ks):
            dkc, ddt = carry
            at = pl.ds(pl.multiple_of(k * tc, tc), tc)
            beta = L["beta"][:, at]
            inv = 1.0 / (1.0 + beta * ks)
            dq = deps[:, at] * (inv * inv)
            dkc = dkc + jnp.sum(dq * beta * beta, axis=-1, keepdims=True)
            dp = (dq * beta * (1.0 - beta)).astype(BF)
            vacc[layer, 5:6, at] = jnp.sum(dp.astype(F32), axis=0, keepdims=True)
            gdt_ref[:, at] = dot_tn(projw, dp)[:rank]
            ddt = ddt + dot_nt(dp, dtp[:, at])
            return dkc, ddt

        dkc, ddt = lax.fori_loop(
            0, inner // tc, first, (jnp.zeros((t_len, 1), F32), jnp.zeros((t_len, LANES), F32)))
        dproj = (jnp.where(colw < rank, ddt, dkq[...]) - 2.0 * kall * dkc).astype(BF)
        mask = mask_ref[...]

        def second(k, carry, L=L, xp=xp, layer=layer, dproj=dproj, ck_ref=vec):
            at = pl.ds(pl.multiple_of(k * tc, tc), tc)
            c = L["c"][:, at]
            act, der = silu_parts(c)
            gxp = dot_tn(act.astype(BF), dproj).astype(BF)
            for i in range(tc // rows_sm):
                j = k * (tc // rows_sm) + i
                bufs[layer]["sm"][(0,) + unpack_index(j, bits)] = gxp[i * rows_sm : (i + 1) * rows_sm]
            dc = (dxc[:, at] + dot_nt(dproj, xp[at, :])) * der
            vacc[layer, 4:5, at] = jnp.sum(dc, axis=0, keepdims=True)
            xi = L["xi"][:, at]
            pad = jnp.zeros((8, tc), F32)
            dxi = ck_ref[3:4, at] * dc
            rim = jnp.zeros((8, tc), F32)
            vacc[layer, 3:4, at] = jnp.sum(dc * xi[lead:], axis=0, keepdims=True)
            for j in range(3):
                m = dc * mask[:, j : j + 1]
                vacc[layer, j : j + 1, at] = jnp.sum(m * xi[lead - 3 + j : lead - 3 + j + t_len], axis=0, keepdims=True)
                m = m * ck_ref[j : j + 1, at]
                ext = jnp.concatenate([pad, m, pad], axis=0)
                dxi = dxi + ext[8 + 3 - j : 8 + 3 - j + t_len]
                rim = rim + ext[8 - j : 16 - j]
            deps[:, at] = dxi
            rims[layer, :, at] = jnp.where(iota((8, tc), 0) < 3, rim, 0.0)
            return carry

        lax.fori_loop(0, inner // tc, second, 0)

        def rim_copy(to, layer=layer):
            return pltpu.make_async_remote_copy(
                src_ref=rims.at[layer], dst_ref=rimr.at[layer], send_sem=rim_sem.at[layer], recv_sem=rimr_sem.at[layer],
                device_id=(sec, to), device_id_type=MESH)

        @pl.when(me > 0)
        def _():
            rim_copy(me - 1).start()

        @pl.when(me == n - 1)
        def _():
            rimr[layer] = jnp.zeros(rimr.shape[1:], F32)

        if layer == 1:
            for name in ("c", "beta", "xi", "y"):
                load(name, 0).start()
        prow = rank // n
        for j in range(n):
            for t in range(inner // LANES):
                gtmp[j, t * prow : (t + 1) * prow, :] = gdt_ref[j * prow : (j + 1) * prow, t * LANES : (t + 1) * LANES]
        drow = prow * (inner // LANES)
        for j in range(n):
            bufs[layer]["sm"][(1,) + owner(j, bits) + (slice(0, drow),)] = gtmp[j, 0:drow].astype(BF)
        begin("sm", layer)
        advance(layer, "go", "gz")
        if layer == 0:
            advance(1, "gx")
        du = jnp.zeros((t_len, width), F32)

        def project(du, i, g, layer=layer):
            slot = i % slots
            arrive(lambda src: in_chunk(in_order[i], slot, src), in_own)
            du = du + dot_nt(g, w_in[slot])
            if i + slots < n_in:
                fetch(layer, lambda src: in_chunk(in_order[i + slots], slot, src), in_own, in_oth)
            elif layer == 1:
                fetch(0, lambda src: in_chunk(in_order[i + slots - n_in], slot, src), in_own, in_oth)
            return du

        for i in range(n_in // 2):
            du = project(du, i, dz_ref[:, pl.ds(i * cb, cb)])

        @pl.when(me < n - 1)
        def _():
            rim_copy(me).wait_recv()

        tail = jnp.concatenate([jnp.zeros((5, inner), F32), rimr[layer][0:3]], axis=0)
        deps[pl.ds(t_len - 8, 8), :] = deps[pl.ds(t_len - 8, 8), :] + tail
        dx_both[layer] = deps[...].astype(BF)
        ops[layer]["dx"].send()
        advance(layer, "go", "gz", "sm")
        for i in range(n_in // 2, n_in):
            du = project(du, i, dx_both[layer, :, pl.ds((i - n_in // 2) * cb, cb)])
        load("h", layer).wait()
        hf = L["h"][...].astype(F32)
        inv = lax.rsqrt(jnp.mean(hf * hf, axis=-1, keepdims=True) + NORM_EPS)
        unit = hf * inv
        vacc[layer, 7:8, pl.ds(0, width)] = jnp.sum(du * unit, axis=0, keepdims=True)
        dn = du * vec[7:8, 0:width]
        dh = g_ref[...].astype(F32) + inv * (dn - unit * jnp.mean(dn * unit, axis=-1, keepdims=True))
        if layer == 1:
            g_both[0] = dh.astype(BF)
            ops[0]["dr"].send()
        else:
            dh_out[...] = dh.astype(BF)
        vecs[layer].begin()
        if layer == 0:
            advance(0, "sm")

    grad_in("gx", 0, "dx", dx_both, dx4)
    left = [s for layer in range(2) for v in subs[layer].values() for s in v]
    while any(s.stage <= s.last for s in left) or vecs[0].stage <= bits or vecs[1].stage <= bits:
        for v in vecs[::-1]:
            v.advance()
        for s in left[::-1]:
            s.advance()
    for v in vecs:
        v.drain()
    for layer in range(2):
        vec_out[layer] = vacc[layer]
    for s in left:
        s.finish()
    for layer in range(2):
        for g in ops[layer].values():
            g.sent()

    @pl.when(me > 0)
    def _():
        for layer in range(2):
            pltpu.make_async_remote_copy(
                src_ref=rims.at[layer], dst_ref=rimr.at[layer], send_sem=rim_sem.at[layer], recv_sem=rimr_sem.at[layer],
                device_id=(sec, me - 1), device_id_type=MESH).wait_send()

    for cr in carries:
        cr.sent()


def backward(n, rank, cid, cot, mask, in_own, in_oth, out_own, out_oth, saved, vec2, xp2, dtp2):
    t_len, width = cot.shape[1:]
    inner = out_own.shape[0]
    bits = n.bit_length() - 1
    lead = saved[0]["xi"].shape[0] - t_len
    args = [cot, mask, in_own, in_oth, out_own, out_oth]
    specs = [ANYSPEC, VSPEC] + [ANYSPEC] * 4
    for layer in range(2):
        args += [saved[layer][name] for name in LOADS + ("s", "ut4", "ot4")]
        specs += [ANYSPEC] * (len(LOADS) + 3)
    args += [vec2, xp2, dtp2]
    specs += [VSPEC] * 3
    rows_go, rows_in, rows_sm = inner // n, width // n, inner // n

    def sd(t, *s):
        return jax.ShapeDtypeStruct(s, t)

    outs = [
        sd(BF, t_len, width), sd(F32, rows_in, 2 * inner), sd(F32, rows_go, width), sd(F32, 2, rows_sm, LANES),
        sd(F32, 2, 16, inner),
    ]
    scratch = []
    for name in LOADS:
        a = saved[0][name]
        scratch += [pltpu.VMEM(a.shape, a.dtype)] * (2 if name in BOTH else 1)
    slots = 4
    scratch += [
        pltpu.VMEM((2, t_len, width), BF), pltpu.VMEM((inner, width), BF), pltpu.VMEM((slots, width, 512), BF),
        pltpu.VMEM((2, BT * N, inner), BF), pltpu.VMEM((2, BT * N, 512), BF), pltpu.VMEM((2, BT * N, 512), BF),
        pltpu.VMEM((N, inner), F32), pltpu.VMEM((t_len, inner), F32),
        pltpu.VMEM((t_len, LANES), F32), pltpu.VMEM((t_len, inner), F32), pltpu.VMEM((2, t_len, inner), BF),
        pltpu.VMEM((2, t_len, inner), BF),
        pltpu.VMEM((rank, inner), F32), pltpu.VMEM((n, max(8, rank * inner // (LANES * n)), LANES), F32),
        pltpu.VMEM((2, 8, inner), F32), pltpu.VMEM((2, 8, inner), F32),
    ]
    scratch += [
        pltpu.VMEM((2, n // 2, rows_in, 4 * t_len), BF), pltpu.VMEM((2, n // 2, rows_go, 4 * t_len), BF),
        pltpu.VMEM((2, 4, t_len, width // 2), BF), pltpu.VMEM((2, 4, t_len, inner // 2), BF),
        pltpu.VMEM((2, 4, t_len, inner // 2), BF),
    ]
    dims = (("go", rows_go, width // 2), ("gz", rows_in, inner // 2), ("gx", rows_in, inner // 2), ("sm", rows_sm, LANES))
    for _ in range(2):
        for name, r, ln in dims:
            count = bits + 1 if name == "sm" else bits - 1
            scratch.append(pltpu.VMEM((2,) * count + (r, ln), BF))
    for _ in range(2):
        for name, r, ln in dims:
            count = bits + 1 if name == "sm" else bits - 1
            scratch += [pltpu.VMEM((2,) * (count - 1 - q) + (r, ln), BF) for q in range(count)]
    scratch += [pltpu.VMEM((r, ln), F32) for _, r, ln in dims]
    scratch += [pltpu.VMEM((2, 16, inner), F32)] + [pltpu.VMEM((2, bits + 1, 16, inner), BF)] * 2
    scratch += [
        pltpu.VMEM((2, N, inner), BF), pltpu.VMEM((2, n, N, LANES), BF), pltpu.VMEM((2, n, N, LANES), BF),
        pltpu.VMEM((2, N, inner), BF),
    ]
    nsub = 1 + sum(len(lane_parts(ln)) for _, _, ln in dims[:3])
    dma = pltpu.SemaphoreType.DMA
    scratch += [
        dma((len(LOADS), 2)), dma(()), dma((inner // 512,)), dma((slots,)), dma((2,)), dma((2,)), dma((2,)), dma((2, 2)),
        dma((2, 3, 3)), dma((2, 3, 4)), dma((2, nsub, bits + 1)), dma((2, nsub, bits + 1)),
        dma((2, nsub)), dma((2, nsub)), dma((2, bits + 1)), dma((2, bits + 1)),
        dma((2, n)), dma((2, n)), dma((2, n)), dma((2, n)),
    ]
    return pl.pallas_call(
        functools.partial(back_kernel, n, rank, {"lead": lead}),
        out_shape=outs,
        in_specs=specs,
        out_specs=[VSPEC] * len(outs),
        scratch_shapes=scratch,
        compiler_params=pltpu.CompilerParams(
            vmem_limit_bytes=63 * MIB, collective_id=cid, has_side_effects=True),
        name="backward",
    )(*args)


def on_device(
    tokens, cotangent, bounds, norm_gain, in_proj, conv_kernel, conv_bias, x_proj, dt_proj, dt_bias, skip_gain, out_proj
):
    sec = lax.axis_index("section")
    n = lax.axis_size("ctx")
    me = lax.axis_index("ctx")
    rank = dt_proj.shape[1]
    inner = out_proj.shape[1]
    used = x_proj.shape[2]
    in_own, out_own = in_proj[0], out_proj[0]
    smalls = (norm_gain, conv_kernel[0], conv_bias, dt_bias, skip_gain, x_proj[0], dt_proj[0])
    first, saved = forward(n, rank, 1, bounds, tokens, smalls, in_own, out_own)
    in_oth, out_oth, mask, xp2, dtp2, vec2, hmid, hout = first
    saved[0]["h"] = lax.dynamic_index_in_dim(tokens, sec, 0, keepdims=False)
    saved[1]["h"] = hmid
    dh, g_in, g_out, g_sm, g_vec = backward(
        n, rank, 2, cotangent, mask, in_own, in_oth, out_own, out_oth, saved, vec2, xp2, dtp2)
    vec = lax.dynamic_index_in_dim(g_vec, sec, 0, keepdims=False)

    def share(rows, length):
        size = length // n
        return lax.dynamic_slice_in_dim(vec[rows, :length], me * size, size, axis=1)

    every = share(slice(0, 7), inner)
    tiles = inner // LANES
    prow = rank // n
    g_dt = g_sm[1, : prow * tiles].reshape(tiles, prow, LANES).transpose(1, 0, 2).reshape(prow, inner)
    return (
        hout[None],
        dh[None],
        share(slice(7, 8), tokens.shape[2]),
        g_in[None],
        every[None, 0:4],
        every[4:5],
        g_sm[0][None, :, :used],
        g_dt[None],
        every[5:6],
        every[6:7],
        g_out[None],
    )


def solution(mesh):
    placed = (
        P(None, "ctx", None), P(None, "ctx", None), P(), P("section", None), P("section", None, None),
        P("section", None, None), P("section", None), P("section", None, None), P("section", None, None),
        P("section", None), P("section", None), P("section", None, None),
    )
    return jax.shard_map(
        on_device,
        mesh=mesh,
        in_specs=placed,
        out_specs=(
            P("section", "ctx", None), P("section", "ctx", None), P("section", "ctx"), P("section", "ctx", None),
            P("section", None, "ctx"), P("section", "ctx"), P("section", "ctx", None), P("section", "ctx", None),
            P("section", "ctx"), P("section", "ctx"), P("section", "ctx", None),
        ),
        check_vma=False,
    )
```

```python
import functools
import math

import jax
import jax.numpy as jnp
from jax import lax
from jax.experimental import pallas as pl
from jax.experimental.pallas import tpu as pltpu
from jax.sharding import PartitionSpec as P

NORM_EPS = 1e-05
LOG2E = math.log2(math.e)
BF = jnp.bfloat16
F32 = jnp.float32
MESH = pl.DeviceIdType.MESH
LANES = 128
BT = 16
N = 16
MIB = 2**20
VSPEC = pl.BlockSpec(memory_space=pltpu.VMEM)
ANYSPEC = pl.BlockSpec(memory_space=pl.ANY)


def dot(a, b):
    return jnp.dot(a, b, preferred_element_type=F32)


def dot_nt(a, b):
    return lax.dot_general(a, b, (((1,), (1,)), ((), ())), preferred_element_type=F32)


def dot_tn(a, b):
    return lax.dot_general(a, b, (((0,), (0,)), ((), ())), preferred_element_type=F32)


def iota(shape, dim):
    return lax.broadcasted_iota(jnp.int32, shape, dim)


def silu_parts(v):
    s = jax.nn.sigmoid(v)
    return v * s, s * (1.0 + v * (1.0 - s))


def coords(n):
    bits = n.bit_length() - 1
    me = lax.axis_index("ctx")
    return bits, me, [lax.rem(me // 2**b, 2) for b in range(bits)]


def unpack_index(k, dims):
    return tuple(lax.rem(k // 2 ** (dims - 1 - d), 2) for d in range(dims))


class Carry:
    def __init__(self, sec, me, n, src, recv, pre, dst, sems, decay, inner):
        self.sec, self.me, self.n = sec, me, n
        self.src, self.recv, self.pre, self.dst, self.decay = src, recv, pre, dst, decay
        self.send1, self.recv1, self.send2, self.recv2 = sems
        self.blocks = min(n, inner // LANES)
        self.stride = n // self.blocks
        self.mine = me // self.stride
        self.reverse = decay is not None

    def when(self, cond, fn):
        if self.stride == 1:
            fn()
        else:
            pl.when(cond)(fn)

    def to(self, k):
        return lax.rem(self.me + k, self.n)

    def frm(self, k):
        return lax.rem(self.me - k + self.n, self.n)

    def lane(self, dev):
        return pl.ds(pl.multiple_of((dev // self.stride) * LANES, LANES), LANES)

    def owns(self, dev):
        return lax.rem(dev, self.stride) == 0

    def first(self, k, dev, slot):
        return pltpu.make_async_remote_copy(
            src_ref=self.src.at[:, self.lane(dev)], dst_ref=self.recv.at[slot],
            send_sem=self.send1.at[k], recv_sem=self.recv1.at[slot],
            device_id=(self.sec, dev), device_id_type=MESH)

    def second(self, k, dev, frm):
        return pltpu.make_async_remote_copy(
            src_ref=self.pre.at[dev], dst_ref=self.dst.at[:, self.lane(frm)],
            send_sem=self.send2.at[k], recv_sem=self.recv2.at[frm],
            device_id=(self.sec, dev), device_id_type=MESH)

    def send(self):
        for k in range(1, self.n):
            self.when(self.owns(self.to(k)), lambda k=k: self.first(k, self.to(k), self.me).start())

    def combine(self):
        def own():
            self.recv[self.me] = self.src[:, self.lane(self.me)]
            for k in range(1, self.n):
                self.first(k, self.frm(k), self.frm(k)).wait_recv()
            run = jnp.zeros((N, LANES), F32)
            for i in range(self.n):
                d = self.n - 1 - i if self.reverse else i
                self.pre[d] = run.astype(BF)
                if self.reverse:
                    dec, st = self.decay[d], self.recv[d]
                else:
                    dec, st = self.recv[d, 0:N, :], self.recv[d, N : 2 * N, :]
                    self.decay_out[d] = dec
                run = dec.astype(F32) * run + st.astype(F32)
            for k in range(1, self.n):
                self.second(k, self.to(k), self.me).start()
            self.dst[:, self.lane(self.me)] = self.pre[self.me]

        self.when(self.owns(self.me), own)

    def get(self):
        for k in range(1, self.n):
            self.when(
                self.owns(self.frm(k)),
                lambda k=k: pltpu.make_async_remote_copy(
                    src_ref=self.pre.at[0], dst_ref=self.dst.at[:, self.lane(self.frm(k))],
                    send_sem=self.send2.at[k], recv_sem=self.recv2.at[self.frm(k)],
                    device_id=(self.sec, self.frm(k)), device_id_type=MESH).wait_recv())

    def sent(self):
        for k in range(1, self.n):
            self.when(self.owns(self.to(k)), lambda k=k: self.first(k, self.to(k), self.me).wait_send())

        def own():
            for k in range(1, self.n):
                self.second(k, self.to(k), self.me).wait_send()

        self.when(self.owns(self.me), own)


SAVED = ("xi", "z", "c", "beta", "ex", "us", "k2", "qb", "y", "proj", "dec", "sb")


def block_diag(projb, first_col):
    pick = (iota((LANES, BT * N), 0) == first_col + iota((LANES, BT * N), 1) % N).astype(F32).astype(BF)
    vals = dot(projb, pick)
    same = iota((BT, BT * N), 0) == iota((BT, BT * N), 1) // N
    return jnp.where(same, vals, 0.0)


def forward_kernel(n, rank, *refs):
    refs = list(refs)

    def take(k):
        out = refs[:k]
        del refs[:k]
        return out

    bounds_ref, tok_ref, gain_ref, ck_ref, cb_ref, dtb_ref, skip_ref, xproj_ref, dtproj_ref, in_own, out_own = take(11)
    in_oth, out_oth, mask_ref, xp2, dtp2, vec2, hmid_ref, hout_ref = take(8)
    hbm = [dict(zip(SAVED + ("s", "ut4", "ot4"), take(len(SAVED) + 3))) for _ in range(2)]
    loc = dict(zip(SAVED, take(len(SAVED))))
    kb_ref, w_in, w_out, stage, rim_ref, hrow, st, sbuf, o_all, ut_s, ot_s = take(11)
    c_src, c_recv, c_pre, c_dst = take(4)
    (sv_sem, wi_sem, wo_sem, sm_s, sm_r, xz_s, xz_r, oth_s, oth_r, rim_s, rim_r, s_sem, op_s, op_r, own_sem,
     c1, c2, c3, c4) = take(19)
    assert not refs
    sec = lax.axis_index("section")
    bits, me, mybit = coords(n)
    x = mybit[0]
    neigh = me + 1 - 2 * x
    t_len, width = hout_ref.shape
    inner = w_out.shape[0]
    used = xproj_ref.shape[0]
    cb = 512
    n_half = inner // cb
    rim = rim_ref.shape[2]
    barrier = pltpu.get_barrier_semaphore()
    for k in range(1, n):
        pl.semaphore_signal(barrier, inc=1, device_id=(sec, lax.rem(me + k, n)), device_id_type=MESH)
    pl.semaphore_signal(barrier, inc=1, device_id=(1 - sec, me), device_id_type=MESH)

    in_order = list(range(n_half, 2 * n_half)) + list(range(n_half))

    def in_copy(k, src):
        at = pl.ds(k * cb, cb)
        return pltpu.make_async_copy(src.at[:, at], w_in.at[:, at], wi_sem.at[k])

    def out_copy(src):
        return pltpu.make_async_copy(src, w_out, wo_sem)

    @pl.when(sec == 0)
    def _():
        for k in in_order:
            in_copy(k, in_own).start()
        out_copy(out_own).start()

    @pl.when(sec == 1)
    def _():
        for k in in_order:
            in_copy(k, in_own).start()

    vec2[sec, 0:4, :] = ck_ref[...].astype(F32)
    vec2[sec, 4:5, :] = cb_ref[...].astype(F32)
    vec2[sec, 5:6, :] = dtb_ref[...].astype(F32)
    vec2[sec, 6:7, :] = skip_ref[...].astype(F32)
    vec2[sec, 7:8, 0:width] = gain_ref[...].astype(F32)
    vec2[sec, 7:8, width:inner] = jnp.zeros((1, inner - width), F32)
    xp2[sec, 0:used, :] = xproj_ref[...]
    xp2[sec, used:LANES, :] = jnp.zeros((LANES - used, inner), BF)
    dtp2[sec, 0:rank, :] = dtproj_ref[...]
    dtp2[sec, rank:LANES, :] = jnp.zeros((LANES - rank, inner), BF)
    row = me * t_len + iota((t_len, LANES), 0)
    col = iota((t_len, LANES), 1)
    start = jnp.zeros((t_len, LANES), jnp.int32)
    for cut in range(1, 7):
        bound = bounds_ref[sec, cut]
        start = jnp.where(row >= bound, bound, start)
    tap = jnp.where(row - 3 + col >= start, 1.0, 0.0)
    keeps = jnp.where(row != start, 1.0, 0.0)
    mask_ref[...] = jnp.where(col < 4, tap, jnp.where(col == 4, keeps, 0.0))

    pl.semaphore_wait(barrier, n)

    def sibling(src, dst, a, b):
        return pltpu.make_async_remote_copy(
            src_ref=src, dst_ref=dst, send_sem=a, recv_sem=b, device_id=(1 - sec, me), device_id_type=MESH)

    small = [sibling(r.at[sec], r.at[sec], sm_s.at[i], sm_r.at[i]) for i, r in enumerate((vec2, xp2, dtp2))]
    for cp in small:
        cp.start()

    def rim_copy(layer, to):
        src = tok_ref.at[:, pl.ds(t_len - rim, rim), :] if layer == 0 else hrow.at[pl.ds(t_len - rim, rim), :]
        dst = rim_ref.at[0] if layer == 0 else rim_ref.at[1, 0]
        return pltpu.make_async_remote_copy(
            src_ref=src, dst_ref=dst, send_sem=rim_s.at[layer], recv_sem=rim_r.at[layer],
            device_id=(sec, to), device_id_type=MESH)

    def has_rim(layer, cond):
        return cond & (sec == 0) if layer == 0 else cond

    def send_rim(layer):
        @pl.when(has_rim(layer, me < n - 1))
        def _():
            rim_copy(layer, me + 1).start()

        @pl.when(me == 0)
        def _():
            if layer == 0:
                rim_ref[0] = jnp.zeros(rim_ref.shape[1:], BF)
            else:
                rim_ref[1, 0] = jnp.zeros(rim_ref.shape[2:], BF)

    def get_rim(layer):
        @pl.when(has_rim(layer, me > 0))
        def _():
            rim_copy(layer, me).wait_recv()

    def oth(k):
        if k == 0:
            return sibling(out_own, out_oth, oth_s.at[0], oth_r.at[0])
        return sibling(in_own, in_oth, oth_s.at[1], oth_r.at[1])

    send_rim(0)

    @pl.when(sec == 1)
    def _():
        oth(1).start()

    def xz_copy(k, rows):
        at = pl.ds((k % n_half) * cb, cb)
        dst = loc["z"] if k >= n_half else loc["xi"]
        return sibling(stage.at[k, pl.ds(0, rows), :], dst.at[:, at], xz_s.at[k], xz_r.at[k])

    def normed(h, layer):
        hf = h.astype(F32)
        inv = lax.rsqrt(jnp.mean(hf * hf, axis=-1, keepdims=True) + NORM_EPS)
        return (hf * inv * vec2[layer, 7:8, 0:width]).astype(BF)

    @pl.when(sec == 0)
    def _():
        both = normed(jnp.concatenate([tok_ref[0], tok_ref[1]], axis=0), 0)
        for k in in_order[:n_half]:
            in_copy(k, in_own).wait()
            r = dot(both, w_in[:, k * cb : (k + 1) * cb])
            loc["z"][:, pl.ds((k - n_half) * cb, cb)] = r[:t_len]
            stage[k, 0:t_len, :] = r[t_len:]
            xz_copy(k, t_len).start()
        get_rim(0)
        edge = normed(jnp.concatenate([rim_ref[0, 0], rim_ref[0, 1]], axis=0), 0)
        rows = jnp.concatenate([edge[:rim], both[:t_len], edge[rim:], both[t_len:]], axis=0)
        for k in in_order[n_half:]:
            in_copy(k, in_own).wait()
            r = dot(rows, w_in[:, k * cb : (k + 1) * cb])
            loc["xi"][:, pl.ds(k * cb, cb)] = r[: rim + t_len]
            stage[k] = r[rim + t_len :]
            xz_copy(k, rim + t_len).start()

    hrow[...] = tok_ref[sec]
    for cp in small:
        cp.wait_recv()

    @pl.when(sec == 1)
    def _():
        for k in in_order:
            xz_copy(k, t_len if k >= n_half else rim + t_len).wait_recv()

    @pl.when(sec == 0)
    def _():
        oth(0).start()

    carries = []
    saved = []

    def keep(name, layer):
        cp = pltpu.make_async_copy(loc[name], hbm[layer][name], sv_sem.at[layer, SAVED.index(name)])
        cp.start()
        saved.append((layer, name))

    def kept(name, layer):
        pltpu.make_async_copy(loc[name], hbm[layer][name], sv_sem.at[layer, SAVED.index(name)]).wait()

    def part_copy(kind, layer, k):
        src = (ut_s, ot_s)[kind].at[layer]
        dst = hbm[layer][("ut4", "ot4")[kind]]

        def slot(i):
            return pl.ds(pl.multiple_of(i * t_len, LANES), t_len)

        mine = 2 * sec + x
        if k == 0:
            s, i, to = src.at[:, x], mine, (1 - sec, me)
        elif k == 1:
            s, i, to = src.at[:, 1 - x], mine, (sec, neigh)
        else:
            i, to = 2 * sec + 1 - x, (1 - sec, me)
            s = dst.at[:, :, slot(i)]
        return pltpu.make_async_remote_copy(
            src_ref=s, dst_ref=dst.at[:, :, slot(i)], send_sem=op_s.at[layer, kind, k], recv_sem=op_r.at[layer, kind, i],
            device_id=to, device_id_type=MESH)

    def part_arrived(kind, layer, i):
        dst = hbm[layer][("ut4", "ot4")[kind]]
        at = pl.ds(pl.multiple_of(i * t_len, LANES), t_len)
        pltpu.make_async_remote_copy(
            src_ref=(ut_s, ot_s)[kind].at[layer, :, 0], dst_ref=dst.at[:, :, at], send_sem=op_s.at[layer, kind, 0],
            recv_sem=op_r.at[layer, kind, i], device_id=(1 - sec, me), device_id_type=MESH).wait_recv()

    def part_own(kind, layer):
        at = pl.ds(pl.multiple_of((2 * sec + x) * t_len, LANES), t_len)
        return pltpu.make_async_copy(
            (ut_s, ot_s)[kind].at[layer, :, x], hbm[layer][("ut4", "ot4")[kind]].at[:, :, at], own_sem.at[layer, kind])

    def part_send(kind, layer):
        part_copy(kind, layer, 0).start()
        part_copy(kind, layer, 1).start()
        part_own(kind, layer).start()

    def part_forward(kind, layer):
        part_arrived(kind, layer, 2 * sec + 1 - x)
        part_copy(kind, layer, 2).start()

    mask = mask_ref[...]
    cols = iota((t_len, LANES), 1)
    keepc = mask[:, 4:5]
    for layer in range(2):
        vec, xp, dtp = vec2.at[layer], xp2.at[layer], dtp2.at[layer]
        u = normed(hrow[...], layer)
        if layer == 1:
            for k in in_order[:n_half]:
                in_copy(k, in_own).wait()
                loc["z"][:, pl.ds((k - n_half) * cb, cb)] = dot(u, w_in[:, k * cb : (k + 1) * cb])
            get_rim(1)
            rows = jnp.concatenate([normed(rim_ref[1, 0], 1), u], axis=0)
            for k in in_order[n_half:]:
                in_copy(k, in_own).wait()
                loc["xi"][:, pl.ds(k * cb, cb)] = dot(rows, w_in[:, k * cb : (k + 1) * cb])
        keep("z", layer)
        keep("xi", layer)
        proj = jnp.zeros((t_len, LANES), F32)
        for k in range(n_half):
            at = pl.ds(k * cb, cb)
            xi = loc["xi"][:, at]
            c = vec[4:5, at] + vec[3:4, at] * xi[rim:]
            for j in range(3):
                c = c + vec[j : j + 1, at] * xi[rim - 3 + j : rim - 3 + j + t_len] * mask[:, j : j + 1]
            loc["c"][:, at] = c
            xc = c * jax.nn.sigmoid(c)
            loc["us"][:, at] = xc
            proj = proj + dot_nt(xc.astype(BF), xp[:, at])
        keep("c", layer)
        projb = jnp.where(cols == rank + 2 * N, keepc, proj).astype(BF)
        loc["proj"][...] = projb
        keep("proj", layer)
        pf = projb.astype(F32)
        ksum = jnp.sum(jnp.where((cols >= rank) & (cols < rank + N), pf * pf, 0.0), axis=-1, keepdims=True)
        for k in range(n_half):
            at = pl.ds(k * cb, cb)
            beta = jax.nn.sigmoid(dot(projb, dtp[:, at]) + vec[5:6, at])
            eps = beta / (1.0 + beta * ksum)
            loc["beta"][:, at] = beta
            loc["us"][:, at] = loc["us"][:, at] * eps
            loc["ex"][:, at] = jnp.where(keepc > 0.0, eps, 1.0)
        for name in ("beta", "us", "ex"):
            keep(name, layer)
        nrow = t_len * N
        sel = (iota((nrow, t_len), 0) // N == iota((nrow, t_len), 1)).astype(F32).astype(BF)
        spread = dot(sel, projb).astype(BF)
        rn = iota((nrow, LANES), 0) % N
        cl = iota((nrow, LANES), 1)
        ones = jnp.ones((LANES, LANES), BF)
        zero = jnp.zeros((nrow, LANES), BF)
        kb = dot(jnp.where(cl == rank + rn, spread, zero), ones)
        kb_ref[...] = kb
        loc["qb"][...] = dot(jnp.where(cl == rank + N + rn, spread, zero), ones)
        keepb = dot(jnp.where(cl == rank + 2 * N, spread, zero), ones)
        loc["k2"][...] = jnp.where(keepb > 0.5, -LOG2E * kb * kb, -1e30)
        keep("qb", layer)
        keep("k2", layer)
        ec = 512
        nt = ec // LANES
        un = 8
        k2_ref, ex_ref, us_ref = loc["k2"], loc["ex"], loc["us"]

        def chunk(ci, carry, layer=layer):
            e0 = pl.multiple_of(ci * ec, ec)

            def body(i, sd):
                s, d = [list(v) for v in sd]
                g0 = pl.multiple_of(i * un, un)
                for t in range(un):
                    r = pl.multiple_of(g0 * N + t * N, N)
                    k2 = k2_ref[pl.ds(r, N), :]
                    kv = kb_ref[pl.ds(r, N), :]
                    for j in range(nt):
                        lane = pl.ds(e0 + LANES * j, LANES)
                        a = jnp.exp2(k2 * ex_ref.at[pl.ds(g0, un), lane][t : t + 1, :])
                        s[j] = a * s[j] + kv * us_ref.at[pl.ds(g0, un), lane][t : t + 1, :]
                        d[j] = a * d[j]
                return tuple(s), tuple(d)

            zeros = tuple(jnp.zeros((N, LANES), F32) for _ in range(nt))
            one = tuple(jnp.ones((N, LANES), F32) for _ in range(nt))
            s, d = lax.fori_loop(0, t_len // un, body, (zeros, one))
            for j in range(nt):
                lane = pl.ds(e0 + LANES * j, LANES)
                c_src[layer, 0:N, lane] = d[j].astype(BF)
                c_src[layer, N : 2 * N, lane] = s[j].astype(BF)
            return carry

        lax.fori_loop(0, inner // ec, chunk, 0)
        cr = Carry(sec, me, n, c_src.at[layer], c_recv.at[layer], c_pre.at[layer], c_dst.at[layer],
                   [s.at[layer] for s in (c1, c2, c3, c4)], None, inner)
        cr.decay_out = loc["dec"]
        carries.append(cr)
        if layer == 1:
            for name in ("dec", "sb", "y"):
                kept(name, 0)
        cr.send()
        ut_s[layer] = u.T.reshape(ut_s.shape[1:])
        cr.combine()
        keep("dec", layer)
        cr.get()
        st[...] = c_dst[layer].astype(F32)
        part_send(0, layer)
        if layer == 0:
            @pl.when(sec == 0)
            def _():
                oth(1).start()

            @pl.when(sec == 1)
            def _():
                oth(0).start()
        else:
            part_forward(1, 0)

        def s_copy(blk, slot, layer=layer):
            return pltpu.make_async_copy(
                sbuf.at[slot], hbm[layer]["s"].at[pl.ds(pl.multiple_of(blk * BT * N, BT * N), BT * N), :], s_sem.at[slot])

        steps = t_len // BT

        def block(i, carry, s_copy=s_copy, vec=vec):
            slot = lax.rem(i, 2)
            rows = pl.ds(pl.multiple_of(i * BT, BT), BT)
            rbase = pl.multiple_of(i * BT * N, BT * N)

            @pl.when(i >= 2)
            def _():
                s_copy(i - 2, slot).wait()

            loc["sb"][rows, :] = st[...].astype(BF)
            qbd = block_diag(loc["proj"][rows, :], rank + N).astype(BF)
            s_ref = sbuf.at[slot]
            for ci in range(inner // ec):
                e0 = ci * ec
                s = [st[:, pl.ds(e0 + LANES * j, LANES)] for j in range(nt)]
                for t in range(BT):
                    krow = pl.ds(pl.multiple_of(rbase + t * N, N), N)
                    k2 = k2_ref[krow, :]
                    kv = kb_ref[krow, :]
                    for j in range(nt):
                        lane = pl.ds(e0 + LANES * j, LANES)
                        a = jnp.exp2(k2 * ex_ref.at[rows, lane][t : t + 1, :])
                        s[j] = a * s[j] + kv * us_ref.at[rows, lane][t : t + 1, :]
                        s_ref[t * N : (t + 1) * N, lane] = s[j].astype(BF)
                for j in range(nt):
                    st[:, pl.ds(e0 + LANES * j, LANES)] = s[j]
                at = pl.ds(e0, ec)
                c = loc["c"][rows, at]
                y = dot(qbd, s_ref[:, at]) + vec[6:7, at] * (c * jax.nn.sigmoid(c))
                loc["y"][rows, at] = y
                z = loc["z"][rows, at]
                o_all[rows, at] = (y * (z * jax.nn.sigmoid(z))).astype(BF)
            s_copy(i, slot).start()
            return carry

        lax.fori_loop(0, steps, block, 0)
        keep("sb", layer)
        keep("y", layer)
        part_forward(0, layer)
        if layer == 0:
            @pl.when(sec == 1)
            def _():
                oth(0).wait_recv()
                out_copy(out_oth).start()

            @pl.when(sec == 0)
            def _():
                oth(1).wait_recv()
                for k in in_order:
                    in_copy(k, in_oth).start()

        out_copy(out_own).wait()
        o = o_all[...]
        hn = (hrow[...].astype(F32) + dot(o, w_out[...])).astype(BF)
        if layer == 0:
            hrow[...] = hn
            hmid_ref[...] = hn
            send_rim(1)

            @pl.when(sec == 0)
            def _():
                oth(0).wait_recv()
                out_copy(out_oth).start()

            @pl.when(sec == 1)
            def _():
                oth(1).wait_recv()
                out_copy(out_own).start()
        else:
            hout_ref[...] = hn
        ot_s[layer] = o.T.reshape(ot_s.shape[1:])
        if layer == 0:
            part_send(1, 0)
        else:
            last_o = pltpu.make_async_copy(ot_s.at[1], hbm[1]["ot4"], own_sem.at[1, 1])
            last_o.start()
        for slot in range(2):
            s_copy(steps - 2 + slot, slot).wait()
        if layer == 0:
            for name in SAVED:
                if name not in ("dec", "sb", "y"):
                    kept(name, 0)

    for name in SAVED:
        kept(name, 1)
    last_o.wait()
    for layer, kind in ((0, 0), (0, 1), (1, 0)):
        part_own(kind, layer).wait()
        for i in range(2):
            part_arrived(kind, layer, 2 * (1 - sec) + (x if i == 0 else 1 - x))
        for k in range(3):
            part_copy(kind, layer, k).wait_send()
    for cp in small:
        cp.wait_send()
    for k in range(2):
        oth(k).wait_send()

    @pl.when(sec == 0)
    def _():
        for k in in_order:
            xz_copy(k, t_len if k >= n_half else rim + t_len).wait_send()

    for layer in range(2):
        @pl.when(has_rim(layer, me < n - 1))
        def _(layer=layer):
            rim_copy(layer, me + 1).wait_send()

    for cr in carries:
        cr.sent()


def forward(n, rank, cid, bounds, tokens, smalls, in_own, out_own):
    t_len, width = tokens.shape[1:]
    inner = out_own.shape[0]
    rim = 16
    rows = t_len * N

    def f32(*s):
        return jax.ShapeDtypeStruct(s, F32)

    def b16(*s):
        return jax.ShapeDtypeStruct(s, BF)

    shapes = {
        "xi": f32(t_len + rim, inner), "z": f32(t_len, inner), "c": f32(t_len, inner), "beta": f32(t_len, inner),
        "ex": f32(t_len, inner), "us": f32(t_len, inner), "k2": f32(rows, LANES), "qb": f32(rows, LANES),
        "y": f32(t_len, inner), "proj": b16(t_len, LANES), "dec": b16(n, N, LANES), "sb": b16(t_len, inner),
    }
    outs = [
        b16(width, 2 * inner), b16(inner, width), f32(t_len, LANES), b16(2, LANES, inner), b16(2, LANES, inner),
        f32(2, 8, inner), b16(t_len, width), b16(t_len, width),
    ]
    specs = [ANYSPEC, ANYSPEC] + [VSPEC] * 6
    for layer in range(2):
        outs += [shapes[name] for name in SAVED]
        outs += [b16(rows, inner), b16(n // 2, width // n, 4 * t_len)]
        outs += [b16(n // 2, 2, inner // n, t_len) if layer else b16(n // 2, inner // n, 4 * t_len)]
        specs += [ANYSPEC] * (len(SAVED) + 3)
    scratch = [pltpu.VMEM(shapes[name].shape, shapes[name].dtype) for name in SAVED]
    scratch += [
        pltpu.VMEM((rows, LANES), F32), pltpu.VMEM((width, 2 * inner), BF), pltpu.VMEM((inner, width), BF),
        pltpu.VMEM((2 * inner // 512, rim + t_len, 512), F32), pltpu.VMEM((2, 2, rim, width), BF),
        pltpu.VMEM((t_len, width), BF), pltpu.VMEM((N, inner), F32), pltpu.VMEM((2, BT * N, inner), BF),
        pltpu.VMEM((t_len, inner), BF), pltpu.VMEM((2, n // 2, 2, width // n, t_len), BF),
        pltpu.VMEM((2, n // 2, 2, inner // n, t_len), BF),
        pltpu.VMEM((2, 2 * N, inner), BF), pltpu.VMEM((2, n, 2 * N, LANES), BF), pltpu.VMEM((2, n, N, LANES), BF),
        pltpu.VMEM((2, N, inner), BF),
    ]
    dma = pltpu.SemaphoreType.DMA
    n_in = 2 * inner // 512
    scratch += [
        dma((2, len(SAVED))), dma((n_in,)), dma(()), dma((3,)), dma((3,)), dma((n_in,)), dma((n_in,)), dma((2,)), dma((2,)),
        dma((2,)), dma((2,)), dma((2,)), dma((2, 2, 3)), dma((2, 2, 4)), dma((2, 2)),
        dma((2, n)), dma((2, n)), dma((2, n)), dma((2, n)),
    ]
    res = pl.pallas_call(
        functools.partial(forward_kernel, n, rank),
        out_shape=outs,
        in_specs=[pl.BlockSpec(memory_space=pltpu.SMEM)] + [VSPEC] * 8 + [ANYSPEC] * 2,
        out_specs=specs,
        scratch_shapes=scratch,
        compiler_params=pltpu.CompilerParams(vmem_limit_bytes=60 * MIB, collective_id=cid, has_side_effects=True),
        name="forward",
    )(bounds, tokens, *smalls, in_own, out_own)
    first, rest = res[:8], res[8:]
    per = len(SAVED) + 3
    saved = [dict(zip(SAVED + ("s", "ut4", "ot4"), rest[i * per : (i + 1) * per])) for i in range(2)]
    return first, saved


class Sub:
    def __init__(self, kit, num, layer, buf, recvs, out, lane0, lanes, steps, held):
        self.kit, self.num, self.layer = kit, num, layer
        self.at = pl.ds(lane0, lanes)
        self.buf, self.recvs, self.out = buf, recvs, out
        self.steps, self.held = steps, held
        self.last = len(steps) - 1
        self.stage = 0

    def bit(self, what):
        return self.kit.sec if what == "s" else self.kit.mybit[what]

    def partner(self, i):
        kit, what = self.kit, self.steps[i]
        if what == "s":
            return (1 - kit.sec, kit.me)
        return (kit.sec, kit.me + 2**what * (1 - 2 * kit.mybit[what]))

    def index(self, i, away):
        done = {w: self.bit(w) for w in self.steps[:i]}
        what = self.steps[i]
        done[what] = 1 - self.bit(what) if away else self.bit(what)
        return tuple(done.get(w, slice(None)) for w in self.held)

    def copy(self, i):
        free = len(self.held) - 1 - i
        return pltpu.make_async_remote_copy(
            src_ref=self.buf.at[self.index(i, True) + (slice(None), self.at)],
            dst_ref=self.recvs[i].at[(slice(None),) * (free + 1) + (self.at,)],
            send_sem=self.kit.ssem.at[self.layer, self.num, i], recv_sem=self.kit.rsem.at[self.layer, self.num, i],
            device_id=self.partner(i), device_id_type=MESH)

    def begin(self):
        self.copy(0).start()

    def place(self, half):
        return self.kit.place[self.out](half, self.at)

    def final(self):
        kit = self.kit
        return pltpu.make_async_remote_copy(
            src_ref=kit.res[self.out].at[:, self.at], dst_ref=self.place(1 - self.layer),
            send_sem=kit.fsem.at[self.layer, self.num], recv_sem=kit.frsem.at[self.layer, self.num],
            device_id=(1 - kit.sec, kit.me), device_id_type=MESH)

    def advance(self):
        i = self.stage
        if i > self.last:
            return
        kit = self.kit
        self.copy(i).wait_recv()
        free = len(self.held) - 1 - i
        fixed = self.index(i, False)
        res = kit.res[self.out]

        def body(k, carry):
            sub = list(unpack_index(k, free))
            src = tuple(sub) + (slice(None), self.at)
            dst = tuple(sub.pop(0) if isinstance(f, slice) else f for f in fixed) + (slice(None), self.at)
            if i == self.last:
                val = self.buf[dst].astype(F32) + self.recvs[i][src].astype(F32)

                @pl.when(kit.sec == self.layer)
                def _():
                    self.place(self.layer)[...] = val

                @pl.when(kit.sec != self.layer)
                def _():
                    res[:, self.at] = val
            else:
                self.buf[dst] = self.buf[dst] + self.recvs[i][src]
            return carry

        if free:
            lax.fori_loop(0, 2**free, body, 0)
        else:
            body(0, 0)
        self.stage = i + 1
        if i < self.last:
            self.copy(i + 1).start()
        else:
            @pl.when(kit.sec != self.layer)
            def _():
                self.final().start()

    def finish(self):
        assert self.stage > self.last
        for i in range(self.last + 1):
            self.copy(i).wait_send()

        @pl.when(self.kit.sec != self.layer)
        def _():
            self.final().wait_send()

        @pl.when(self.kit.sec == self.layer)
        def _():
            self.final().wait_recv()


class VecSum:
    def __init__(self, kit, layer, n, acc, sib, msg, got, out):
        self.kit, self.layer, self.n = kit, layer, n
        self.acc, self.sib, self.msg, self.got, self.out = acc, sib, msg, got, out
        self.stage = 0

    def across(self):
        kit = self.kit
        return pltpu.make_async_remote_copy(
            src_ref=self.acc.at[self.layer], dst_ref=self.sib.at[self.layer],
            send_sem=kit.vsem.at[self.layer], recv_sem=kit.vrsem.at[self.layer],
            device_id=(1 - kit.sec, kit.me), device_id_type=MESH)

    def copy(self, k, dev, slot):
        kit = self.kit
        return pltpu.make_async_remote_copy(
            src_ref=self.msg.at[dev], dst_ref=self.got.at[slot],
            send_sem=kit.v2sem.at[self.layer, k], recv_sem=kit.v2rsem.at[self.layer, slot],
            device_id=(kit.sec, dev), device_id_type=MESH)

    def begin(self):
        @pl.when(self.kit.sec != self.layer)
        def _():
            self.across().start()

    def advance(self):
        kit, n = self.kit, self.n
        if self.stage > 1:
            return
        first = self.stage == 0
        self.stage += 1

        @pl.when(kit.sec == self.layer)
        def _():
            if first:
                self.across().wait_recv()
                total = self.acc[self.layer] + self.sib[self.layer]
                inner = total.shape[1]
                for j in range(n):
                    l0 = (j * (inner // n)) // LANES * LANES
                    g0 = (j * (kit.width // n)) // LANES * LANES
                    self.msg[j, 0:8, :] = total[:, l0 : l0 + LANES]
                    self.msg[j, 8:16, :] = total[:, g0 : g0 + LANES]
                for k in range(1, n):
                    self.copy(k, lax.rem(kit.me + k, n), kit.me).start()
                self.got[kit.me] = self.msg[kit.me]
            else:
                for k in range(1, n):
                    frm = lax.rem(kit.me + k, n)
                    self.copy(k, frm, frm).wait_recv()
                val = self.got[0]
                for j in range(1, n):
                    val = val + self.got[j]
                self.out[...] = val

    def drain(self):
        kit = self.kit
        while self.stage < 2:
            self.advance()

        @pl.when(kit.sec != self.layer)
        def _():
            self.across().wait_send()

        @pl.when(kit.sec == self.layer)
        def _():
            for k in range(1, self.n):
                self.copy(k, lax.rem(kit.me + k, self.n), kit.me).wait_send()


class Kit:
    pass


class Gather:
    def __init__(self, kit, kind, layer, src, dst):
        self.kit, self.kind, self.layer = kit, kind, layer
        self.src, self.dst = src, dst

    def peers(self):
        kit = self.kit
        x = kit.mybit[0]
        other = kit.me + 1 - 2 * x
        return [(1 - kit.sec, kit.me, x), (kit.sec, other, 1 - x), (1 - kit.sec, other, 1 - x)]

    def copy(self, k, slot):
        kit = self.kit
        sec, dev, bit = self.peers()[k]
        return pltpu.make_async_remote_copy(
            src_ref=self.src(sec, bit), dst_ref=self.dst(slot),
            send_sem=kit.osem.at[self.layer, self.kind, k], recv_sem=kit.orsem.at[self.layer, self.kind, slot],
            device_id=(sec, dev), device_id_type=MESH)

    def slot(self, sec, bit):
        return 2 * sec + bit

    def send(self, order=(1, 2, 0)):
        mine = self.slot(self.kit.sec, self.kit.mybit[0])
        for k in order:
            self.copy(k, mine).start()

    def wait(self):
        for k in range(3):
            sec, dev, bit = self.peers()[k]
            self.copy(k, self.slot(sec, bit)).wait_recv()

    def sent(self):
        mine = self.slot(self.kit.sec, self.kit.mybit[0])
        for k in range(3):
            self.copy(k, mine).wait_send()


LOADS = ("h", "xi", "z", "c", "proj", "beta", "ex", "us", "k2", "qb", "sb", "y", "dec")
BOTH = ("h", "proj", "dec", "sb")
BIG = ("go", "gz", "gx")


def lane_parts(lanes):
    unit = lanes // LANES
    a = max(1, (3 * unit) // 4)
    return [(0, a * LANES, 0), (a * LANES, lanes - a * LANES, 1)]


def two_parts(lanes):
    return [(0, lanes // 2, 0), (lanes // 2, lanes // 4, 0), (3 * lanes // 4, lanes // 4, 1)]


def bit_orders(bits):
    low = list(range(1, bits))
    return [low, [2, 1] + low[2:]]


def back_kernel(n, rank, shapes, *refs):
    refs = list(refs)

    def take(k):
        out = refs[:k]
        del refs[:k]
        return out

    tokens, cots, mask_ref, in_own, in_oth, out_own, out_oth = take(7)
    hbm = [dict(zip(LOADS + ("s", "ut4", "ot4"), take(len(LOADS) + 3))) for _ in range(2)]
    vec2, xp2, dtp2 = take(3)
    dh_out, gin_out, gout_out, gsm_out, vec_out = take(5)
    loc = {name: (take(2) if name in BOTH else take(1) * 2) for name in LOADS}
    (g_both, w_out, w_in, sbuf, qs2, ws2, bst, deps, dkq, dy_ref, dz_both, dx_both, gdt_ref, gtmp, rims, rimr) = take(16)
    dxc = loc["y"][0]
    ut4, ot4, dr4, dz4, dx4 = take(5)
    kit = Kit()
    bits, me, mybit = coords(n)
    bufs = [dict(zip(BIG + ("sm",), take(4))) for _ in range(2)]
    recvs = []
    for _ in range(2):
        got = {name: take(bits - 1) for name in BIG}
        got["sm"] = take(bits + 1)
        recvs.append(got)
    kit.res = dict(zip(BIG + ("sm",), take(4)))
    vacc, vsib, vmsg, vgot = take(4)
    c_src, c_recv, c_pre, c_dst = take(4)
    (ld_sem, g_sem, wo_sem, wi_sem, s_sem, rim_sem, rimr_sem, own_sem, kit.osem, kit.orsem, kit.ssem, kit.rsem,
     kit.fsem, kit.frsem, kit.vsem, kit.vrsem, kit.v2sem, kit.v2rsem, o_sem, o_rsem, c1, c2, c3, c4) = take(24)
    assert not refs
    sec = lax.axis_index("section")
    kit.sec, kit.me, kit.bits, kit.mybit = sec, me, bits, mybit
    t_len, width = dh_out.shape
    inner = w_out.shape[0]
    cb = 512
    lead = shapes["lead"]

    barrier = pltpu.get_barrier_semaphore()
    for k in range(1, n):
        pl.semaphore_signal(barrier, inc=1, device_id=(sec, lax.rem(me + k, n)), device_id_type=MESH)
    for to in (me, me + 1 - 2 * mybit[0]):
        pl.semaphore_signal(barrier, inc=1, device_id=(1 - sec, to), device_id_type=MESH)

    pos = {name: i for i, name in enumerate(LOADS)}

    def load(name, layer):
        src = tokens.at[sec] if (name, layer) == ("h", 0) else hbm[layer][name]
        return pltpu.make_async_copy(src, loc[name][layer], ld_sem.at[pos[name], layer])

    def out_chunk(k, src):
        at = pl.ds(k * cb, cb)
        return src.at[at, :], w_out.at[at, :], wo_sem.at[k]

    def in_chunk(k, slot, src):
        return src.at[:, pl.ds(k * cb, cb)], w_in.at[slot], wi_sem.at[slot]

    def fetch(layer, chunk, own, oth):
        a, b, s = chunk(own)
        a2 = chunk(oth)[0]

        @pl.when(sec == layer)
        def _():
            pltpu.make_async_copy(a, b, s).start()

        @pl.when(sec != layer)
        def _():
            pltpu.make_async_copy(a2, b, s).start()

    def arrive(chunk, own):
        a, b, s = chunk(own)
        pltpu.make_async_copy(a, b, s).wait()

    n_out = inner // cb
    n_in = 2 * inner // cb
    in_order = list(range(n_in // 2, n_in)) + list(range(n_in // 2))
    slots = w_in.shape[0]

    cot_hbm = cots.at[sec]
    pltpu.make_async_copy(cot_hbm, g_both.at[1], g_sem).start()
    for k in range(n_out):
        fetch(1, lambda src, k=k: out_chunk(k, src), out_own, out_oth)
    for name in ("z", "y", "c", "ex", "k2", "qb", "dec", "proj", "beta", "us", "sb", "xi", "h"):
        load(name, 1).start()
    for name in BOTH:
        load(name, 0).start()
    for i in range(slots):
        fetch(1, lambda src, i=i: in_chunk(in_order[i], i, src), in_own, in_oth)

    half_go = width // 2
    half_in = inner // 2
    kit.place = {
        "go": lambda hf, at: gout_out.at[:, pl.ds(hf * half_go + at.start, at.size)],
        "gz": lambda hf, at: gin_out.at[:, pl.ds(inner + hf * half_in + at.start, at.size)],
        "gx": lambda hf, at: gin_out.at[:, pl.ds(hf * half_in + at.start, at.size)],
        "sm": lambda hf, at: gsm_out.at[hf, :, at],
    }
    gx_parts = two_parts(half_in)
    subs = []
    for layer in range(2):
        mine = {}
        num = 0
        for name, parts in (("go", lane_parts(half_go)), ("gz", lane_parts(half_in)), ("gx", gx_parts)):
            mine[name] = []
            for l0, ln, which in parts:
                mine[name].append(
                    Sub(kit, num, layer, bufs[layer][name], recvs[layer][name], name, l0, ln, bit_orders(bits)[which],
                        list(range(bits - 1, 0, -1))))
                num += 1
        mine["sm"] = [Sub(kit, num, layer, bufs[layer]["sm"], recvs[layer]["sm"], "sm", 0, LANES,
                          ["s", 2, 1, 0] + list(range(3, bits)), ["s"] + list(range(bits - 1, -1, -1)))]
        subs.append(mine)

    def begin(layer, name):
        for s in subs[layer][name]:
            s.begin()

    def advance(layer, *names):
        for name in names:
            if name == "vec":
                vecs[layer].advance()
            else:
                for s in subs[layer][name]:
                    s.advance()

    rows_go = inner // n
    rows_in = width // n
    rows_sm = inner // n
    x = mybit[0]

    def owner(j, count):
        return tuple((j >> (count - 1 - d)) & 1 for d in range(count))

    my_slot = 2 * sec + x

    def operands(layer):
        half = n // 2

        def lanes_of(ref, size):
            return lambda sc, b: ref.at[:, pl.ds(pl.multiple_of(sc * size, LANES), size)]

        def rows_of(ref):
            return lambda slot: ref.at[layer, slot]

        quarter = half_in // 2

        def part_of(ref, p):
            return lambda sc, b: ref.at[:, pl.ds(pl.multiple_of(sc * half_in + p * quarter, LANES), quarter)]

        def part_to(ref, p):
            return lambda slot: ref.at[layer, slot, :, pl.ds(p * quarter, quarter)]

        return {
            "dr": Gather(kit, 0, layer, lanes_of(g_both.at[layer], half_go), rows_of(dr4)),
            "dz": Gather(kit, 1, layer, lanes_of(dz_both.at[layer], half_in), rows_of(dz4)),
            "dx0": Gather(kit, 2, layer, part_of(dx_both.at[layer], 0), part_to(dx4, 0)),
            "dx1": Gather(kit, 3, layer, part_of(dx_both.at[layer], 1), part_to(dx4, 1)),
        }

    ops = [operands(layer) for layer in range(2)]

    def part_load(layer, k):
        src, dst = (("ut4", ut4), ("ot4", ot4))[k]
        return pltpu.make_async_copy(hbm[layer][src], dst.at[layer], own_sem.at[layer, k])

    def own_half(ref, layer, size):
        return ref[layer, :, pl.ds(pl.multiple_of(sec * size, LANES), size)]

    pl.semaphore_wait(barrier, n + 1)
    kit.width = width
    vecs = [VecSum(kit, layer, n, vacc, vsib, vmsg, vgot, vec_out) for layer in range(2)]
    pltpu.make_async_copy(cot_hbm, g_both.at[1], g_sem).wait()
    def slot_at(i):
        return pl.ds(pl.multiple_of(i * t_len, LANES), t_len)

    o_hbm = hbm[1]["ot4"]
    o_own = pltpu.make_async_copy(o_hbm.at[:, x], ot4.at[1, :, :, slot_at(my_slot)], own_sem.at[1, 1])

    def o_copy(k):
        i = my_slot if k < 2 else 2 * sec + 1 - x
        dst = ot4.at[1, :, :, slot_at(i)]
        src = (o_hbm.at[:, 1 - x], o_hbm.at[:, x], dst)[k]
        return pltpu.make_async_remote_copy(
            src_ref=src, dst_ref=dst, send_sem=o_sem.at[k], recv_sem=o_rsem.at[i],
            device_id=(sec, me + 1 - 2 * x) if k == 0 else (1 - sec, me), device_id_type=MESH)

    def o_wait(i):
        dst = ot4.at[1, :, :, slot_at(i)]
        pltpu.make_async_remote_copy(
            src_ref=dst, dst_ref=dst, send_sem=o_sem.at[0], recv_sem=o_rsem.at[i],
            device_id=(1 - sec, me), device_id_type=MESH).wait_recv()

    o_copy(0).start()
    o_copy(1).start()
    o_own.start()
    ops[1]["dr"].send()
    for layer, k in ((1, 0), (0, 1), (0, 0)):
        part_load(layer, k).start()

    def grad_go(layer):
        ops[layer]["dr"].wait()
        if layer == 1:
            o_own.wait()
            o_wait(2 * (1 - sec) + x)
            o_wait(2 * (1 - sec) + 1 - x)
        else:
            part_load(layer, 1).wait()
        dr4[layer, my_slot] = own_half(g_both, layer, half_go)
        rhs = dr4[layer].reshape(4 * t_len, half_go)
        for j in range(n // 2):
            bufs[layer]["go"][owner(j, bits - 1)] = dot(ot4[layer, j], rhs).astype(BF)

    def grad_in(name, layer, four, l0):
        lhs = ut4[layer].reshape(n // 2 * rows_in, 4 * t_len)
        at = pl.ds(l0, cb)
        g = dot(lhs, four[layer, :, :, at].reshape(4 * t_len, cb)).astype(BF)
        for j in range(n // 2):
            bufs[layer][name][owner(j, bits - 1) + (slice(None), at)] = g[j * rows_in : (j + 1) * rows_in]

    def grad_gz(layer):
        ops[layer]["dz"].wait()
        part_load(layer, 0).wait()
        dz4[layer, my_slot] = own_half(dz_both, layer, half_in)
        for l0 in range(0, half_in, cb):
            grad_in("gz", layer, dz4, l0)
        begin(layer, "gz")

    def grad_gx(layer, p):
        if p == 0:
            dx4[layer, my_slot] = own_half(dx_both, layer, half_in)
        ops[layer]["dx0" if p == 0 else "dx1"].wait()
        for l0 in range(p * half_in // 2, (p + 1) * half_in // 2, cb):
            grad_in("gx", layer, dx4, l0)

    carries = []
    for layer in (1, 0):
        g_ref = g_both.at[layer]
        dz_ref = dz_both.at[layer]
        L = {name: loc[name][layer] for name in LOADS}
        vec, xp, dtp = vec2.at[layer], xp2.at[layer], dtp2.at[layer]
        vacc[layer] = jnp.zeros(vacc.shape[1:], F32)
        for name in ("z", "y", "c"):
            load(name, layer).wait()
        dr = g_ref[...]
        for k in range(n_out):
            at = pl.ds(k * cb, cb)
            arrive(lambda src, k=k: out_chunk(k, src), out_own)
            do = dot_nt(dr, w_out[at, :])
            act, der = silu_parts(L["z"][:, at])
            dy = do * act
            dy_ref[:, at] = dy
            dz_ref[:, at] = (do * L["y"][:, at] * der).astype(BF)
            c = L["c"][:, at]
            vacc[layer, 6:7, at] = jnp.sum(dy * (c * jax.nn.sigmoid(c)), axis=0, keepdims=True)
        if layer == 1:
            for k in range(n_out):
                fetch(0, lambda src, k=k: out_chunk(k, src), out_own, out_oth)
            load("z", 0).start()
        if layer == 0:
            advance(1, "gz", "vec", "sm")
        for name in ("ex", "k2", "qb"):
            load(name, layer).wait()
        k2_ref, qb_ref, ex_ref = L["k2"], L["qb"], L["ex"]
        ec = 512
        nt = ec // LANES
        un = 8

        def chunk(ci, carry, k2_ref=k2_ref, qb_ref=qb_ref, ex_ref=ex_ref, layer=layer):
            e0 = pl.multiple_of(ci * ec, ec)

            def body(i, b):
                b = list(b)
                g0 = pl.multiple_of((t_len // un - 1 - i) * un, un)
                for t in range(un - 1, -1, -1):
                    r = pl.multiple_of(g0 * N + t * N, N)
                    k2 = k2_ref[pl.ds(r, N), :]
                    qv = qb_ref[pl.ds(r, N), :]
                    for j in range(nt):
                        lane = pl.ds(e0 + LANES * j, LANES)
                        a = jnp.exp2(k2 * ex_ref.at[pl.ds(g0, un), lane][t : t + 1, :])
                        b[j] = a * (qv * dy_ref.at[pl.ds(g0, un), lane][t : t + 1, :] + b[j])
                return tuple(b)

            b = lax.fori_loop(0, t_len // un, body, tuple(jnp.zeros((N, LANES), F32) for _ in range(nt)))
            for j in range(nt):
                c_src[layer, :, pl.ds(e0 + LANES * j, LANES)] = b[j].astype(BF)
            return carry

        lax.fori_loop(0, inner // ec, chunk, 0)
        load("dec", layer).wait()
        cr = Carry(sec, me, n, c_src.at[layer], c_recv.at[layer], c_pre.at[layer], c_dst.at[layer],
                   [s.at[layer] for s in (c1, c2, c3, c4)], L["dec"], inner)
        carries.append(cr)
        cr.send()
        if layer == 1:
            o_wait(2 * sec + 1 - x)
            o_copy(2).start()
        else:
            grad_go(0)
        cr.combine()
        if layer == 0:
            grad_gx(1, 0)
            grad_gx(1, 1)
        steps = t_len // BT

        def s_copy(blk, slot, layer=layer):
            return pltpu.make_async_copy(
                hbm[layer]["s"].at[pl.ds(pl.multiple_of(blk * BT * N, BT * N), BT * N), :], sbuf.at[slot],
                s_sem.at[slot])

        s_copy(steps - 1, 0).start()
        for name in ("proj", "beta", "us", "sb"):
            load(name, layer).wait()
        cr.get()
        bst[...] = c_dst[layer].astype(F32)
        if layer == 0:
            begin(1, "gx")
            advance(1, "gz", "vec", "sm")
        ops[layer]["dz"].send()
        if layer == 1:
            grad_go(1)
        begin(layer, "go")

        def block(i, carry, L=L, vec=vec, s_copy=s_copy, dy_ref=dy_ref):
            blk = steps - 1 - i
            slot = lax.rem(i, 2)
            base = pl.multiple_of(blk * BT, BT)
            rows = pl.ds(base, BT)
            rbase = pl.multiple_of(blk * BT * N, BT * N)

            @pl.when(i + 1 < steps)
            def _():
                s_copy(blk - 1, 1 - slot).start()

            s_copy(blk, slot).wait()
            projb = L["proj"][rows, :]
            pf = projb.astype(F32)
            cols = iota((BT, LANES), 1)
            is_k = (cols >= rank) & (cols < rank + N)
            ksum = jnp.sum(jnp.where(is_k, pf * pf, 0.0), axis=-1, keepdims=True)
            kbd = block_diag(projb, rank)
            k2bd = (kbd * kbd).astype(BF)
            kbd = kbd.astype(BF)
            r1 = jnp.zeros((BT, BT * N), F32)
            r2 = jnp.zeros((BT, BT * N), F32)
            r3 = jnp.zeros((BT, BT * N), F32)
            s_blk = sbuf.at[slot]
            for ci in range(inner // ec):
                e0 = ci * ec
                qs, ws = qs2.at[ci % 2], ws2.at[ci % 2]
                b = [bst[:, pl.ds(e0 + LANES * j, LANES)] for j in range(nt)]
                for t in range(BT - 1, -1, -1):
                    row = slice(t * N, (t + 1) * N)
                    krow = pl.ds(pl.multiple_of(rbase + t * N, N), N)
                    k2 = L["k2"][krow, :]
                    qv = L["qb"][krow, :]
                    for j in range(nt):
                        lane = pl.ds(e0 + LANES * j, LANES)
                        a = jnp.exp2(k2 * L["ex"].at[rows, lane][t : t + 1, :])
                        q = qv * dy_ref.at[rows, lane][t : t + 1, :] + b[j]
                        b[j] = a * q
                        prev = s_blk[(t - 1) * N : t * N, lane] if t > 0 else L["sb"][rows, lane]
                        qs[row, LANES * j : LANES * (j + 1)] = q.astype(BF)
                        ws[row, LANES * j : LANES * (j + 1)] = (b[j] * prev.astype(F32)).astype(BF)
                for j in range(nt):
                    bst[:, pl.ds(e0 + LANES * j, LANES)] = b[j]
                at = pl.ds(e0, ec)
                p1 = dot(kbd, qs[...])
                p2 = dot(k2bd, ws[...])
                c = L["c"][rows, at]
                beta = L["beta"][rows, at]
                eps = beta / (1.0 + beta * ksum)
                dy = dy_ref[rows, at]
                deps[rows, at] = (c * jax.nn.sigmoid(c)) * p1 - p2
                dxc[rows, at] = dy * vec[6:7, at] + eps * p1
                r1 = r1 + dot_nt(L["us"][rows, at].astype(BF), qs[...])
                r2 = r2 + dot_nt(eps.astype(BF), ws[...])
                r3 = r3 + dot_nt(dy.astype(BF), s_blk[:, at])
            same = iota((BT, BT * N), 0) == iota((BT, BT * N), 1) // N
            gather_k = (iota((BT * N, LANES), 1) == rank + iota((BT * N, LANES), 0) % N).astype(F32)
            gather_q = (iota((BT * N, LANES), 1) == rank + N + iota((BT * N, LANES), 0) % N).astype(F32)

            def pick(r, g):
                return jnp.dot(
                    jnp.where(same, r, 0.0), g, precision=lax.Precision.HIGHEST, preferred_element_type=F32)

            dkq[rows, :] = pick(r1, gather_k) - 2.0 * pf * pick(r2, gather_k) + pick(r3, gather_q)
            return carry

        def tick(k, layer=layer):
            if layer == 1:
                if k == 2:
                    grad_gz(1)
                if k == 3:
                    advance(1, "go")
                return
            if k == 1:
                advance(1, "sm")
            if k == 2:
                advance(1, "gx")
                grad_gz(0)
            if k == 3:
                advance(0, "go")
                advance(1, "gx", "sm")

        def block_and_tick(i, carry):
            block(i, carry)
            for k in range(4):
                @pl.when(i == (k + 1) * steps // 4 - 1)
                def _(k=k):
                    tick(k)

            return carry

        lax.fori_loop(0, steps, block_and_tick, 0)
        if layer == 1:
            for name in ("k2", "qb", "ex", "us"):
                load(name, 0).start()
        load("xi", layer).wait()
        projw = L["proj"][...]
        pw = projw.astype(F32)
        colw = iota((t_len, LANES), 1)
        kall = jnp.where((colw >= rank) & (colw < rank + N), pw, 0.0)
        ks = jnp.sum(kall * kall, axis=-1, keepdims=True)
        tc = 256
        def first(k, carry, L=L, dtp=dtp, layer=layer, projw=projw, ks=ks):
            dkc, ddt = carry
            at = pl.ds(pl.multiple_of(k * tc, tc), tc)
            beta = L["beta"][:, at]
            inv = 1.0 / (1.0 + beta * ks)
            dq = deps[:, at] * (inv * inv)
            dkc = dkc + jnp.sum(dq * beta * beta, axis=-1, keepdims=True)
            dp = (dq * beta * (1.0 - beta)).astype(BF)
            vacc[layer, 5:6, at] = jnp.sum(dp.astype(F32), axis=0, keepdims=True)
            gdt_ref[:, at] = dot_tn(projw, dp)[:rank]
            ddt = ddt + dot_nt(dp, dtp[:, at])
            return dkc, ddt

        dkc, ddt = lax.fori_loop(
            0, inner // tc, first, (jnp.zeros((t_len, 1), F32), jnp.zeros((t_len, LANES), F32)))
        dproj = (jnp.where(colw < rank, ddt, dkq[...]) - 2.0 * kall * dkc).astype(BF)
        mask = mask_ref[...]

        def second(k, carry, L=L, xp=xp, layer=layer, dproj=dproj, ck_ref=vec):
            at = pl.ds(pl.multiple_of(k * tc, tc), tc)
            c = L["c"][:, at]
            act, der = silu_parts(c)
            gxp = dot_tn(act.astype(BF), dproj).astype(BF)
            for i in range(tc // rows_sm):
                j = k * (tc // rows_sm) + i
                bufs[layer]["sm"][(0,) + unpack_index(j, bits)] = gxp[i * rows_sm : (i + 1) * rows_sm]
            dc = (dxc[:, at] + dot(dproj, xp[:, at])) * der
            vacc[layer, 4:5, at] = jnp.sum(dc, axis=0, keepdims=True)
            xi = L["xi"][:, at]
            pad = jnp.zeros((8, tc), F32)
            dxi = ck_ref[3:4, at] * dc
            rim = jnp.zeros((8, tc), F32)
            vacc[layer, 3:4, at] = jnp.sum(dc * xi[lead:], axis=0, keepdims=True)
            for j in range(3):
                m = dc * mask[:, j : j + 1]
                vacc[layer, j : j + 1, at] = jnp.sum(m * xi[lead - 3 + j : lead - 3 + j + t_len], axis=0, keepdims=True)
                m = m * ck_ref[j : j + 1, at]
                ext = jnp.concatenate([pad, m, pad], axis=0)
                dxi = dxi + ext[8 + 3 - j : 8 + 3 - j + t_len]
                rim = rim + ext[8 - j : 16 - j]
            deps[:, at] = dxi
            rims[layer, :, at] = jnp.where(iota((8, tc), 0) < 3, rim, 0.0)
            return carry

        lax.fori_loop(0, inner // tc, second, 0)

        def rim_copy(to, layer=layer):
            return pltpu.make_async_remote_copy(
                src_ref=rims.at[layer], dst_ref=rimr.at[layer], send_sem=rim_sem.at[layer], recv_sem=rimr_sem.at[layer],
                device_id=(sec, to), device_id_type=MESH)

        @pl.when(me > 0)
        def _():
            rim_copy(me - 1).start()

        @pl.when(me == n - 1)
        def _():
            rimr[layer] = jnp.zeros(rimr.shape[1:], F32)

        if layer == 1:
            for name in ("c", "beta", "xi", "y"):
                load(name, 0).start()
        prow = rank // n
        for j in range(n):
            for t in range(inner // LANES):
                gtmp[j, t * prow : (t + 1) * prow, :] = gdt_ref[j * prow : (j + 1) * prow, t * LANES : (t + 1) * LANES]
        drow = prow * (inner // LANES)
        for j in range(n):
            bufs[layer]["sm"][(1,) + owner(j, bits) + (slice(0, drow),)] = gtmp[j, 0:drow].astype(BF)
        begin(layer, "sm")
        advance(layer, "go")
        if layer == 0:
            advance(1, "gx")
            advance(0, "gz")
        du = jnp.zeros((t_len, width), F32)

        def project(du, i, g, layer=layer):
            slot = i % slots
            arrive(lambda src: in_chunk(in_order[i], slot, src), in_own)
            du = du + dot_nt(g, w_in[slot])
            if i + slots < n_in:
                fetch(layer, lambda src: in_chunk(in_order[i + slots], slot, src), in_own, in_oth)
            elif layer == 1:
                fetch(0, lambda src: in_chunk(in_order[i + slots - n_in], slot, src), in_own, in_oth)
            return du

        for i in range(n_in // 2):
            du = project(du, i, dz_ref[:, pl.ds(i * cb, cb)])

        @pl.when(me < n - 1)
        def _():
            rim_copy(me).wait_recv()

        tail = jnp.concatenate([jnp.zeros((5, inner), F32), rimr[layer][0:3]], axis=0)
        deps[pl.ds(t_len - 8, 8), :] = deps[pl.ds(t_len - 8, 8), :] + tail
        dx_both[layer] = deps[...].astype(BF)
        ops[layer]["dx0"].send()
        ops[layer]["dx1"].send()
        advance(layer, "go", "gz", "sm")
        for i in range(n_in // 2, n_in):
            du = project(du, i, dx_both[layer, :, pl.ds((i - n_in // 2) * cb, cb)])
        load("h", layer).wait()
        hf = L["h"][...].astype(F32)
        inv = lax.rsqrt(jnp.mean(hf * hf, axis=-1, keepdims=True) + NORM_EPS)
        unit = hf * inv
        vacc[layer, 7:8, pl.ds(0, width)] = jnp.sum(du * unit, axis=0, keepdims=True)
        dn = du * vec[7:8, 0:width]
        dh = g_ref[...].astype(F32) + inv * (dn - unit * jnp.mean(dn * unit, axis=-1, keepdims=True))
        if layer == 1:
            g_both[0] = dh.astype(BF)
            ops[0]["dr"].send()
        else:
            dh_out[...] = dh.astype(BF)
        vecs[layer].begin()

    parts0 = subs[0]["gx"]
    advance(0, "sm")
    grad_gx(0, 0)
    parts0[0].begin()
    advance(0, "vec")
    grad_gx(0, 1)
    parts0[1].begin()
    parts0[2].begin()
    advance(0, "gz", "sm")
    for _ in range(bits - 1):
        parts0[0].advance()
        parts0[2].advance()
        parts0[1].advance()
        advance(0, "sm", "vec")
    left = [s for layer in range(2) for v in subs[layer].values() for s in v]
    while any(s.stage <= s.last for s in left):
        for s in left[::-1]:
            s.advance()
    for k in range(3):
        o_copy(k).wait_send()
    for v in vecs:
        v.drain()
    for s in left:
        s.finish()
    for layer in range(2):
        for g in ops[layer].values():
            g.sent()

    @pl.when(me > 0)
    def _():
        for layer in range(2):
            pltpu.make_async_remote_copy(
                src_ref=rims.at[layer], dst_ref=rimr.at[layer], send_sem=rim_sem.at[layer], recv_sem=rimr_sem.at[layer],
                device_id=(sec, me - 1), device_id_type=MESH).wait_send()

    for cr in carries:
        cr.sent()


def backward(n, rank, cid, tokens, cot, mask, in_own, in_oth, out_own, out_oth, saved, vec2, xp2, dtp2):
    t_len, width = cot.shape[1:]
    inner = out_own.shape[0]
    bits = n.bit_length() - 1
    lead = saved[0]["xi"].shape[0] - t_len
    args = [tokens, cot, mask, in_own, in_oth, out_own, out_oth]
    specs = [ANYSPEC, ANYSPEC, VSPEC] + [ANYSPEC] * 4
    for layer in range(2):
        args += [saved[layer][name] for name in LOADS + ("s", "ut4", "ot4")]
        specs += [ANYSPEC] * (len(LOADS) + 3)
    args += [vec2, xp2, dtp2]
    specs += [VSPEC] * 3
    rows_go, rows_in, rows_sm = inner // n, width // n, inner // n

    def sd(t, *s):
        return jax.ShapeDtypeStruct(s, t)

    outs = [
        sd(BF, t_len, width), sd(F32, rows_in, 2 * inner), sd(F32, rows_go, width), sd(F32, 2, rows_sm, LANES),
        sd(F32, 16, LANES),
    ]
    scratch = []
    for name in LOADS:
        a = saved[0][name]
        scratch += [pltpu.VMEM(a.shape, a.dtype)] * (2 if name in BOTH else 1)
    slots = 4
    scratch += [
        pltpu.VMEM((2, t_len, width), BF), pltpu.VMEM((inner, width), BF), pltpu.VMEM((slots, width, 512), BF),
        pltpu.VMEM((2, BT * N, inner), BF), pltpu.VMEM((2, BT * N, 512), BF), pltpu.VMEM((2, BT * N, 512), BF),
        pltpu.VMEM((N, inner), F32), pltpu.VMEM((t_len, inner), F32),
        pltpu.VMEM((t_len, LANES), F32), pltpu.VMEM((t_len, inner), F32), pltpu.VMEM((2, t_len, inner), BF),
        pltpu.VMEM((2, t_len, inner), BF),
        pltpu.VMEM((rank, inner), F32), pltpu.VMEM((n, max(8, rank * inner // (LANES * n)), LANES), F32),
        pltpu.VMEM((2, 8, inner), F32), pltpu.VMEM((2, 8, inner), F32),
    ]
    scratch += [
        pltpu.VMEM((2, n // 2, rows_in, 4 * t_len), BF), pltpu.VMEM((2, n // 2, rows_go, 4 * t_len), BF),
        pltpu.VMEM((2, 4, t_len, width // 2), BF), pltpu.VMEM((2, 4, t_len, inner // 2), BF),
        pltpu.VMEM((2, 4, t_len, inner // 2), BF),
    ]
    dims = (("go", rows_go, width // 2), ("gz", rows_in, inner // 2), ("gx", rows_in, inner // 2), ("sm", rows_sm, LANES))
    for _ in range(2):
        for name, r, ln in dims:
            count = bits + 1 if name == "sm" else bits - 1
            scratch.append(pltpu.VMEM((2,) * count + (r, ln), BF))
    for _ in range(2):
        for name, r, ln in dims:
            count = bits + 1 if name == "sm" else bits - 1
            scratch += [pltpu.VMEM((2,) * (count - 1 - q) + (r, ln), BF) for q in range(count)]
    scratch += [pltpu.VMEM((r, ln), F32) for _, r, ln in dims]
    scratch += [pltpu.VMEM((2, 8, inner), F32)] * 2 + [pltpu.VMEM((n, 16, LANES), F32)] * 2
    scratch += [
        pltpu.VMEM((2, N, inner), BF), pltpu.VMEM((2, n, N, LANES), BF), pltpu.VMEM((2, n, N, LANES), BF),
        pltpu.VMEM((2, N, inner), BF),
    ]
    nsub = 1 + 2 + 2 + 3
    dma = pltpu.SemaphoreType.DMA
    scratch += [
        dma((len(LOADS), 2)), dma(()), dma((inner // 512,)), dma((slots,)), dma((2,)), dma((2,)), dma((2,)), dma((2, 2)),
        dma((2, 4, 3)), dma((2, 4, 4)), dma((2, nsub, bits + 1)), dma((2, nsub, bits + 1)),
        dma((2, nsub)), dma((2, nsub)), dma((2,)), dma((2,)), dma((2, n)), dma((2, n)), dma((3,)), dma((4,)),
        dma((2, n)), dma((2, n)), dma((2, n)), dma((2, n)),
    ]
    return pl.pallas_call(
        functools.partial(back_kernel, n, rank, {"lead": lead}),
        out_shape=outs,
        in_specs=specs,
        out_specs=[VSPEC] * len(outs),
        scratch_shapes=scratch,
        compiler_params=pltpu.CompilerParams(
            vmem_limit_bytes=63 * MIB, collective_id=cid, has_side_effects=True),
        name="backward",
    )(*args)


def finish_kernel(n, rank, used, hout, dh, g_in, g_out, g_sm, g_vec, *refs):
    o_h, o_dh, o_gain, o_in, o_ck, o_cb, o_xp, o_dt, o_dtb, o_skip, o_out, v0, v1, v2, v3, sems = refs
    moves = ((hout, v0, o_h), (dh, v1, o_dh), (g_in, v2, o_in), (g_out, v3, o_out))
    loads = [pltpu.make_async_copy(a, v, sems.at[i]) for i, (a, v, _) in enumerate(moves)]
    stores = [pltpu.make_async_copy(v, b.at[0], sems.at[i]) for i, (_, v, b) in enumerate(moves)]
    for cp in loads:
        cp.start()
    me = lax.axis_index("ctx")
    inner = o_dt.shape[2]
    o_xp[0] = g_sm[0].T[0:used]
    prow = rank // n
    for t in range(inner // LANES):
        o_dt[0, :, t * LANES : (t + 1) * LANES] = g_sm[1, t * prow : (t + 1) * prow, :]

    def pick(size, body):
        for l0 in range(0, LANES, size):
            @pl.when(lax.rem(me * size, LANES) == l0)
            def _():
                body(slice(l0, l0 + size))

    def vectors(at):
        o_ck[0] = g_vec[0:4, at]
        o_cb[...] = g_vec[4:5, at]
        o_dtb[...] = g_vec[5:6, at]
        o_skip[...] = g_vec[6:7, at]

    def gain(at):
        o_gain[...] = g_vec[15:16, at]

    pick(o_cb.shape[1], vectors)
    pick(o_gain.shape[1], gain)
    for a, b in zip(loads, stores):
        a.wait()
        b.start()
    for cp in stores:
        cp.wait()


def finish(n, rank, used, hout, dh, g_in, g_out, g_sm, g_vec):
    t_len, width = hout.shape
    inner = g_in.shape[1] // 2
    part = inner // n

    def f32(*s):
        return jax.ShapeDtypeStruct((1,) + s, F32)

    whole = jax.ShapeDtypeStruct((1, t_len, width), BF)
    return tuple(pl.pallas_call(
        functools.partial(finish_kernel, n, rank, used),
        out_shape=[
            whole, whole, f32(width // n), f32(*g_in.shape), f32(4, part), f32(part), f32(used, part),
            f32(rank // n, inner), f32(part), f32(part), f32(*g_out.shape),
        ],
        in_specs=[ANYSPEC] * 4 + [VSPEC] * 2,
        out_specs=[ANYSPEC, ANYSPEC, VSPEC, ANYSPEC] + [VSPEC] * 6 + [ANYSPEC],
        scratch_shapes=[pltpu.VMEM(a.shape, a.dtype) for a in (hout, dh, g_in, g_out)] + [pltpu.SemaphoreType.DMA((4,))],
        compiler_params=pltpu.CompilerParams(vmem_limit_bytes=60 * MIB),
        name="finish",
    )(hout, dh, g_in, g_out, g_sm, g_vec))


def on_device(
    tokens, cotangent, bounds, norm_gain, in_proj, conv_kernel, conv_bias, x_proj, dt_proj, dt_bias, skip_gain, out_proj
):
    sec = lax.axis_index("section")
    n = lax.axis_size("ctx")
    me = lax.axis_index("ctx")
    rank = dt_proj.shape[1]
    inner = out_proj.shape[1]
    used = x_proj.shape[2]
    in_own, out_own = in_proj[0], out_proj[0]
    smalls = (norm_gain, conv_kernel[0], conv_bias, dt_bias, skip_gain, x_proj[0].T, dt_proj[0])
    first, saved = forward(n, rank, 1, bounds, tokens, smalls, in_own, out_own)
    in_oth, out_oth, mask, xp2, dtp2, vec2, hmid, hout = first
    saved[0]["h"] = saved[1]["h"] = hmid
    dh, g_in, g_out, g_sm, g_vec = backward(
        n, rank, 2, tokens, cotangent, mask, in_own, in_oth, out_own, out_oth, saved, vec2, xp2, dtp2)
    outs = finish(n, rank, used, hout, dh, g_in, g_out, g_sm, g_vec)
    return outs[:6] + (outs[6].transpose(0, 2, 1),) + outs[7:]


def solution(mesh):
    placed = (
        P(None, "ctx", None), P(None, "ctx", None), P(), P("section", None), P("section"),
        P("section"), P("section", None), P("section"), P("section"),
        P("section", None), P("section", None), P("section"),
    )
    return jax.shard_map(
        on_device,
        mesh=mesh,
        in_specs=placed,
        out_specs=(
            P("section", "ctx", None), P("section", "ctx", None), P("section", "ctx"), P("section", "ctx", None),
            P("section", None, "ctx"), P("section", "ctx"), P("section", "ctx", None), P("section", "ctx", None),
            P("section", "ctx"), P("section", "ctx"), P("section", "ctx", None),
        ),
        check_vma=False,
    )
```

```python
import functools
import math

import jax
import jax.numpy as jnp
from jax import lax
from jax.experimental import pallas as pl
from jax.experimental.pallas import tpu as pltpu
from jax.sharding import PartitionSpec as P

NORM_EPS = 1e-05
LOG2E = math.log2(math.e)
BF = jnp.bfloat16
F32 = jnp.float32
MESH = pl.DeviceIdType.MESH
LANES = 128
BT = 16
N = 16
MIB = 2**20
VSPEC = pl.BlockSpec(memory_space=pltpu.VMEM)
ANYSPEC = pl.BlockSpec(memory_space=pl.ANY)


def dot(a, b):
    return jnp.dot(a, b, preferred_element_type=F32)


def dot_nt(a, b):
    return lax.dot_general(a, b, (((1,), (1,)), ((), ())), preferred_element_type=F32)


def dot_tn(a, b):
    return lax.dot_general(a, b, (((0,), (0,)), ((), ())), preferred_element_type=F32)


def iota(shape, dim):
    return lax.broadcasted_iota(jnp.int32, shape, dim)


def silu_parts(v):
    s = jax.nn.sigmoid(v)
    return v * s, s * (1.0 + v * (1.0 - s))


def coords(n):
    bits = n.bit_length() - 1
    me = lax.axis_index("ctx")
    return bits, me, [lax.rem(me // 2**b, 2) for b in range(bits)]


def unpack_index(k, dims):
    return tuple(lax.rem(k // 2 ** (dims - 1 - d), 2) for d in range(dims))


class Carry:
    def __init__(self, sec, me, n, src, recv, pre, dst, sems, decay, inner):
        self.sec, self.me, self.n = sec, me, n
        self.src, self.recv, self.pre, self.dst, self.decay = src, recv, pre, dst, decay
        self.send1, self.recv1, self.send2, self.recv2 = sems
        self.blocks = min(n, inner // LANES)
        self.stride = n // self.blocks
        self.mine = me // self.stride
        self.reverse = decay is not None

    def when(self, cond, fn):
        if self.stride == 1:
            fn()
        else:
            pl.when(cond)(fn)

    def to(self, k):
        return lax.rem(self.me + k, self.n)

    def frm(self, k):
        return lax.rem(self.me - k + self.n, self.n)

    def lane(self, dev):
        return pl.ds(pl.multiple_of((dev // self.stride) * LANES, LANES), LANES)

    def owns(self, dev):
        return lax.rem(dev, self.stride) == 0

    def first(self, k, dev, slot):
        return pltpu.make_async_remote_copy(
            src_ref=self.src.at[:, self.lane(dev)], dst_ref=self.recv.at[slot],
            send_sem=self.send1.at[k], recv_sem=self.recv1.at[slot],
            device_id=(self.sec, dev), device_id_type=MESH)

    def second(self, k, dev, frm):
        return pltpu.make_async_remote_copy(
            src_ref=self.pre.at[dev], dst_ref=self.dst.at[:, self.lane(frm)],
            send_sem=self.send2.at[k], recv_sem=self.recv2.at[frm],
            device_id=(self.sec, dev), device_id_type=MESH)

    def send(self):
        for k in range(1, self.n):
            self.when(self.owns(self.to(k)), lambda k=k: self.first(k, self.to(k), self.me).start())

    def combine(self):
        def own():
            self.recv[self.me] = self.src[:, self.lane(self.me)]
            for k in range(1, self.n):
                self.first(k, self.frm(k), self.frm(k)).wait_recv()
            run = jnp.zeros((N, LANES), F32)
            for i in range(self.n):
                d = self.n - 1 - i if self.reverse else i
                self.pre[d] = run.astype(BF)
                if self.reverse:
                    dec, st = self.decay[d], self.recv[d]
                else:
                    dec, st = self.recv[d, 0:N, :], self.recv[d, N : 2 * N, :]
                    self.decay_out[d] = dec
                run = dec.astype(F32) * run + st.astype(F32)
            for k in range(1, self.n):
                self.second(k, self.to(k), self.me).start()
            self.dst[:, self.lane(self.me)] = self.pre[self.me]

        self.when(self.owns(self.me), own)

    def get(self):
        for k in range(1, self.n):
            self.when(
                self.owns(self.frm(k)),
                lambda k=k: pltpu.make_async_remote_copy(
                    src_ref=self.pre.at[0], dst_ref=self.dst.at[:, self.lane(self.frm(k))],
                    send_sem=self.send2.at[k], recv_sem=self.recv2.at[self.frm(k)],
                    device_id=(self.sec, self.frm(k)), device_id_type=MESH).wait_recv())

    def sent(self):
        for k in range(1, self.n):
            self.when(self.owns(self.to(k)), lambda k=k: self.first(k, self.to(k), self.me).wait_send())

        def own():
            for k in range(1, self.n):
                self.second(k, self.to(k), self.me).wait_send()

        self.when(self.owns(self.me), own)


SAVED = ("xi", "z", "c", "beta", "ex", "us", "k2", "qb", "y", "proj", "dec", "sb")


def block_diag(projb, first_col):
    pick = (iota((LANES, BT * N), 0) == first_col + iota((LANES, BT * N), 1) % N).astype(F32).astype(BF)
    vals = dot(projb, pick)
    same = iota((BT, BT * N), 0) == iota((BT, BT * N), 1) // N
    return jnp.where(same, vals, 0.0)


def forward_kernel(n, rank, *refs):
    refs = list(refs)

    def take(k):
        out = refs[:k]
        del refs[:k]
        return out

    bounds_ref, tok_ref, gain_ref, ck_ref, cb_ref, dtb_ref, skip_ref, xproj_ref, dtproj_ref, in_own, out_own = take(11)
    in_oth, out_oth, mask_ref, xp2, dtp2, vec2, hmid_ref, hout_ref = take(8)
    hbm = [dict(zip(SAVED + ("s", "ut4", "ot4"), take(len(SAVED) + 3))) for _ in range(2)]
    loc = dict(zip(SAVED, take(len(SAVED))))
    kb_ref, w_in, w_out, stage, rim_ref, hrow, st, sbuf, o_all, ut_s, ot_s = take(11)
    c_src, c_recv, c_pre, c_dst = take(4)
    (sv_sem, wi_sem, wo_sem, sm_s, sm_r, xz_s, xz_r, oth_s, oth_r, rim_s, rim_r, s_sem, op_s, op_r, own_sem,
     c1, c2, c3, c4) = take(19)
    assert not refs
    sec = lax.axis_index("section")
    bits, me, mybit = coords(n)
    x = mybit[0]
    neigh = me + 1 - 2 * x
    t_len, width = hout_ref.shape
    inner = w_out.shape[0]
    used = xproj_ref.shape[0]
    cb = 512
    n_half = inner // cb
    rim = rim_ref.shape[2]
    barrier = pltpu.get_barrier_semaphore()
    for k in range(1, n):
        pl.semaphore_signal(barrier, inc=1, device_id=(sec, lax.rem(me + k, n)), device_id_type=MESH)
    pl.semaphore_signal(barrier, inc=1, device_id=(1 - sec, me), device_id_type=MESH)

    in_order = list(range(n_half, 2 * n_half)) + list(range(n_half))

    def in_copy(k, src):
        at = pl.ds(k * cb, cb)
        return pltpu.make_async_copy(src.at[:, at], w_in.at[:, at], wi_sem.at[k])

    def out_copy(src):
        return pltpu.make_async_copy(src, w_out, wo_sem)

    @pl.when(sec == 0)
    def _():
        for k in in_order:
            in_copy(k, in_own).start()
        out_copy(out_own).start()

    @pl.when(sec == 1)
    def _():
        for k in in_order:
            in_copy(k, in_own).start()

    vec2[sec, 0:4, :] = ck_ref[...].astype(F32)
    vec2[sec, 4:5, :] = cb_ref[...].astype(F32)
    vec2[sec, 5:6, :] = dtb_ref[...].astype(F32)
    vec2[sec, 6:7, :] = skip_ref[...].astype(F32)
    vec2[sec, 7:8, 0:width] = gain_ref[...].astype(F32)
    vec2[sec, 7:8, width:inner] = jnp.zeros((1, inner - width), F32)
    xp2[sec, 0:used, :] = xproj_ref[...]
    xp2[sec, used:LANES, :] = jnp.zeros((LANES - used, inner), BF)
    dtp2[sec, 0:rank, :] = dtproj_ref[...]
    dtp2[sec, rank:LANES, :] = jnp.zeros((LANES - rank, inner), BF)
    row = me * t_len + iota((t_len, LANES), 0)
    col = iota((t_len, LANES), 1)
    start = jnp.zeros((t_len, LANES), jnp.int32)
    for cut in range(1, 7):
        bound = bounds_ref[sec, cut]
        start = jnp.where(row >= bound, bound, start)
    tap = jnp.where(row - 3 + col >= start, 1.0, 0.0)
    keeps = jnp.where(row != start, 1.0, 0.0)
    mask_ref[...] = jnp.where(col < 4, tap, jnp.where(col == 4, keeps, 0.0))

    pl.semaphore_wait(barrier, n)

    def sibling(src, dst, a, b):
        return pltpu.make_async_remote_copy(
            src_ref=src, dst_ref=dst, send_sem=a, recv_sem=b, device_id=(1 - sec, me), device_id_type=MESH)

    small = [sibling(r.at[sec], r.at[sec], sm_s.at[i], sm_r.at[i]) for i, r in enumerate((vec2, xp2, dtp2))]
    for cp in small:
        cp.start()

    def rim_copy(layer, to):
        src = tok_ref.at[:, pl.ds(t_len - rim, rim), :] if layer == 0 else hrow.at[pl.ds(t_len - rim, rim), :]
        dst = rim_ref.at[0] if layer == 0 else rim_ref.at[1, 0]
        return pltpu.make_async_remote_copy(
            src_ref=src, dst_ref=dst, send_sem=rim_s.at[layer], recv_sem=rim_r.at[layer],
            device_id=(sec, to), device_id_type=MESH)

    def has_rim(layer, cond):
        return cond & (sec == 0) if layer == 0 else cond

    def send_rim(layer):
        @pl.when(has_rim(layer, me < n - 1))
        def _():
            rim_copy(layer, me + 1).start()

        @pl.when(me == 0)
        def _():
            if layer == 0:
                rim_ref[0] = jnp.zeros(rim_ref.shape[1:], BF)
            else:
                rim_ref[1, 0] = jnp.zeros(rim_ref.shape[2:], BF)

    def get_rim(layer):
        @pl.when(has_rim(layer, me > 0))
        def _():
            rim_copy(layer, me).wait_recv()

    def oth(k):
        if k == 0:
            return sibling(out_own, out_oth, oth_s.at[0], oth_r.at[0])
        return sibling(in_own, in_oth, oth_s.at[1], oth_r.at[1])

    send_rim(0)

    @pl.when(sec == 1)
    def _():
        oth(1).start()

    def xz_copy(k, rows):
        at = pl.ds((k % n_half) * cb, cb)
        dst = loc["z"] if k >= n_half else loc["xi"]
        return sibling(stage.at[k, pl.ds(0, rows), :], dst.at[:, at], xz_s.at[k], xz_r.at[k])

    def normed(h, layer):
        hf = h.astype(F32)
        inv = lax.rsqrt(jnp.mean(hf * hf, axis=-1, keepdims=True) + NORM_EPS)
        return (hf * inv * vec2[layer, 7:8, 0:width]).astype(BF)

    @pl.when(sec == 0)
    def _():
        both = normed(jnp.concatenate([tok_ref[0], tok_ref[1]], axis=0), 0)
        for k in in_order[:n_half]:
            in_copy(k, in_own).wait()
            r = dot(both, w_in[:, k * cb : (k + 1) * cb])
            loc["z"][:, pl.ds((k - n_half) * cb, cb)] = r[:t_len]
            stage[k, 0:t_len, :] = r[t_len:]
            xz_copy(k, t_len).start()
        get_rim(0)
        edge = normed(jnp.concatenate([rim_ref[0, 0], rim_ref[0, 1]], axis=0), 0)
        rows = jnp.concatenate([edge[:rim], both[:t_len], edge[rim:], both[t_len:]], axis=0)
        for k in in_order[n_half:]:
            in_copy(k, in_own).wait()
            r = dot(rows, w_in[:, k * cb : (k + 1) * cb])
            loc["xi"][:, pl.ds(k * cb, cb)] = r[: rim + t_len]
            stage[k] = r[rim + t_len :]
            xz_copy(k, rim + t_len).start()

    hrow[...] = tok_ref[sec]
    for cp in small:
        cp.wait_recv()

    @pl.when(sec == 1)
    def _():
        for k in in_order:
            xz_copy(k, t_len if k >= n_half else rim + t_len).wait_recv()

    @pl.when(sec == 0)
    def _():
        oth(0).start()

    carries = []
    saved = []

    def keep(name, layer):
        cp = pltpu.make_async_copy(loc[name], hbm[layer][name], sv_sem.at[layer, SAVED.index(name)])
        cp.start()
        saved.append((layer, name))

    def kept(name, layer):
        pltpu.make_async_copy(loc[name], hbm[layer][name], sv_sem.at[layer, SAVED.index(name)]).wait()

    def part_copy(kind, layer, k):
        src = (ut_s, ot_s)[kind].at[layer]
        dst = hbm[layer][("ut4", "ot4")[kind]]

        def slot(i):
            return pl.ds(pl.multiple_of(i * t_len, LANES), t_len)

        mine = 2 * sec + x
        if k == 0:
            s, i, to = src.at[:, x], mine, (1 - sec, me)
        elif k == 1:
            s, i, to = src.at[:, 1 - x], mine, (sec, neigh)
        else:
            i, to = 2 * sec + 1 - x, (1 - sec, me)
            s = dst.at[:, :, slot(i)]
        return pltpu.make_async_remote_copy(
            src_ref=s, dst_ref=dst.at[:, :, slot(i)], send_sem=op_s.at[layer, kind, k], recv_sem=op_r.at[layer, kind, i],
            device_id=to, device_id_type=MESH)

    def part_arrived(kind, layer, i):
        dst = hbm[layer][("ut4", "ot4")[kind]]
        at = pl.ds(pl.multiple_of(i * t_len, LANES), t_len)
        pltpu.make_async_remote_copy(
            src_ref=(ut_s, ot_s)[kind].at[layer, :, 0], dst_ref=dst.at[:, :, at], send_sem=op_s.at[layer, kind, 0],
            recv_sem=op_r.at[layer, kind, i], device_id=(1 - sec, me), device_id_type=MESH).wait_recv()

    def part_own(kind, layer):
        at = pl.ds(pl.multiple_of((2 * sec + x) * t_len, LANES), t_len)
        return pltpu.make_async_copy(
            (ut_s, ot_s)[kind].at[layer, :, x], hbm[layer][("ut4", "ot4")[kind]].at[:, :, at], own_sem.at[layer, kind])

    def part_send(kind, layer):
        part_copy(kind, layer, 0).start()
        part_copy(kind, layer, 1).start()
        part_own(kind, layer).start()

    def part_forward(kind, layer):
        part_arrived(kind, layer, 2 * sec + 1 - x)
        part_copy(kind, layer, 2).start()

    mask = mask_ref[...]
    cols = iota((t_len, LANES), 1)
    keepc = mask[:, 4:5]
    for layer in range(2):
        vec, xp, dtp = vec2.at[layer], xp2.at[layer], dtp2.at[layer]
        u = normed(hrow[...], layer)
        if layer == 1:
            for k in in_order[:n_half]:
                in_copy(k, in_own).wait()
                loc["z"][:, pl.ds((k - n_half) * cb, cb)] = dot(u, w_in[:, k * cb : (k + 1) * cb])
            get_rim(1)
            rows = jnp.concatenate([normed(rim_ref[1, 0], 1), u], axis=0)
            for k in in_order[n_half:]:
                in_copy(k, in_own).wait()
                loc["xi"][:, pl.ds(k * cb, cb)] = dot(rows, w_in[:, k * cb : (k + 1) * cb])
        keep("z", layer)
        keep("xi", layer)
        proj = jnp.zeros((t_len, LANES), F32)
        for k in range(n_half):
            at = pl.ds(k * cb, cb)
            xi = loc["xi"][:, at]
            c = vec[4:5, at] + vec[3:4, at] * xi[rim:]
            for j in range(3):
                c = c + vec[j : j + 1, at] * xi[rim - 3 + j : rim - 3 + j + t_len] * mask[:, j : j + 1]
            loc["c"][:, at] = c
            xc = c * jax.nn.sigmoid(c)
            loc["us"][:, at] = xc
            proj = proj + dot_nt(xc.astype(BF), xp[:, at])
        keep("c", layer)
        projb = jnp.where(cols == rank + 2 * N, keepc, proj).astype(BF)
        loc["proj"][...] = projb
        keep("proj", layer)
        pf = projb.astype(F32)
        ksum = jnp.sum(jnp.where((cols >= rank) & (cols < rank + N), pf * pf, 0.0), axis=-1, keepdims=True)
        for k in range(n_half):
            at = pl.ds(k * cb, cb)
            beta = jax.nn.sigmoid(dot(projb, dtp[:, at]) + vec[5:6, at])
            eps = beta / (1.0 + beta * ksum)
            loc["beta"][:, at] = beta
            loc["us"][:, at] = loc["us"][:, at] * eps
            loc["ex"][:, at] = jnp.where(keepc > 0.0, eps, 1.0)
        for name in ("beta", "us", "ex"):
            keep(name, layer)
        nrow = t_len * N
        sel = (iota((nrow, t_len), 0) // N == iota((nrow, t_len), 1)).astype(F32).astype(BF)
        spread = dot(sel, projb).astype(BF)
        rn = iota((nrow, LANES), 0) % N
        cl = iota((nrow, LANES), 1)
        ones = jnp.ones((LANES, LANES), BF)
        zero = jnp.zeros((nrow, LANES), BF)
        kb = dot(jnp.where(cl == rank + rn, spread, zero), ones)
        kb_ref[...] = kb
        loc["qb"][...] = dot(jnp.where(cl == rank + N + rn, spread, zero), ones)
        keepb = dot(jnp.where(cl == rank + 2 * N, spread, zero), ones)
        loc["k2"][...] = jnp.where(keepb > 0.5, -LOG2E * kb * kb, -1e30)
        keep("qb", layer)
        keep("k2", layer)
        ec = 512
        nt = ec // LANES
        un = 8
        k2_ref, ex_ref, us_ref = loc["k2"], loc["ex"], loc["us"]

        def chunk(ci, carry, layer=layer):
            e0 = pl.multiple_of(ci * ec, ec)

            def body(i, sd):
                s, d = [list(v) for v in sd]
                g0 = pl.multiple_of(i * un, un)
                for t in range(un):
                    r = pl.multiple_of(g0 * N + t * N, N)
                    k2 = k2_ref[pl.ds(r, N), :]
                    kv = kb_ref[pl.ds(r, N), :]
                    for j in range(nt):
                        lane = pl.ds(e0 + LANES * j, LANES)
                        a = jnp.exp2(k2 * ex_ref.at[pl.ds(g0, un), lane][t : t + 1, :])
                        s[j] = a * s[j] + kv * us_ref.at[pl.ds(g0, un), lane][t : t + 1, :]
                        d[j] = a * d[j]
                return tuple(s), tuple(d)

            zeros = tuple(jnp.zeros((N, LANES), F32) for _ in range(nt))
            one = tuple(jnp.ones((N, LANES), F32) for _ in range(nt))
            s, d = lax.fori_loop(0, t_len // un, body, (zeros, one))
            for j in range(nt):
                lane = pl.ds(e0 + LANES * j, LANES)
                c_src[layer, 0:N, lane] = d[j].astype(BF)
                c_src[layer, N : 2 * N, lane] = s[j].astype(BF)
            return carry

        lax.fori_loop(0, inner // ec, chunk, 0)
        cr = Carry(sec, me, n, c_src.at[layer], c_recv.at[layer], c_pre.at[layer], c_dst.at[layer],
                   [s.at[layer] for s in (c1, c2, c3, c4)], None, inner)
        cr.decay_out = loc["dec"]
        carries.append(cr)
        if layer == 1:
            for name in ("dec", "sb", "y"):
                kept(name, 0)
        cr.send()
        ut_s[layer] = u.T.reshape(ut_s.shape[1:])
        cr.combine()
        keep("dec", layer)
        cr.get()
        st[...] = c_dst[layer].astype(F32)
        part_send(0, layer)
        if layer == 0:
            @pl.when(sec == 0)
            def _():
                oth(1).start()

            @pl.when(sec == 1)
            def _():
                oth(0).start()
        else:
            part_forward(1, 0)

        def s_copy(blk, slot, layer=layer):
            return pltpu.make_async_copy(
                sbuf.at[slot], hbm[layer]["s"].at[pl.ds(pl.multiple_of(blk * BT * N, BT * N), BT * N), :], s_sem.at[slot])

        steps = t_len // BT

        def block(i, carry, s_copy=s_copy, vec=vec):
            slot = lax.rem(i, 2)
            rows = pl.ds(pl.multiple_of(i * BT, BT), BT)
            rbase = pl.multiple_of(i * BT * N, BT * N)

            @pl.when(i >= 2)
            def _():
                s_copy(i - 2, slot).wait()

            loc["sb"][rows, :] = st[...].astype(BF)
            qbd = block_diag(loc["proj"][rows, :], rank + N).astype(BF)
            s_ref = sbuf.at[slot]
            for ci in range(inner // ec):
                e0 = ci * ec
                s = [st[:, pl.ds(e0 + LANES * j, LANES)] for j in range(nt)]
                for t in range(BT):
                    krow = pl.ds(pl.multiple_of(rbase + t * N, N), N)
                    k2 = k2_ref[krow, :]
                    kv = kb_ref[krow, :]
                    for j in range(nt):
                        lane = pl.ds(e0 + LANES * j, LANES)
                        a = jnp.exp2(k2 * ex_ref.at[rows, lane][t : t + 1, :])
                        s[j] = a * s[j] + kv * us_ref.at[rows, lane][t : t + 1, :]
                        s_ref[t * N : (t + 1) * N, lane] = s[j].astype(BF)
                for j in range(nt):
                    st[:, pl.ds(e0 + LANES * j, LANES)] = s[j]
                at = pl.ds(e0, ec)
                c = loc["c"][rows, at]
                y = dot(qbd, s_ref[:, at]) + vec[6:7, at] * (c * jax.nn.sigmoid(c))
                loc["y"][rows, at] = y
                z = loc["z"][rows, at]
                o_all[rows, at] = (y * (z * jax.nn.sigmoid(z))).astype(BF)
            s_copy(i, slot).start()
            return carry

        lax.fori_loop(0, steps, block, 0)
        keep("sb", layer)
        keep("y", layer)
        part_forward(0, layer)
        if layer == 0:
            @pl.when(sec == 1)
            def _():
                oth(0).wait_recv()
                out_copy(out_oth).start()

            @pl.when(sec == 0)
            def _():
                oth(1).wait_recv()
                for k in in_order:
                    in_copy(k, in_oth).start()

        out_copy(out_own).wait()
        o = o_all[...]
        hn = (hrow[...].astype(F32) + dot(o, w_out[...])).astype(BF)
        if layer == 0:
            hrow[...] = hn
            hmid_ref[...] = hn
            send_rim(1)

            @pl.when(sec == 0)
            def _():
                oth(0).wait_recv()
                out_copy(out_oth).start()

            @pl.when(sec == 1)
            def _():
                oth(1).wait_recv()
                out_copy(out_own).start()
        else:
            hout_ref[...] = hn
        ot_s[layer] = o.T.reshape(ot_s.shape[1:])
        if layer == 0:
            part_send(1, 0)
        else:
            last_o = pltpu.make_async_copy(ot_s.at[1], hbm[1]["ot4"], own_sem.at[1, 1])
            last_o.start()
        for slot in range(2):
            s_copy(steps - 2 + slot, slot).wait()
        if layer == 0:
            for name in SAVED:
                if name not in ("dec", "sb", "y"):
                    kept(name, 0)

    for name in SAVED:
        kept(name, 1)
    last_o.wait()
    for layer, kind in ((0, 0), (0, 1), (1, 0)):
        part_own(kind, layer).wait()
        for i in range(2):
            part_arrived(kind, layer, 2 * (1 - sec) + (x if i == 0 else 1 - x))
        for k in range(3):
            part_copy(kind, layer, k).wait_send()
    for cp in small:
        cp.wait_send()
    for k in range(2):
        oth(k).wait_send()

    @pl.when(sec == 0)
    def _():
        for k in in_order:
            xz_copy(k, t_len if k >= n_half else rim + t_len).wait_send()

    for layer in range(2):
        @pl.when(has_rim(layer, me < n - 1))
        def _(layer=layer):
            rim_copy(layer, me + 1).wait_send()

    for cr in carries:
        cr.sent()


def forward(n, rank, cid, bounds, tokens, smalls, in_own, out_own):
    t_len, width = tokens.shape[1:]
    inner = out_own.shape[0]
    rim = 16
    rows = t_len * N

    def f32(*s):
        return jax.ShapeDtypeStruct(s, F32)

    def b16(*s):
        return jax.ShapeDtypeStruct(s, BF)

    shapes = {
        "xi": f32(t_len + rim, inner), "z": f32(t_len, inner), "c": f32(t_len, inner), "beta": f32(t_len, inner),
        "ex": f32(t_len, inner), "us": f32(t_len, inner), "k2": f32(rows, LANES), "qb": f32(rows, LANES),
        "y": f32(t_len, inner), "proj": b16(t_len, LANES), "dec": b16(n, N, LANES), "sb": b16(t_len, inner),
    }
    outs = [
        b16(width, 2 * inner), b16(inner, width), f32(t_len, LANES), b16(2, LANES, inner), b16(2, LANES, inner),
        f32(2, 8, inner), b16(t_len, width), b16(t_len, width),
    ]
    specs = [ANYSPEC, ANYSPEC] + [VSPEC] * 6
    for layer in range(2):
        outs += [shapes[name] for name in SAVED]
        outs += [b16(rows, inner), b16(n // 2, width // n, 4 * t_len)]
        outs += [b16(n // 2, 2, inner // n, t_len) if layer else b16(n // 2, inner // n, 4 * t_len)]
        specs += [ANYSPEC] * (len(SAVED) + 3)
    scratch = [pltpu.VMEM(shapes[name].shape, shapes[name].dtype) for name in SAVED]
    scratch += [
        pltpu.VMEM((rows, LANES), F32), pltpu.VMEM((width, 2 * inner), BF), pltpu.VMEM((inner, width), BF),
        pltpu.VMEM((2 * inner // 512, rim + t_len, 512), F32), pltpu.VMEM((2, 2, rim, width), BF),
        pltpu.VMEM((t_len, width), BF), pltpu.VMEM((N, inner), F32), pltpu.VMEM((2, BT * N, inner), BF),
        pltpu.VMEM((t_len, inner), BF), pltpu.VMEM((2, n // 2, 2, width // n, t_len), BF),
        pltpu.VMEM((2, n // 2, 2, inner // n, t_len), BF),
        pltpu.VMEM((2, 2 * N, inner), BF), pltpu.VMEM((2, n, 2 * N, LANES), BF), pltpu.VMEM((2, n, N, LANES), BF),
        pltpu.VMEM((2, N, inner), BF),
    ]
    dma = pltpu.SemaphoreType.DMA
    n_in = 2 * inner // 512
    scratch += [
        dma((2, len(SAVED))), dma((n_in,)), dma(()), dma((3,)), dma((3,)), dma((n_in,)), dma((n_in,)), dma((2,)), dma((2,)),
        dma((2,)), dma((2,)), dma((2,)), dma((2, 2, 3)), dma((2, 2, 4)), dma((2, 2)),
        dma((2, n)), dma((2, n)), dma((2, n)), dma((2, n)),
    ]
    res = pl.pallas_call(
        functools.partial(forward_kernel, n, rank),
        out_shape=outs,
        in_specs=[pl.BlockSpec(memory_space=pltpu.SMEM)] + [VSPEC] * 8 + [ANYSPEC] * 2,
        out_specs=specs,
        scratch_shapes=scratch,
        compiler_params=pltpu.CompilerParams(vmem_limit_bytes=60 * MIB, collective_id=cid, has_side_effects=True),
        name="forward",
    )(bounds, tokens, *smalls, in_own, out_own)
    first, rest = res[:8], res[8:]
    per = len(SAVED) + 3
    saved = [dict(zip(SAVED + ("s", "ut4", "ot4"), rest[i * per : (i + 1) * per])) for i in range(2)]
    return first, saved


class Sub:
    def __init__(self, kit, num, layer, buf, recvs, out, lane0, lanes, steps, held):
        self.kit, self.num, self.layer = kit, num, layer
        self.at = pl.ds(lane0, lanes)
        self.buf, self.recvs, self.out = buf, recvs, out
        self.steps, self.held = steps, held
        self.last = len(steps) - 1
        self.stage = 0

    def bit(self, what):
        return self.kit.sec if what == "s" else self.kit.mybit[what]

    def partner(self, i):
        kit, what = self.kit, self.steps[i]
        if what == "s":
            return (1 - kit.sec, kit.me)
        return (kit.sec, kit.me + 2**what * (1 - 2 * kit.mybit[what]))

    def index(self, i, away):
        done = {w: self.bit(w) for w in self.steps[:i]}
        what = self.steps[i]
        done[what] = 1 - self.bit(what) if away else self.bit(what)
        return tuple(done.get(w, slice(None)) for w in self.held)

    def copy(self, i):
        free = len(self.held) - 1 - i
        return pltpu.make_async_remote_copy(
            src_ref=self.buf.at[self.index(i, True) + (slice(None), self.at)],
            dst_ref=self.recvs[i].at[(slice(None),) * (free + 1) + (self.at,)],
            send_sem=self.kit.ssem.at[self.layer, self.num, i], recv_sem=self.kit.rsem.at[self.layer, self.num, i],
            device_id=self.partner(i), device_id_type=MESH)

    def begin(self):
        self.copy(0).start()

    def place(self, half):
        return self.kit.place[self.out](half, self.at)

    def final(self):
        kit = self.kit
        return pltpu.make_async_remote_copy(
            src_ref=kit.res[self.out].at[:, self.at], dst_ref=self.place(1 - self.layer),
            send_sem=kit.fsem.at[self.layer, self.num], recv_sem=kit.frsem.at[self.layer, self.num],
            device_id=(1 - kit.sec, kit.me), device_id_type=MESH)

    def advance(self):
        i = self.stage
        if i > self.last:
            return
        kit = self.kit
        self.copy(i).wait_recv()
        free = len(self.held) - 1 - i
        fixed = self.index(i, False)
        res = kit.res[self.out]

        def body(k, carry):
            sub = list(unpack_index(k, free))
            src = tuple(sub) + (slice(None), self.at)
            dst = tuple(sub.pop(0) if isinstance(f, slice) else f for f in fixed) + (slice(None), self.at)
            if i == self.last:
                val = self.buf[dst].astype(F32) + self.recvs[i][src].astype(F32)

                @pl.when(kit.sec == self.layer)
                def _():
                    self.place(self.layer)[...] = val

                @pl.when(kit.sec != self.layer)
                def _():
                    res[:, self.at] = val
            else:
                self.buf[dst] = self.buf[dst] + self.recvs[i][src]
            return carry

        if free:
            lax.fori_loop(0, 2**free, body, 0)
        else:
            body(0, 0)
        self.stage = i + 1
        if i < self.last:
            self.copy(i + 1).start()
        else:
            @pl.when(kit.sec != self.layer)
            def _():
                self.final().start()

    def finish(self):
        assert self.stage > self.last
        for i in range(self.last + 1):
            self.copy(i).wait_send()

        @pl.when(self.kit.sec != self.layer)
        def _():
            self.final().wait_send()

        @pl.when(self.kit.sec == self.layer)
        def _():
            self.final().wait_recv()


class VecSum:
    def __init__(self, kit, layer, n, acc, sib, msg, got, out):
        self.kit, self.layer, self.n = kit, layer, n
        self.acc, self.sib, self.msg, self.got, self.out = acc, sib, msg, got, out
        self.stage = 0

    def across(self):
        kit = self.kit
        return pltpu.make_async_remote_copy(
            src_ref=self.acc.at[self.layer], dst_ref=self.sib.at[self.layer],
            send_sem=kit.vsem.at[self.layer], recv_sem=kit.vrsem.at[self.layer],
            device_id=(1 - kit.sec, kit.me), device_id_type=MESH)

    def copy(self, k, dev, slot):
        kit = self.kit
        return pltpu.make_async_remote_copy(
            src_ref=self.msg.at[dev], dst_ref=self.got.at[slot],
            send_sem=kit.v2sem.at[self.layer, k], recv_sem=kit.v2rsem.at[self.layer, slot],
            device_id=(kit.sec, dev), device_id_type=MESH)

    def begin(self):
        @pl.when(self.kit.sec != self.layer)
        def _():
            self.across().start()

    def advance(self):
        kit, n = self.kit, self.n
        if self.stage > 1:
            return
        first = self.stage == 0
        self.stage += 1

        @pl.when(kit.sec == self.layer)
        def _():
            if first:
                self.across().wait_recv()
                total = self.acc[self.layer] + self.sib[self.layer]
                inner = total.shape[1]
                for j in range(n):
                    l0 = (j * (inner // n)) // LANES * LANES
                    g0 = (j * (kit.width // n)) // LANES * LANES
                    self.msg[j, 0:8, :] = total[:, l0 : l0 + LANES]
                    self.msg[j, 8:16, :] = total[:, g0 : g0 + LANES]
                for k in range(1, n):
                    self.copy(k, lax.rem(kit.me + k, n), kit.me).start()
                self.got[kit.me] = self.msg[kit.me]
            else:
                for k in range(1, n):
                    frm = lax.rem(kit.me + k, n)
                    self.copy(k, frm, frm).wait_recv()
                val = self.got[0]
                for j in range(1, n):
                    val = val + self.got[j]
                self.out[...] = val

    def drain(self):
        kit = self.kit
        while self.stage < 2:
            self.advance()

        @pl.when(kit.sec != self.layer)
        def _():
            self.across().wait_send()

        @pl.when(kit.sec == self.layer)
        def _():
            for k in range(1, self.n):
                self.copy(k, lax.rem(kit.me + k, self.n), kit.me).wait_send()


class Kit:
    pass


class Gather:
    def __init__(self, kit, kind, layer, src, dst):
        self.kit, self.kind, self.layer = kit, kind, layer
        self.src, self.dst = src, dst

    def peers(self):
        kit = self.kit
        x = kit.mybit[0]
        other = kit.me + 1 - 2 * x
        return [(1 - kit.sec, kit.me, x), (kit.sec, other, 1 - x), (1 - kit.sec, other, 1 - x)]

    def copy(self, k, slot):
        kit = self.kit
        sec, dev, bit = self.peers()[k]
        return pltpu.make_async_remote_copy(
            src_ref=self.src(sec, bit), dst_ref=self.dst(slot),
            send_sem=kit.osem.at[self.layer, self.kind, k], recv_sem=kit.orsem.at[self.layer, self.kind, slot],
            device_id=(sec, dev), device_id_type=MESH)

    def slot(self, sec, bit):
        return 2 * sec + bit

    def send(self, order=(1, 2, 0)):
        mine = self.slot(self.kit.sec, self.kit.mybit[0])
        for k in order:
            self.copy(k, mine).start()

    def wait(self):
        for k in range(3):
            sec, dev, bit = self.peers()[k]
            self.copy(k, self.slot(sec, bit)).wait_recv()

    def sent(self):
        mine = self.slot(self.kit.sec, self.kit.mybit[0])
        for k in range(3):
            self.copy(k, mine).wait_send()


LOADS = ("h", "xi", "z", "c", "proj", "beta", "ex", "us", "k2", "qb", "sb", "y", "dec")
BOTH = ("h", "proj", "dec", "sb")
BIG = ("go", "gz", "gx")


def lane_parts(lanes):
    unit = lanes // LANES
    a = max(1, (3 * unit) // 4)
    return [(0, a * LANES, 0), (a * LANES, lanes - a * LANES, 1)]


def two_parts(lanes):
    q = lanes // 4
    return [(0, q, 0), (q, q, 1), (2 * q, q, 0), (3 * q, q, 1)]


def bit_orders(bits):
    low = list(range(1, bits))
    return [low, [2, 1] + low[2:]]


def back_kernel(n, rank, shapes, *refs):
    refs = list(refs)

    def take(k):
        out = refs[:k]
        del refs[:k]
        return out

    tokens, cots, mask_ref, in_own, in_oth, out_own, out_oth = take(7)
    hbm = [dict(zip(LOADS + ("s", "ut4", "ot4"), take(len(LOADS) + 3))) for _ in range(2)]
    vec2, xp2, dtp2 = take(3)
    dh_out, gin_out, gout_out, gsm_out, vec_out = take(5)
    loc = {name: (take(2) if name in BOTH else take(1) * 2) for name in LOADS}
    (g_both, w_out, w_in, sbuf, qs2, ws2, bst, deps, dkq, dy_ref, dz_both, dx_both, gdt_ref, gtmp, rims, rimr) = take(16)
    dxc = loc["y"][0]
    ut4, ot4, dr4, dz4, dx4 = take(5)
    kit = Kit()
    bits, me, mybit = coords(n)
    bufs = [dict(zip(BIG + ("sm",), take(4))) for _ in range(2)]
    recvs = []
    for _ in range(2):
        got = {name: take(bits - 1) for name in BIG}
        got["sm"] = take(bits + 1)
        recvs.append(got)
    kit.res = dict(zip(BIG + ("sm",), take(4)))
    vacc, vsib, vmsg, vgot = take(4)
    c_src, c_recv, c_pre, c_dst = take(4)
    (ld_sem, g_sem, wo_sem, wi_sem, s_sem, rim_sem, rimr_sem, own_sem, kit.osem, kit.orsem, kit.ssem, kit.rsem,
     kit.fsem, kit.frsem, kit.vsem, kit.vrsem, kit.v2sem, kit.v2rsem, o_sem, o_rsem, c1, c2, c3, c4) = take(24)
    assert not refs
    sec = lax.axis_index("section")
    kit.sec, kit.me, kit.bits, kit.mybit = sec, me, bits, mybit
    t_len, width = dh_out.shape
    inner = w_out.shape[0]
    cb = 512
    lead = shapes["lead"]

    barrier = pltpu.get_barrier_semaphore()
    for k in range(1, n):
        pl.semaphore_signal(barrier, inc=1, device_id=(sec, lax.rem(me + k, n)), device_id_type=MESH)
    for to in (me, me + 1 - 2 * mybit[0]):
        pl.semaphore_signal(barrier, inc=1, device_id=(1 - sec, to), device_id_type=MESH)

    pos = {name: i for i, name in enumerate(LOADS)}

    def load(name, layer):
        src = tokens.at[sec] if (name, layer) == ("h", 0) else hbm[layer][name]
        return pltpu.make_async_copy(src, loc[name][layer], ld_sem.at[pos[name], layer])

    def out_chunk(k, src):
        at = pl.ds(k * cb, cb)
        return src.at[at, :], w_out.at[at, :], wo_sem.at[k]

    def in_chunk(k, slot, src):
        return src.at[:, pl.ds(k * cb, cb)], w_in.at[slot], wi_sem.at[slot]

    def fetch(layer, chunk, own, oth):
        a, b, s = chunk(own)
        a2 = chunk(oth)[0]

        @pl.when(sec == layer)
        def _():
            pltpu.make_async_copy(a, b, s).start()

        @pl.when(sec != layer)
        def _():
            pltpu.make_async_copy(a2, b, s).start()

    def arrive(chunk, own):
        a, b, s = chunk(own)
        pltpu.make_async_copy(a, b, s).wait()

    n_out = inner // cb
    n_in = 2 * inner // cb
    in_order = list(range(n_in // 2, n_in)) + list(range(n_in // 2))
    slots = w_in.shape[0]

    cot_hbm = cots.at[sec]
    pltpu.make_async_copy(cot_hbm, g_both.at[1], g_sem).start()
    for k in range(n_out):
        fetch(1, lambda src, k=k: out_chunk(k, src), out_own, out_oth)
    for name in ("z", "y", "c", "ex", "k2", "qb", "dec", "proj", "beta", "us", "sb", "xi", "h"):
        load(name, 1).start()
    for name in BOTH:
        load(name, 0).start()
    for i in range(slots):
        fetch(1, lambda src, i=i: in_chunk(in_order[i], i, src), in_own, in_oth)

    half_go = width // 2
    half_in = inner // 2
    kit.place = {
        "go": lambda hf, at: gout_out.at[:, pl.ds(hf * half_go + at.start, at.size)],
        "gz": lambda hf, at: gin_out.at[:, pl.ds(inner + hf * half_in + at.start, at.size)],
        "gx": lambda hf, at: gin_out.at[:, pl.ds(hf * half_in + at.start, at.size)],
        "sm": lambda hf, at: gsm_out.at[hf, :, at],
    }
    gx_parts = two_parts(half_in)
    subs = []
    for layer in range(2):
        mine = {}
        num = 0
        for name, parts in (("go", lane_parts(half_go)), ("gz", lane_parts(half_in)), ("gx", gx_parts)):
            mine[name] = []
            for l0, ln, which in parts:
                mine[name].append(
                    Sub(kit, num, layer, bufs[layer][name], recvs[layer][name], name, l0, ln, bit_orders(bits)[which],
                        list(range(bits - 1, 0, -1))))
                num += 1
        mine["sm"] = [Sub(kit, num, layer, bufs[layer]["sm"], recvs[layer]["sm"], "sm", 0, LANES,
                          ["s", 2, 1, 0] + list(range(3, bits)), ["s"] + list(range(bits - 1, -1, -1)))]
        subs.append(mine)

    def begin(layer, name):
        for s in subs[layer][name]:
            s.begin()

    def advance(layer, *names):
        for name in names:
            if name == "vec":
                vecs[layer].advance()
            else:
                for s in subs[layer][name]:
                    s.advance()

    rows_go = inner // n
    rows_in = width // n
    rows_sm = inner // n
    x = mybit[0]

    def owner(j, count):
        return tuple((j >> (count - 1 - d)) & 1 for d in range(count))

    my_slot = 2 * sec + x

    def operands(layer):
        half = n // 2

        def lanes_of(ref, size):
            return lambda sc, b: ref.at[:, pl.ds(pl.multiple_of(sc * size, LANES), size)]

        def rows_of(ref):
            return lambda slot: ref.at[layer, slot]

        quarter = half_in // 2

        def part_of(ref, p):
            return lambda sc, b: ref.at[:, pl.ds(pl.multiple_of(sc * half_in + p * quarter, LANES), quarter)]

        def part_to(ref, p):
            return lambda slot: ref.at[layer, slot, :, pl.ds(p * quarter, quarter)]

        return {
            "dr": Gather(kit, 0, layer, lanes_of(g_both.at[layer], half_go), rows_of(dr4)),
            "dz": Gather(kit, 1, layer, lanes_of(dz_both.at[layer], half_in), rows_of(dz4)),
            "dx0": Gather(kit, 2, layer, part_of(dx_both.at[layer], 0), part_to(dx4, 0)),
            "dx1": Gather(kit, 3, layer, part_of(dx_both.at[layer], 1), part_to(dx4, 1)),
        }

    ops = [operands(layer) for layer in range(2)]

    def part_load(layer, k):
        src, dst = (("ut4", ut4), ("ot4", ot4))[k]
        return pltpu.make_async_copy(hbm[layer][src], dst.at[layer], own_sem.at[layer, k])

    def own_half(ref, layer, size):
        return ref[layer, :, pl.ds(pl.multiple_of(sec * size, LANES), size)]

    pl.semaphore_wait(barrier, n + 1)
    kit.width = width
    vecs = [VecSum(kit, layer, n, vacc, vsib, vmsg, vgot, vec_out) for layer in range(2)]
    pltpu.make_async_copy(cot_hbm, g_both.at[1], g_sem).wait()
    def slot_at(i):
        return pl.ds(pl.multiple_of(i * t_len, LANES), t_len)

    o_hbm = hbm[1]["ot4"]
    o_own = pltpu.make_async_copy(o_hbm.at[:, x], ot4.at[1, :, :, slot_at(my_slot)], own_sem.at[1, 1])

    def o_copy(k):
        i = my_slot if k < 2 else 2 * sec + 1 - x
        dst = ot4.at[1, :, :, slot_at(i)]
        src = (o_hbm.at[:, 1 - x], o_hbm.at[:, x], dst)[k]
        return pltpu.make_async_remote_copy(
            src_ref=src, dst_ref=dst, send_sem=o_sem.at[k], recv_sem=o_rsem.at[i],
            device_id=(sec, me + 1 - 2 * x) if k == 0 else (1 - sec, me), device_id_type=MESH)

    def o_wait(i):
        dst = ot4.at[1, :, :, slot_at(i)]
        pltpu.make_async_remote_copy(
            src_ref=dst, dst_ref=dst, send_sem=o_sem.at[0], recv_sem=o_rsem.at[i],
            device_id=(1 - sec, me), device_id_type=MESH).wait_recv()

    o_copy(0).start()
    o_copy(1).start()
    o_own.start()
    ops[1]["dr"].send()
    for layer, k in ((1, 0), (0, 1), (0, 0)):
        part_load(layer, k).start()

    def grad_go(layer):
        ops[layer]["dr"].wait()
        if layer == 1:
            o_own.wait()
            o_wait(2 * (1 - sec) + x)
            o_wait(2 * (1 - sec) + 1 - x)
        else:
            part_load(layer, 1).wait()
        dr4[layer, my_slot] = own_half(g_both, layer, half_go)
        rhs = dr4[layer].reshape(4 * t_len, half_go)
        for j in range(n // 2):
            bufs[layer]["go"][owner(j, bits - 1)] = dot(ot4[layer, j], rhs).astype(BF)

    def grad_in(name, layer, four, l0):
        lhs = ut4[layer].reshape(n // 2 * rows_in, 4 * t_len)
        at = pl.ds(l0, cb)
        g = dot(lhs, four[layer, :, :, at].reshape(4 * t_len, cb)).astype(BF)
        for j in range(n // 2):
            bufs[layer][name][owner(j, bits - 1) + (slice(None), at)] = g[j * rows_in : (j + 1) * rows_in]

    def grad_gz(layer):
        ops[layer]["dz"].wait()
        part_load(layer, 0).wait()
        dz4[layer, my_slot] = own_half(dz_both, layer, half_in)
        for l0 in range(0, half_in, cb):
            grad_in("gz", layer, dz4, l0)
        begin(layer, "gz")

    def grad_gx(layer, p):
        if p == 0:
            dx4[layer, my_slot] = own_half(dx_both, layer, half_in)
        ops[layer]["dx0" if p == 0 else "dx1"].wait()
        for l0 in range(p * half_in // 2, (p + 1) * half_in // 2, cb):
            grad_in("gx", layer, dx4, l0)

    carries = []
    for layer in (1, 0):
        g_ref = g_both.at[layer]
        dz_ref = dz_both.at[layer]
        L = {name: loc[name][layer] for name in LOADS}
        vec, xp, dtp = vec2.at[layer], xp2.at[layer], dtp2.at[layer]
        vacc[layer] = jnp.zeros(vacc.shape[1:], F32)
        for name in ("z", "y", "c"):
            load(name, layer).wait()
        dr = g_ref[...]
        for k in range(n_out):
            at = pl.ds(k * cb, cb)
            arrive(lambda src, k=k: out_chunk(k, src), out_own)
            do = dot_nt(dr, w_out[at, :])
            act, der = silu_parts(L["z"][:, at])
            dy = do * act
            dy_ref[:, at] = dy
            dz_ref[:, at] = (do * L["y"][:, at] * der).astype(BF)
            c = L["c"][:, at]
            vacc[layer, 6:7, at] = jnp.sum(dy * (c * jax.nn.sigmoid(c)), axis=0, keepdims=True)
        if layer == 1:
            for k in range(n_out):
                fetch(0, lambda src, k=k: out_chunk(k, src), out_own, out_oth)
            load("z", 0).start()
        for name in ("ex", "k2", "qb"):
            load(name, layer).wait()
        k2_ref, qb_ref, ex_ref = L["k2"], L["qb"], L["ex"]
        ec = 512
        nt = ec // LANES
        un = 8

        def chunk(ci, carry, k2_ref=k2_ref, qb_ref=qb_ref, ex_ref=ex_ref, layer=layer):
            e0 = pl.multiple_of(ci * ec, ec)

            def body(i, b):
                b = list(b)
                g0 = pl.multiple_of((t_len // un - 1 - i) * un, un)
                for t in range(un - 1, -1, -1):
                    r = pl.multiple_of(g0 * N + t * N, N)
                    k2 = k2_ref[pl.ds(r, N), :]
                    qv = qb_ref[pl.ds(r, N), :]
                    for j in range(nt):
                        lane = pl.ds(e0 + LANES * j, LANES)
                        a = jnp.exp2(k2 * ex_ref.at[pl.ds(g0, un), lane][t : t + 1, :])
                        b[j] = a * (qv * dy_ref.at[pl.ds(g0, un), lane][t : t + 1, :] + b[j])
                return tuple(b)

            b = lax.fori_loop(0, t_len // un, body, tuple(jnp.zeros((N, LANES), F32) for _ in range(nt)))
            for j in range(nt):
                c_src[layer, :, pl.ds(e0 + LANES * j, LANES)] = b[j].astype(BF)
            return carry

        lax.fori_loop(0, inner // ec, chunk, 0)
        load("dec", layer).wait()
        cr = Carry(sec, me, n, c_src.at[layer], c_recv.at[layer], c_pre.at[layer], c_dst.at[layer],
                   [s.at[layer] for s in (c1, c2, c3, c4)], L["dec"], inner)
        carries.append(cr)
        cr.send()
        if layer == 1:
            o_wait(2 * sec + 1 - x)
            o_copy(2).start()
        else:
            grad_go(0)
        cr.combine()
        if layer == 0:
            grad_gx(1, 0)
            grad_gx(1, 1)
        steps = t_len // BT

        def s_copy(blk, slot, layer=layer):
            return pltpu.make_async_copy(
                hbm[layer]["s"].at[pl.ds(pl.multiple_of(blk * BT * N, BT * N), BT * N), :], sbuf.at[slot],
                s_sem.at[slot])

        s_copy(steps - 1, 0).start()
        for name in ("proj", "beta", "us", "sb"):
            load(name, layer).wait()
        cr.get()
        bst[...] = c_dst[layer].astype(F32)
        if layer == 0:
            begin(1, "gx")
            advance(1, "go", "gz", "vec", "sm")
        ops[layer]["dz"].send()
        if layer == 1:
            grad_go(1)
        begin(layer, "go")

        def block(i, carry, L=L, vec=vec, s_copy=s_copy, dy_ref=dy_ref):
            blk = steps - 1 - i
            slot = lax.rem(i, 2)
            base = pl.multiple_of(blk * BT, BT)
            rows = pl.ds(base, BT)
            rbase = pl.multiple_of(blk * BT * N, BT * N)

            @pl.when(i + 1 < steps)
            def _():
                s_copy(blk - 1, 1 - slot).start()

            s_copy(blk, slot).wait()
            projb = L["proj"][rows, :]
            pf = projb.astype(F32)
            cols = iota((BT, LANES), 1)
            is_k = (cols >= rank) & (cols < rank + N)
            ksum = jnp.sum(jnp.where(is_k, pf * pf, 0.0), axis=-1, keepdims=True)
            kbd = block_diag(projb, rank)
            k2bd = (kbd * kbd).astype(BF)
            kbd = kbd.astype(BF)
            r1 = jnp.zeros((BT, BT * N), F32)
            r2 = jnp.zeros((BT, BT * N), F32)
            r3 = jnp.zeros((BT, BT * N), F32)
            s_blk = sbuf.at[slot]
            for ci in range(inner // ec):
                e0 = ci * ec
                qs, ws = qs2.at[ci % 2], ws2.at[ci % 2]
                b = [bst[:, pl.ds(e0 + LANES * j, LANES)] for j in range(nt)]
                for t in range(BT - 1, -1, -1):
                    row = slice(t * N, (t + 1) * N)
                    krow = pl.ds(pl.multiple_of(rbase + t * N, N), N)
                    k2 = L["k2"][krow, :]
                    qv = L["qb"][krow, :]
                    for j in range(nt):
                        lane = pl.ds(e0 + LANES * j, LANES)
                        a = jnp.exp2(k2 * L["ex"].at[rows, lane][t : t + 1, :])
                        q = qv * dy_ref.at[rows, lane][t : t + 1, :] + b[j]
                        b[j] = a * q
                        prev = s_blk[(t - 1) * N : t * N, lane] if t > 0 else L["sb"][rows, lane]
                        qs[row, LANES * j : LANES * (j + 1)] = q.astype(BF)
                        ws[row, LANES * j : LANES * (j + 1)] = (b[j] * prev.astype(F32)).astype(BF)
                for j in range(nt):
                    bst[:, pl.ds(e0 + LANES * j, LANES)] = b[j]
                at = pl.ds(e0, ec)
                p1 = dot(kbd, qs[...])
                p2 = dot(k2bd, ws[...])
                c = L["c"][rows, at]
                beta = L["beta"][rows, at]
                eps = beta / (1.0 + beta * ksum)
                dy = dy_ref[rows, at]
                deps[rows, at] = (c * jax.nn.sigmoid(c)) * p1 - p2
                dxc[rows, at] = dy * vec[6:7, at] + eps * p1
                r1 = r1 + dot_nt(L["us"][rows, at].astype(BF), qs[...])
                r2 = r2 + dot_nt(eps.astype(BF), ws[...])
                r3 = r3 + dot_nt(dy.astype(BF), s_blk[:, at])
            same = iota((BT, BT * N), 0) == iota((BT, BT * N), 1) // N
            gather_k = (iota((BT * N, LANES), 1) == rank + iota((BT * N, LANES), 0) % N).astype(F32)
            gather_q = (iota((BT * N, LANES), 1) == rank + N + iota((BT * N, LANES), 0) % N).astype(F32)

            def pick(r, g):
                return jnp.dot(
                    jnp.where(same, r, 0.0), g, precision=lax.Precision.HIGHEST, preferred_element_type=F32)

            dkq[rows, :] = pick(r1, gather_k) - 2.0 * pf * pick(r2, gather_k) + pick(r3, gather_q)
            return carry

        def tick(k, layer=layer):
            if layer == 1:
                if k == 2:
                    grad_gz(1)
                return
            if k == 1:
                advance(1, "sm")
            if k == 2:
                grad_gz(0)
            if k == 3:
                advance(1, "gz", "gx", "sm", "vec")

        def block_and_tick(i, carry):
            block(i, carry)
            for k in range(4):
                @pl.when(i == (k + 1) * steps // 4 - 1)
                def _(k=k):
                    tick(k)

            return carry

        lax.fori_loop(0, steps, block_and_tick, 0)
        if layer == 1:
            for name in ("k2", "qb", "ex", "us"):
                load(name, 0).start()
        load("xi", layer).wait()
        projw = L["proj"][...]
        pw = projw.astype(F32)
        colw = iota((t_len, LANES), 1)
        kall = jnp.where((colw >= rank) & (colw < rank + N), pw, 0.0)
        ks = jnp.sum(kall * kall, axis=-1, keepdims=True)
        tc = 256
        def first(k, carry, L=L, dtp=dtp, layer=layer, projw=projw, ks=ks):
            dkc, ddt = carry
            at = pl.ds(pl.multiple_of(k * tc, tc), tc)
            beta = L["beta"][:, at]
            inv = 1.0 / (1.0 + beta * ks)
            dq = deps[:, at] * (inv * inv)
            dkc = dkc + jnp.sum(dq * beta * beta, axis=-1, keepdims=True)
            dp = (dq * beta * (1.0 - beta)).astype(BF)
            vacc[layer, 5:6, at] = jnp.sum(dp.astype(F32), axis=0, keepdims=True)
            gdt_ref[:, at] = dot_tn(projw, dp)[:rank]
            ddt = ddt + dot_nt(dp, dtp[:, at])
            return dkc, ddt

        dkc, ddt = lax.fori_loop(
            0, inner // tc, first, (jnp.zeros((t_len, 1), F32), jnp.zeros((t_len, LANES), F32)))
        dproj = (jnp.where(colw < rank, ddt, dkq[...]) - 2.0 * kall * dkc).astype(BF)
        mask = mask_ref[...]

        def rim_copy(to, layer=layer):
            return pltpu.make_async_remote_copy(
                src_ref=rims.at[layer], dst_ref=rimr.at[layer], send_sem=rim_sem.at[layer], recv_sem=rimr_sem.at[layer],
                device_id=(sec, to), device_id_type=MESH)

        for k in range(n_out):
            at = pl.ds(k * cb, cb)
            der = silu_parts(L["c"][0:BT, at])[1]
            dc = (dxc[0:BT, at] + dot(dproj[0:BT], xp[:, at])) * der
            rim = jnp.zeros((8, cb), F32)
            for j in range(3):
                m = dc[0:8] * mask[0:8, j : j + 1] * vec[j : j + 1, at]
                rim = rim + jnp.concatenate([jnp.zeros((8, cb), F32), m], axis=0)[8 - j : 16 - j]
            rims[layer, :, at] = jnp.where(iota((8, cb), 0) < 3, rim, 0.0)

        @pl.when(me > 0)
        def _():
            rim_copy(me - 1).start()

        @pl.when(me == n - 1)
        def _():
            rimr[layer] = jnp.zeros(rimr.shape[1:], F32)

        per_part = half_in // 2 // tc

        def add_rim(p, layer=layer):
            for hf in range(2):
                at = pl.ds(hf * half_in + p * half_in // 2, half_in // 2)
                rows = pl.ds(t_len - BT, BT)
                edge = jnp.concatenate([jnp.zeros((BT - 3, half_in // 2), F32), rimr[layer, 0:3, at]], axis=0)
                dx_both[layer, rows, at] = (deps[rows, at] + edge).astype(BF)
            ops[layer]["dx0" if p == 0 else "dx1"].send()

        def second(i, carry, L=L, xp=xp, layer=layer, dproj=dproj, ck_ref=vec):
            p, left = i // (2 * per_part), lax.rem(i, 2 * per_part)
            k = left // per_part * (half_in // tc) + p * per_part + lax.rem(left, per_part)
            at = pl.ds(pl.multiple_of(k * tc, tc), tc)
            c = L["c"][:, at]
            act, der = silu_parts(c)
            gxp = dot_tn(act.astype(BF), dproj).astype(BF)
            for r in range(tc // rows_sm):
                j = k * (tc // rows_sm) + r
                bufs[layer]["sm"][(0,) + unpack_index(j, bits)] = gxp[r * rows_sm : (r + 1) * rows_sm]
            dc = (dxc[:, at] + dot(dproj, xp[:, at])) * der
            vacc[layer, 4:5, at] = jnp.sum(dc, axis=0, keepdims=True)
            xi = L["xi"][:, at]
            pad = jnp.zeros((8, tc), F32)
            dxi = ck_ref[3:4, at] * dc
            vacc[layer, 3:4, at] = jnp.sum(dc * xi[lead:], axis=0, keepdims=True)
            for j in range(3):
                m = dc * mask[:, j : j + 1]
                vacc[layer, j : j + 1, at] = jnp.sum(m * xi[lead - 3 + j : lead - 3 + j + t_len], axis=0, keepdims=True)
                ext = jnp.concatenate([m * ck_ref[j : j + 1, at], pad], axis=0)
                dxi = dxi + ext[3 - j : 3 - j + t_len]
            dx_both[layer, :, at] = dxi.astype(BF)
            deps[pl.ds(t_len - BT, BT), at] = dxi[t_len - BT :]

            @pl.when(i == 2 * per_part - 1)
            def _():
                @pl.when(me < n - 1)
                def _():
                    rim_copy(me).wait_recv()

                add_rim(0)

            return carry

        lax.fori_loop(0, inner // tc, second, 0)
        add_rim(1)
        if layer == 1:
            for name in ("c", "beta", "xi", "y"):
                load(name, 0).start()
        prow = rank // n
        for j in range(n):
            for t in range(inner // LANES):
                gtmp[j, t * prow : (t + 1) * prow, :] = gdt_ref[j * prow : (j + 1) * prow, t * LANES : (t + 1) * LANES]
        drow = prow * (inner // LANES)
        for j in range(n):
            bufs[layer]["sm"][(1,) + owner(j, bits) + (slice(0, drow),)] = gtmp[j, 0:drow].astype(BF)
        begin(layer, "sm")
        advance(layer, "go")
        du = jnp.zeros((t_len, width), F32)

        def project(du, i, g, layer=layer):
            slot = i % slots
            arrive(lambda src: in_chunk(in_order[i], slot, src), in_own)
            du = du + dot_nt(g, w_in[slot])
            if i + slots < n_in:
                fetch(layer, lambda src: in_chunk(in_order[i + slots], slot, src), in_own, in_oth)
            elif layer == 1:
                fetch(0, lambda src: in_chunk(in_order[i + slots - n_in], slot, src), in_own, in_oth)
            return du

        for i in range(n_in // 2):
            du = project(du, i, dz_ref[:, pl.ds(i * cb, cb)])

        if layer == 0:
            advance(1, "gx", "sm")
        advance(layer, "gz", "sm")
        for i in range(n_in // 2, n_in):
            du = project(du, i, dx_both[layer, :, pl.ds((i - n_in // 2) * cb, cb)])
        advance(layer, "go")
        if layer == 0:
            advance(1, "gx")
            advance(0, "gz", "sm")
        load("h", layer).wait()
        hf = L["h"][...].astype(F32)
        inv = lax.rsqrt(jnp.mean(hf * hf, axis=-1, keepdims=True) + NORM_EPS)
        unit = hf * inv
        vacc[layer, 7:8, pl.ds(0, width)] = jnp.sum(du * unit, axis=0, keepdims=True)
        dn = du * vec[7:8, 0:width]
        dh = g_ref[...].astype(F32) + inv * (dn - unit * jnp.mean(dn * unit, axis=-1, keepdims=True))
        if layer == 1:
            g_both[0] = dh.astype(BF)
            ops[0]["dr"].send()
        else:
            dh_out[...] = dh.astype(BF)
        vecs[layer].begin()

    parts0 = subs[0]["gx"]
    half0 = len(parts0) // 2
    grad_gx(0, 0)
    for s in parts0[:half0]:
        s.begin()
    advance(0, "vec", "sm")
    grad_gx(0, 1)
    for s in parts0[half0:]:
        s.begin()
    advance(0, "go", "gz")
    for _ in range(bits - 1):
        for s in parts0[:half0]:
            s.advance()
        advance(0, "sm", "go", "gz")
        for s in parts0[half0:]:
            s.advance()
        advance(0, "vec")
    left = [s for layer in range(2) for v in subs[layer].values() for s in v]
    while any(s.stage <= s.last for s in left):
        for s in left[::-1]:
            s.advance()
    for k in range(3):
        o_copy(k).wait_send()
    for v in vecs:
        v.drain()
    for s in left:
        s.finish()
    for layer in range(2):
        for g in ops[layer].values():
            g.sent()

    @pl.when(me > 0)
    def _():
        for layer in range(2):
            pltpu.make_async_remote_copy(
                src_ref=rims.at[layer], dst_ref=rimr.at[layer], send_sem=rim_sem.at[layer], recv_sem=rimr_sem.at[layer],
                device_id=(sec, me - 1), device_id_type=MESH).wait_send()

    for cr in carries:
        cr.sent()


def backward(n, rank, cid, tokens, cot, mask, in_own, in_oth, out_own, out_oth, saved, vec2, xp2, dtp2):
    t_len, width = cot.shape[1:]
    inner = out_own.shape[0]
    bits = n.bit_length() - 1
    lead = saved[0]["xi"].shape[0] - t_len
    args = [tokens, cot, mask, in_own, in_oth, out_own, out_oth]
    specs = [ANYSPEC, ANYSPEC, VSPEC] + [ANYSPEC] * 4
    for layer in range(2):
        args += [saved[layer][name] for name in LOADS + ("s", "ut4", "ot4")]
        specs += [ANYSPEC] * (len(LOADS) + 3)
    args += [vec2, xp2, dtp2]
    specs += [VSPEC] * 3
    rows_go, rows_in, rows_sm = inner // n, width // n, inner // n

    def sd(t, *s):
        return jax.ShapeDtypeStruct(s, t)

    outs = [
        sd(BF, t_len, width), sd(F32, rows_in, 2 * inner), sd(F32, rows_go, width), sd(F32, 2, rows_sm, LANES),
        sd(F32, 16, LANES),
    ]
    scratch = []
    for name in LOADS:
        a = saved[0][name]
        scratch += [pltpu.VMEM(a.shape, a.dtype)] * (2 if name in BOTH else 1)
    slots = 4
    scratch += [
        pltpu.VMEM((2, t_len, width), BF), pltpu.VMEM((inner, width), BF), pltpu.VMEM((slots, width, 512), BF),
        pltpu.VMEM((2, BT * N, inner), BF), pltpu.VMEM((2, BT * N, 512), BF), pltpu.VMEM((2, BT * N, 512), BF),
        pltpu.VMEM((N, inner), F32), pltpu.VMEM((t_len, inner), F32),
        pltpu.VMEM((t_len, LANES), F32), pltpu.VMEM((t_len, inner), F32), pltpu.VMEM((2, t_len, inner), BF),
        pltpu.VMEM((2, t_len, inner), BF),
        pltpu.VMEM((rank, inner), F32), pltpu.VMEM((n, max(8, rank * inner // (LANES * n)), LANES), F32),
        pltpu.VMEM((2, 8, inner), F32), pltpu.VMEM((2, 8, inner), F32),
    ]
    scratch += [
        pltpu.VMEM((2, n // 2, rows_in, 4 * t_len), BF), pltpu.VMEM((2, n // 2, rows_go, 4 * t_len), BF),
        pltpu.VMEM((2, 4, t_len, width // 2), BF), pltpu.VMEM((2, 4, t_len, inner // 2), BF),
        pltpu.VMEM((2, 4, t_len, inner // 2), BF),
    ]
    dims = (("go", rows_go, width // 2), ("gz", rows_in, inner // 2), ("gx", rows_in, inner // 2), ("sm", rows_sm, LANES))
    for _ in range(2):
        for name, r, ln in dims:
            count = bits + 1 if name == "sm" else bits - 1
            scratch.append(pltpu.VMEM((2,) * count + (r, ln), BF))
    for _ in range(2):
        for name, r, ln in dims:
            count = bits + 1 if name == "sm" else bits - 1
            scratch += [pltpu.VMEM((2,) * (count - 1 - q) + (r, ln), BF) for q in range(count)]
    scratch += [pltpu.VMEM((r, ln), F32) for _, r, ln in dims]
    scratch += [pltpu.VMEM((2, 8, inner), F32)] * 2 + [pltpu.VMEM((n, 16, LANES), F32)] * 2
    scratch += [
        pltpu.VMEM((2, N, inner), BF), pltpu.VMEM((2, n, N, LANES), BF), pltpu.VMEM((2, n, N, LANES), BF),
        pltpu.VMEM((2, N, inner), BF),
    ]
    nsub = 1 + 2 + 2 + 4
    dma = pltpu.SemaphoreType.DMA
    scratch += [
        dma((len(LOADS), 2)), dma(()), dma((inner // 512,)), dma((slots,)), dma((2,)), dma((2,)), dma((2,)), dma((2, 2)),
        dma((2, 4, 3)), dma((2, 4, 4)), dma((2, nsub, bits + 1)), dma((2, nsub, bits + 1)),
        dma((2, nsub)), dma((2, nsub)), dma((2,)), dma((2,)), dma((2, n)), dma((2, n)), dma((3,)), dma((4,)),
        dma((2, n)), dma((2, n)), dma((2, n)), dma((2, n)),
    ]
    return pl.pallas_call(
        functools.partial(back_kernel, n, rank, {"lead": lead}),
        out_shape=outs,
        in_specs=specs,
        out_specs=[VSPEC] * len(outs),
        scratch_shapes=scratch,
        compiler_params=pltpu.CompilerParams(
            vmem_limit_bytes=63 * MIB, collective_id=cid, has_side_effects=True),
        name="backward",
    )(*args)


def finish_kernel(n, rank, used, hout, dh, g_in, g_out, g_sm, g_vec, *refs):
    o_h, o_dh, o_gain, o_in, o_ck, o_cb, o_xp, o_dt, o_dtb, o_skip, o_out, v0, v1, v2, v3, sems = refs
    moves = ((hout, v0, o_h), (dh, v1, o_dh), (g_in, v2, o_in), (g_out, v3, o_out))
    loads = [pltpu.make_async_copy(a, v, sems.at[i]) for i, (a, v, _) in enumerate(moves)]
    stores = [pltpu.make_async_copy(v, b.at[0], sems.at[i]) for i, (_, v, b) in enumerate(moves)]
    for cp in loads:
        cp.start()
    me = lax.axis_index("ctx")
    inner = o_dt.shape[2]
    o_xp[0] = g_sm[0].T[0:used]
    prow = rank // n
    for t in range(inner // LANES):
        o_dt[0, :, t * LANES : (t + 1) * LANES] = g_sm[1, t * prow : (t + 1) * prow, :]

    def pick(size, body):
        for l0 in range(0, LANES, size):
            @pl.when(lax.rem(me * size, LANES) == l0)
            def _():
                body(slice(l0, l0 + size))

    def vectors(at):
        o_ck[0] = g_vec[0:4, at]
        o_cb[...] = g_vec[4:5, at]
        o_dtb[...] = g_vec[5:6, at]
        o_skip[...] = g_vec[6:7, at]

    def gain(at):
        o_gain[...] = g_vec[15:16, at]

    pick(o_cb.shape[1], vectors)
    pick(o_gain.shape[1], gain)
    for a, b in zip(loads, stores):
        a.wait()
        b.start()
    for cp in stores:
        cp.wait()


def finish(n, rank, used, hout, dh, g_in, g_out, g_sm, g_vec):
    t_len, width = hout.shape
    inner = g_in.shape[1] // 2
    part = inner // n

    def f32(*s):
        return jax.ShapeDtypeStruct((1,) + s, F32)

    whole = jax.ShapeDtypeStruct((1, t_len, width), BF)
    return tuple(pl.pallas_call(
        functools.partial(finish_kernel, n, rank, used),
        out_shape=[
            whole, whole, f32(width // n), f32(*g_in.shape), f32(4, part), f32(part), f32(used, part),
            f32(rank // n, inner), f32(part), f32(part), f32(*g_out.shape),
        ],
        in_specs=[ANYSPEC] * 4 + [VSPEC] * 2,
        out_specs=[ANYSPEC, ANYSPEC, VSPEC, ANYSPEC] + [VSPEC] * 6 + [ANYSPEC],
        scratch_shapes=[pltpu.VMEM(a.shape, a.dtype) for a in (hout, dh, g_in, g_out)] + [pltpu.SemaphoreType.DMA((4,))],
        compiler_params=pltpu.CompilerParams(vmem_limit_bytes=60 * MIB),
        name="finish",
    )(hout, dh, g_in, g_out, g_sm, g_vec))


def on_device(
    tokens, cotangent, bounds, norm_gain, in_proj, conv_kernel, conv_bias, x_proj, dt_proj, dt_bias, skip_gain, out_proj
):
    sec = lax.axis_index("section")
    n = lax.axis_size("ctx")
    me = lax.axis_index("ctx")
    rank = dt_proj.shape[1]
    inner = out_proj.shape[1]
    used = x_proj.shape[2]
    in_own, out_own = in_proj[0], out_proj[0]
    smalls = (norm_gain, conv_kernel[0], conv_bias, dt_bias, skip_gain, x_proj[0].T, dt_proj[0])
    first, saved = forward(n, rank, 1, bounds, tokens, smalls, in_own, out_own)
    in_oth, out_oth, mask, xp2, dtp2, vec2, hmid, hout = first
    saved[0]["h"] = saved[1]["h"] = hmid
    dh, g_in, g_out, g_sm, g_vec = backward(
        n, rank, 2, tokens, cotangent, mask, in_own, in_oth, out_own, out_oth, saved, vec2, xp2, dtp2)
    outs = finish(n, rank, used, hout, dh, g_in, g_out, g_sm, g_vec)
    return outs[:6] + (outs[6].transpose(0, 2, 1),) + outs[7:]


def solution(mesh):
    placed = (
        P(None, "ctx", None), P(None, "ctx", None), P(), P("section", None), P("section"),
        P("section"), P("section", None), P("section"), P("section"),
        P("section", None), P("section", None), P("section"),
    )
    return jax.shard_map(
        on_device,
        mesh=mesh,
        in_specs=placed,
        out_specs=(
            P("section", "ctx", None), P("section", "ctx", None), P("section", "ctx"), P("section", "ctx", None),
            P("section", None, "ctx"), P("section", "ctx"), P("section", "ctx", None), P("section", "ctx", None),
            P("section", "ctx"), P("section", "ctx"), P("section", "ctx", None),
        ),
        check_vma=False,
    )
```

```python
import functools
import math

import jax
import jax.numpy as jnp
from jax import lax
from jax.experimental import pallas as pl
from jax.experimental.pallas import tpu as pltpu
from jax.sharding import PartitionSpec as P

NORM_EPS = 1e-05
LOG2E = math.log2(math.e)
BF = jnp.bfloat16
F32 = jnp.float32
MESH = pl.DeviceIdType.MESH
LANES = 128
BT = 16
N = 16
MIB = 2**20
VSPEC = pl.BlockSpec(memory_space=pltpu.VMEM)
ANYSPEC = pl.BlockSpec(memory_space=pl.ANY)


def dot(a, b):
    return jnp.dot(a, b, preferred_element_type=F32)


def dot_nt(a, b):
    return lax.dot_general(a, b, (((1,), (1,)), ((), ())), preferred_element_type=F32)


def dot_tn(a, b):
    return lax.dot_general(a, b, (((0,), (0,)), ((), ())), preferred_element_type=F32)


def iota(shape, dim):
    return lax.broadcasted_iota(jnp.int32, shape, dim)


def silu_parts(v):
    s = jax.nn.sigmoid(v)
    return v * s, s * (1.0 + v * (1.0 - s))


def coords(n):
    bits = n.bit_length() - 1
    me = lax.axis_index("ctx")
    return bits, me, [lax.rem(me // 2**b, 2) for b in range(bits)]


def unpack_index(k, dims):
    return tuple(lax.rem(k // 2 ** (dims - 1 - d), 2) for d in range(dims))


class Carry:
    def __init__(self, sec, me, n, src, recv, pre, dst, sems, decay, inner):
        self.sec, self.me, self.n = sec, me, n
        self.src, self.recv, self.pre, self.dst, self.decay = src, recv, pre, dst, decay
        self.send1, self.recv1, self.send2, self.recv2 = sems
        self.blocks = min(n, inner // LANES)
        self.stride = n // self.blocks
        self.mine = me // self.stride
        self.reverse = decay is not None

    def when(self, cond, fn):
        if self.stride == 1:
            fn()
        else:
            pl.when(cond)(fn)

    def to(self, k):
        return lax.rem(self.me + k, self.n)

    def frm(self, k):
        return lax.rem(self.me - k + self.n, self.n)

    def lane(self, dev):
        return pl.ds(pl.multiple_of((dev // self.stride) * LANES, LANES), LANES)

    def owns(self, dev):
        return lax.rem(dev, self.stride) == 0

    def first(self, k, dev, slot):
        return pltpu.make_async_remote_copy(
            src_ref=self.src.at[:, self.lane(dev)], dst_ref=self.recv.at[slot],
            send_sem=self.send1.at[k], recv_sem=self.recv1.at[slot],
            device_id=(self.sec, dev), device_id_type=MESH)

    def second(self, k, dev, frm):
        return pltpu.make_async_remote_copy(
            src_ref=self.pre.at[dev], dst_ref=self.dst.at[:, self.lane(frm)],
            send_sem=self.send2.at[k], recv_sem=self.recv2.at[frm],
            device_id=(self.sec, dev), device_id_type=MESH)

    def send(self):
        for k in range(1, self.n):
            self.when(self.owns(self.to(k)), lambda k=k: self.first(k, self.to(k), self.me).start())

    def combine(self):
        def own():
            self.recv[self.me] = self.src[:, self.lane(self.me)]
            for k in range(1, self.n):
                self.first(k, self.frm(k), self.frm(k)).wait_recv()
            run = jnp.zeros((N, LANES), F32)
            for i in range(self.n):
                d = self.n - 1 - i if self.reverse else i
                self.pre[d] = run.astype(BF)
                if self.reverse:
                    dec, st = self.decay[d], self.recv[d]
                else:
                    dec, st = self.recv[d, 0:N, :], self.recv[d, N : 2 * N, :]
                    self.decay_out[d] = dec
                run = dec.astype(F32) * run + st.astype(F32)
            for k in range(1, self.n):
                self.second(k, self.to(k), self.me).start()
            self.dst[:, self.lane(self.me)] = self.pre[self.me]

        self.when(self.owns(self.me), own)

    def get(self):
        for k in range(1, self.n):
            self.when(
                self.owns(self.frm(k)),
                lambda k=k: pltpu.make_async_remote_copy(
                    src_ref=self.pre.at[0], dst_ref=self.dst.at[:, self.lane(self.frm(k))],
                    send_sem=self.send2.at[k], recv_sem=self.recv2.at[self.frm(k)],
                    device_id=(self.sec, self.frm(k)), device_id_type=MESH).wait_recv())

    def sent(self):
        for k in range(1, self.n):
            self.when(self.owns(self.to(k)), lambda k=k: self.first(k, self.to(k), self.me).wait_send())

        def own():
            for k in range(1, self.n):
                self.second(k, self.to(k), self.me).wait_send()

        self.when(self.owns(self.me), own)


SAVED = ("xi", "z", "c", "beta", "ex", "us", "k2", "qb", "y", "proj", "dec", "sb")


def block_diag(projb, first_col):
    pick = (iota((LANES, BT * N), 0) == first_col + iota((LANES, BT * N), 1) % N).astype(F32).astype(BF)
    vals = dot(projb, pick)
    same = iota((BT, BT * N), 0) == iota((BT, BT * N), 1) // N
    return jnp.where(same, vals, 0.0)


def forward_kernel(n, rank, *refs):
    refs = list(refs)

    def take(k):
        out = refs[:k]
        del refs[:k]
        return out

    bounds_ref, tok_ref, gain_ref, ck_ref, cb_ref, dtb_ref, skip_ref, xproj_ref, dtproj_ref, in_own, out_own = take(11)
    in_oth, out_oth, mask_ref, xp2, dtp2, vec2, hmid_ref, hout_ref = take(8)
    hbm = [dict(zip(SAVED + ("s", "ut4", "ot4"), take(len(SAVED) + 3))) for _ in range(2)]
    loc = dict(zip(SAVED, take(len(SAVED))))
    kb_ref, w_in, w_out, stage, rim_ref, hrow, st, sbuf, o_all, ut_s, ot_s = take(11)
    c_src, c_recv, c_pre, c_dst = take(4)
    (sv_sem, wi_sem, wo_sem, sm_s, sm_r, xz_s, xz_r, oth_s, oth_r, rim_s, rim_r, s_sem, op_s, op_r, own_sem,
     c1, c2, c3, c4) = take(19)
    assert not refs
    sec = lax.axis_index("section")
    bits, me, mybit = coords(n)
    x = mybit[0]
    neigh = me + 1 - 2 * x
    t_len, width = hout_ref.shape
    inner = w_out.shape[0]
    used = xproj_ref.shape[0]
    cb = 512
    n_half = inner // cb
    rim = rim_ref.shape[2]
    barrier = pltpu.get_barrier_semaphore()
    for k in range(1, n):
        pl.semaphore_signal(barrier, inc=1, device_id=(sec, lax.rem(me + k, n)), device_id_type=MESH)
    pl.semaphore_signal(barrier, inc=1, device_id=(1 - sec, me), device_id_type=MESH)

    in_order = list(range(n_half, 2 * n_half)) + list(range(n_half))

    def in_copy(k, src):
        at = pl.ds(k * cb, cb)
        return pltpu.make_async_copy(src.at[:, at], w_in.at[:, at], wi_sem.at[k])

    def out_copy(src):
        return pltpu.make_async_copy(src, w_out, wo_sem)

    @pl.when(sec == 0)
    def _():
        for k in in_order:
            in_copy(k, in_own).start()
        out_copy(out_own).start()

    @pl.when(sec == 1)
    def _():
        for k in in_order:
            in_copy(k, in_own).start()

    vec2[sec, 0:4, :] = ck_ref[...].astype(F32)
    vec2[sec, 4:5, :] = cb_ref[...].astype(F32)
    vec2[sec, 5:6, :] = dtb_ref[...].astype(F32)
    vec2[sec, 6:7, :] = skip_ref[...].astype(F32)
    vec2[sec, 7:8, 0:width] = gain_ref[...].astype(F32)
    vec2[sec, 7:8, width:inner] = jnp.zeros((1, inner - width), F32)
    xp2[sec, 0:used, :] = xproj_ref[...]
    xp2[sec, used:LANES, :] = jnp.zeros((LANES - used, inner), BF)
    dtp2[sec, 0:rank, :] = dtproj_ref[...]
    dtp2[sec, rank:LANES, :] = jnp.zeros((LANES - rank, inner), BF)
    row = me * t_len + iota((t_len, LANES), 0)
    col = iota((t_len, LANES), 1)
    start = jnp.zeros((t_len, LANES), jnp.int32)
    for cut in range(1, 7):
        bound = bounds_ref[sec, cut]
        start = jnp.where(row >= bound, bound, start)
    tap = jnp.where(row - 3 + col >= start, 1.0, 0.0)
    keeps = jnp.where(row != start, 1.0, 0.0)
    mask_ref[...] = jnp.where(col < 4, tap, jnp.where(col == 4, keeps, 0.0))

    pl.semaphore_wait(barrier, n)

    def sibling(src, dst, a, b):
        return pltpu.make_async_remote_copy(
            src_ref=src, dst_ref=dst, send_sem=a, recv_sem=b, device_id=(1 - sec, me), device_id_type=MESH)

    small = [sibling(r.at[sec], r.at[sec], sm_s.at[i], sm_r.at[i]) for i, r in enumerate((vec2, xp2, dtp2))]
    for cp in small:
        cp.start()

    def rim_copy(layer, to):
        src = tok_ref.at[:, pl.ds(t_len - rim, rim), :] if layer == 0 else hrow.at[pl.ds(t_len - rim, rim), :]
        dst = rim_ref.at[0] if layer == 0 else rim_ref.at[1, 0]
        return pltpu.make_async_remote_copy(
            src_ref=src, dst_ref=dst, send_sem=rim_s.at[layer], recv_sem=rim_r.at[layer],
            device_id=(sec, to), device_id_type=MESH)

    def has_rim(layer, cond):
        return cond & (sec == 0) if layer == 0 else cond

    def send_rim(layer):
        @pl.when(has_rim(layer, me < n - 1))
        def _():
            rim_copy(layer, me + 1).start()

        @pl.when(me == 0)
        def _():
            if layer == 0:
                rim_ref[0] = jnp.zeros(rim_ref.shape[1:], BF)
            else:
                rim_ref[1, 0] = jnp.zeros(rim_ref.shape[2:], BF)

    def get_rim(layer):
        @pl.when(has_rim(layer, me > 0))
        def _():
            rim_copy(layer, me).wait_recv()

    def oth(k):
        if k == 0:
            return sibling(out_own, out_oth, oth_s.at[0], oth_r.at[0])
        return sibling(in_own, in_oth, oth_s.at[1], oth_r.at[1])

    send_rim(0)

    @pl.when(sec == 1)
    def _():
        oth(1).start()

    def xz_copy(k, rows):
        at = pl.ds((k % n_half) * cb, cb)
        dst = loc["z"] if k >= n_half else loc["xi"]
        return sibling(stage.at[k, pl.ds(0, rows), :], dst.at[:, at], xz_s.at[k], xz_r.at[k])

    def normed(h, layer):
        hf = h.astype(F32)
        inv = lax.rsqrt(jnp.mean(hf * hf, axis=-1, keepdims=True) + NORM_EPS)
        return (hf * inv * vec2[layer, 7:8, 0:width]).astype(BF)

    @pl.when(sec == 0)
    def _():
        both = normed(jnp.concatenate([tok_ref[0], tok_ref[1]], axis=0), 0)
        for k in in_order[:n_half]:
            in_copy(k, in_own).wait()
            r = dot(both, w_in[:, k * cb : (k + 1) * cb])
            loc["z"][:, pl.ds((k - n_half) * cb, cb)] = r[:t_len]
            stage[k, 0:t_len, :] = r[t_len:]
            xz_copy(k, t_len).start()
        get_rim(0)
        edge = normed(jnp.concatenate([rim_ref[0, 0], rim_ref[0, 1]], axis=0), 0)
        rows = jnp.concatenate([edge[:rim], both[:t_len], edge[rim:], both[t_len:]], axis=0)
        for k in in_order[n_half:]:
            in_copy(k, in_own).wait()
            r = dot(rows, w_in[:, k * cb : (k + 1) * cb])
            loc["xi"][:, pl.ds(k * cb, cb)] = r[: rim + t_len]
            stage[k] = r[rim + t_len :]
            xz_copy(k, rim + t_len).start()

    hrow[...] = tok_ref[sec]
    for cp in small:
        cp.wait_recv()

    @pl.when(sec == 1)
    def _():
        for k in in_order:
            xz_copy(k, t_len if k >= n_half else rim + t_len).wait_recv()

    @pl.when(sec == 0)
    def _():
        oth(0).start()

    carries = []
    saved = []

    def keep(name, layer):
        cp = pltpu.make_async_copy(loc[name], hbm[layer][name], sv_sem.at[layer, SAVED.index(name)])
        cp.start()
        saved.append((layer, name))

    def kept(name, layer):
        pltpu.make_async_copy(loc[name], hbm[layer][name], sv_sem.at[layer, SAVED.index(name)]).wait()

    def part_copy(kind, layer, k):
        src = (ut_s, ot_s)[kind].at[layer]
        dst = hbm[layer][("ut4", "ot4")[kind]]

        def slot(i):
            return pl.ds(pl.multiple_of(i * t_len, LANES), t_len)

        mine = 2 * sec + x
        if k == 0:
            s, i, to = src.at[:, x], mine, (1 - sec, me)
        elif k == 1:
            s, i, to = src.at[:, 1 - x], mine, (sec, neigh)
        else:
            i, to = 2 * sec + 1 - x, (1 - sec, me)
            s = dst.at[:, :, slot(i)]
        return pltpu.make_async_remote_copy(
            src_ref=s, dst_ref=dst.at[:, :, slot(i)], send_sem=op_s.at[layer, kind, k], recv_sem=op_r.at[layer, kind, i],
            device_id=to, device_id_type=MESH)

    def part_arrived(kind, layer, i):
        dst = hbm[layer][("ut4", "ot4")[kind]]
        at = pl.ds(pl.multiple_of(i * t_len, LANES), t_len)
        pltpu.make_async_remote_copy(
            src_ref=(ut_s, ot_s)[kind].at[layer, :, 0], dst_ref=dst.at[:, :, at], send_sem=op_s.at[layer, kind, 0],
            recv_sem=op_r.at[layer, kind, i], device_id=(1 - sec, me), device_id_type=MESH).wait_recv()

    def part_own(kind, layer):
        at = pl.ds(pl.multiple_of((2 * sec + x) * t_len, LANES), t_len)
        return pltpu.make_async_copy(
            (ut_s, ot_s)[kind].at[layer, :, x], hbm[layer][("ut4", "ot4")[kind]].at[:, :, at], own_sem.at[layer, kind])

    def part_send(kind, layer):
        part_copy(kind, layer, 0).start()
        part_copy(kind, layer, 1).start()
        part_own(kind, layer).start()

    def part_forward(kind, layer):
        part_arrived(kind, layer, 2 * sec + 1 - x)
        part_copy(kind, layer, 2).start()

    mask = mask_ref[...]
    cols = iota((t_len, LANES), 1)
    keepc = mask[:, 4:5]
    for layer in range(2):
        vec, xp, dtp = vec2.at[layer], xp2.at[layer], dtp2.at[layer]
        u = normed(hrow[...], layer)
        if layer == 1:
            for k in in_order[:n_half]:
                in_copy(k, in_own).wait()
                loc["z"][:, pl.ds((k - n_half) * cb, cb)] = dot(u, w_in[:, k * cb : (k + 1) * cb])
            get_rim(1)
            rows = jnp.concatenate([normed(rim_ref[1, 0], 1), u], axis=0)
            for k in in_order[n_half:]:
                in_copy(k, in_own).wait()
                loc["xi"][:, pl.ds(k * cb, cb)] = dot(rows, w_in[:, k * cb : (k + 1) * cb])
        keep("z", layer)
        keep("xi", layer)
        proj = jnp.zeros((t_len, LANES), F32)
        for k in range(n_half):
            at = pl.ds(k * cb, cb)
            xi = loc["xi"][:, at]
            c = vec[4:5, at] + vec[3:4, at] * xi[rim:]
            for j in range(3):
                c = c + vec[j : j + 1, at] * xi[rim - 3 + j : rim - 3 + j + t_len] * mask[:, j : j + 1]
            loc["c"][:, at] = c
            xc = c * jax.nn.sigmoid(c)
            loc["us"][:, at] = xc
            proj = proj + dot_nt(xc.astype(BF), xp[:, at])
        keep("c", layer)
        projb = jnp.where(cols == rank + 2 * N, keepc, proj).astype(BF)
        loc["proj"][...] = projb
        keep("proj", layer)
        pf = projb.astype(F32)
        ksum = jnp.sum(jnp.where((cols >= rank) & (cols < rank + N), pf * pf, 0.0), axis=-1, keepdims=True)
        for k in range(n_half):
            at = pl.ds(k * cb, cb)
            beta = jax.nn.sigmoid(dot(projb, dtp[:, at]) + vec[5:6, at])
            eps = beta / (1.0 + beta * ksum)
            loc["beta"][:, at] = beta
            loc["us"][:, at] = loc["us"][:, at] * eps
            loc["ex"][:, at] = jnp.where(keepc > 0.0, eps, 1.0)
        for name in ("beta", "us", "ex"):
            keep(name, layer)
        nrow = t_len * N
        sel = (iota((nrow, t_len), 0) // N == iota((nrow, t_len), 1)).astype(F32).astype(BF)
        spread = dot(sel, projb).astype(BF)
        rn = iota((nrow, LANES), 0) % N
        cl = iota((nrow, LANES), 1)
        ones = jnp.ones((LANES, LANES), BF)
        zero = jnp.zeros((nrow, LANES), BF)
        kb = dot(jnp.where(cl == rank + rn, spread, zero), ones)
        kb_ref[...] = kb
        loc["qb"][...] = dot(jnp.where(cl == rank + N + rn, spread, zero), ones)
        keepb = dot(jnp.where(cl == rank + 2 * N, spread, zero), ones)
        loc["k2"][...] = jnp.where(keepb > 0.5, -LOG2E * kb * kb, -1e30)
        keep("qb", layer)
        keep("k2", layer)
        ec = 512
        nt = ec // LANES
        un = 16
        k2_ref, ex_ref, us_ref = loc["k2"], loc["ex"], loc["us"]

        def chunk(ci, carry, layer=layer):
            e0 = pl.multiple_of(ci * ec, ec)

            def body(i, sd):
                s, d = [list(v) for v in sd]
                g0 = pl.multiple_of(i * un, un)
                for t in range(un):
                    r = pl.multiple_of(g0 * N + t * N, N)
                    k2 = k2_ref[pl.ds(r, N), :]
                    kv = kb_ref[pl.ds(r, N), :]
                    for j in range(nt):
                        lane = pl.ds(e0 + LANES * j, LANES)
                        a = jnp.exp2(k2 * ex_ref.at[pl.ds(g0, un), lane][t : t + 1, :])
                        s[j] = a * s[j] + kv * us_ref.at[pl.ds(g0, un), lane][t : t + 1, :]
                        d[j] = a * d[j]
                return tuple(s), tuple(d)

            zeros = tuple(jnp.zeros((N, LANES), F32) for _ in range(nt))
            one = tuple(jnp.ones((N, LANES), F32) for _ in range(nt))
            s, d = lax.fori_loop(0, t_len // un, body, (zeros, one))
            for j in range(nt):
                lane = pl.ds(e0 + LANES * j, LANES)
                c_src[layer, 0:N, lane] = d[j].astype(BF)
                c_src[layer, N : 2 * N, lane] = s[j].astype(BF)
            return carry

        lax.fori_loop(0, inner // ec, chunk, 0)
        cr = Carry(sec, me, n, c_src.at[layer], c_recv.at[layer], c_pre.at[layer], c_dst.at[layer],
                   [s.at[layer] for s in (c1, c2, c3, c4)], None, inner)
        cr.decay_out = loc["dec"]
        carries.append(cr)
        if layer == 1:
            for name in ("dec", "sb", "y"):
                kept(name, 0)
        cr.send()
        ut_s[layer] = u.T.reshape(ut_s.shape[1:])
        cr.combine()
        keep("dec", layer)
        cr.get()
        st[...] = c_dst[layer].astype(F32)
        part_send(0, layer)
        if layer == 0:
            @pl.when(sec == 0)
            def _():
                oth(1).start()
                oth(1).wait_recv()
                for k in in_order:
                    in_copy(k, in_oth).start()

            @pl.when(sec == 1)
            def _():
                oth(0).start()
                oth(0).wait_recv()
                out_copy(out_oth).start()
        else:
            part_forward(1, 0)

        def s_copy(blk, slot, layer=layer):
            return pltpu.make_async_copy(
                sbuf.at[slot], hbm[layer]["s"].at[pl.ds(pl.multiple_of(blk * BT * N, BT * N), BT * N), :], s_sem.at[slot])

        steps = t_len // BT

        def block(i, carry, s_copy=s_copy, vec=vec):
            slot = lax.rem(i, 2)
            rows = pl.ds(pl.multiple_of(i * BT, BT), BT)
            rbase = pl.multiple_of(i * BT * N, BT * N)

            @pl.when(i >= 2)
            def _():
                s_copy(i - 2, slot).wait()

            loc["sb"][rows, :] = st[...].astype(BF)
            qbd = block_diag(loc["proj"][rows, :], rank + N).astype(BF)
            s_ref = sbuf.at[slot]
            for ci in range(inner // ec):
                e0 = ci * ec
                s = [st[:, pl.ds(e0 + LANES * j, LANES)] for j in range(nt)]
                for t in range(BT):
                    krow = pl.ds(pl.multiple_of(rbase + t * N, N), N)
                    k2 = k2_ref[krow, :]
                    kv = kb_ref[krow, :]
                    for j in range(nt):
                        lane = pl.ds(e0 + LANES * j, LANES)
                        a = jnp.exp2(k2 * ex_ref.at[rows, lane][t : t + 1, :])
                        s[j] = a * s[j] + kv * us_ref.at[rows, lane][t : t + 1, :]
                        s_ref[t * N : (t + 1) * N, lane] = s[j].astype(BF)
                for j in range(nt):
                    st[:, pl.ds(e0 + LANES * j, LANES)] = s[j]
                at = pl.ds(e0, ec)
                c = loc["c"][rows, at]
                y = dot(qbd, s_ref[:, at]) + vec[6:7, at] * (c * jax.nn.sigmoid(c))
                loc["y"][rows, at] = y
                z = loc["z"][rows, at]
                o_all[rows, at] = (y * (z * jax.nn.sigmoid(z))).astype(BF)
            s_copy(i, slot).start()
            return carry

        lax.fori_loop(0, steps, block, 0)
        keep("sb", layer)
        keep("y", layer)
        part_forward(0, layer)
        out_copy(out_own).wait()
        o = o_all[...]
        hn = (hrow[...].astype(F32) + dot(o, w_out[...])).astype(BF)
        if layer == 0:
            hrow[...] = hn
            hmid_ref[...] = hn
            send_rim(1)

            @pl.when(sec == 0)
            def _():
                oth(0).wait_recv()
                out_copy(out_oth).start()

            @pl.when(sec == 1)
            def _():
                oth(1).wait_recv()
                out_copy(out_own).start()
        else:
            hout_ref[...] = hn
        ot_s[layer] = o.T.reshape(ot_s.shape[1:])
        if layer == 0:
            part_send(1, 0)
        else:
            last_o = pltpu.make_async_copy(ot_s.at[1], hbm[1]["ot4"], own_sem.at[1, 1])
            last_o.start()
        for slot in range(2):
            s_copy(steps - 2 + slot, slot).wait()
        if layer == 0:
            for name in SAVED:
                if name not in ("dec", "sb", "y"):
                    kept(name, 0)

    for name in SAVED:
        kept(name, 1)
    last_o.wait()
    for layer, kind in ((0, 0), (0, 1), (1, 0)):
        part_own(kind, layer).wait()
        for i in range(2):
            part_arrived(kind, layer, 2 * (1 - sec) + (x if i == 0 else 1 - x))
        for k in range(3):
            part_copy(kind, layer, k).wait_send()
    for cp in small:
        cp.wait_send()
    for k in range(2):
        oth(k).wait_send()

    @pl.when(sec == 0)
    def _():
        for k in in_order:
            xz_copy(k, t_len if k >= n_half else rim + t_len).wait_send()

    for layer in range(2):
        @pl.when(has_rim(layer, me < n - 1))
        def _(layer=layer):
            rim_copy(layer, me + 1).wait_send()

    for cr in carries:
        cr.sent()


def forward(n, rank, cid, bounds, tokens, smalls, in_own, out_own):
    t_len, width = tokens.shape[1:]
    inner = out_own.shape[0]
    rim = 16
    rows = t_len * N

    def f32(*s):
        return jax.ShapeDtypeStruct(s, F32)

    def b16(*s):
        return jax.ShapeDtypeStruct(s, BF)

    shapes = {
        "xi": f32(t_len + rim, inner), "z": f32(t_len, inner), "c": f32(t_len, inner), "beta": f32(t_len, inner),
        "ex": f32(t_len, inner), "us": f32(t_len, inner), "k2": f32(rows, LANES), "qb": f32(rows, LANES),
        "y": f32(t_len, inner), "proj": b16(t_len, LANES), "dec": b16(n, N, LANES), "sb": b16(t_len, inner),
    }
    outs = [
        b16(width, 2 * inner), b16(inner, width), f32(t_len, LANES), b16(2, LANES, inner), b16(2, LANES, inner),
        f32(2, 8, inner), b16(t_len, width), b16(t_len, width),
    ]
    specs = [ANYSPEC, ANYSPEC] + [VSPEC] * 6
    for layer in range(2):
        outs += [shapes[name] for name in SAVED]
        outs += [b16(rows, inner), b16(n // 2, width // n, 4 * t_len)]
        outs += [b16(n // 2, 2, inner // n, t_len) if layer else b16(n // 2, inner // n, 4 * t_len)]
        specs += [ANYSPEC] * (len(SAVED) + 3)
    scratch = [pltpu.VMEM(shapes[name].shape, shapes[name].dtype) for name in SAVED]
    scratch += [
        pltpu.VMEM((rows, LANES), F32), pltpu.VMEM((width, 2 * inner), BF), pltpu.VMEM((inner, width), BF),
        pltpu.VMEM((2 * inner // 512, rim + t_len, 512), F32), pltpu.VMEM((2, 2, rim, width), BF),
        pltpu.VMEM((t_len, width), BF), pltpu.VMEM((N, inner), F32), pltpu.VMEM((2, BT * N, inner), BF),
        pltpu.VMEM((t_len, inner), BF), pltpu.VMEM((2, n // 2, 2, width // n, t_len), BF),
        pltpu.VMEM((2, n // 2, 2, inner // n, t_len), BF),
        pltpu.VMEM((2, 2 * N, inner), BF), pltpu.VMEM((2, n, 2 * N, LANES), BF), pltpu.VMEM((2, n, N, LANES), BF),
        pltpu.VMEM((2, N, inner), BF),
    ]
    dma = pltpu.SemaphoreType.DMA
    n_in = 2 * inner // 512
    scratch += [
        dma((2, len(SAVED))), dma((n_in,)), dma(()), dma((3,)), dma((3,)), dma((n_in,)), dma((n_in,)), dma((2,)), dma((2,)),
        dma((2,)), dma((2,)), dma((2,)), dma((2, 2, 3)), dma((2, 2, 4)), dma((2, 2)),
        dma((2, n)), dma((2, n)), dma((2, n)), dma((2, n)),
    ]
    res = pl.pallas_call(
        functools.partial(forward_kernel, n, rank),
        out_shape=outs,
        in_specs=[pl.BlockSpec(memory_space=pltpu.SMEM)] + [VSPEC] * 8 + [ANYSPEC] * 2,
        out_specs=specs,
        scratch_shapes=scratch,
        compiler_params=pltpu.CompilerParams(vmem_limit_bytes=60 * MIB, collective_id=cid, has_side_effects=True),
        name="forward",
    )(bounds, tokens, *smalls, in_own, out_own)
    first, rest = res[:8], res[8:]
    per = len(SAVED) + 3
    saved = [dict(zip(SAVED + ("s", "ut4", "ot4"), rest[i * per : (i + 1) * per])) for i in range(2)]
    return first, saved


class Sub:
    def __init__(self, kit, num, layer, buf, recvs, out, lane0, lanes, steps, held):
        self.kit, self.num, self.layer = kit, num, layer
        self.at = pl.ds(lane0, lanes)
        self.buf, self.recvs, self.out = buf, recvs, out
        self.steps, self.held = steps, held
        self.last = len(steps) - 1
        self.stage = 0

    def bit(self, what):
        return self.kit.sec if what == "s" else self.kit.mybit[what]

    def partner(self, i):
        kit, what = self.kit, self.steps[i]
        if what == "s":
            return (1 - kit.sec, kit.me)
        return (kit.sec, kit.me + 2**what * (1 - 2 * kit.mybit[what]))

    def index(self, i, away):
        done = {w: self.bit(w) for w in self.steps[:i]}
        what = self.steps[i]
        done[what] = 1 - self.bit(what) if away else self.bit(what)
        return tuple(done.get(w, slice(None)) for w in self.held)

    def copy(self, i):
        free = len(self.held) - 1 - i
        return pltpu.make_async_remote_copy(
            src_ref=self.buf.at[self.index(i, True) + (slice(None), self.at)],
            dst_ref=self.recvs[i].at[(slice(None),) * (free + 1) + (self.at,)],
            send_sem=self.kit.ssem.at[self.layer, self.num, i], recv_sem=self.kit.rsem.at[self.layer, self.num, i],
            device_id=self.partner(i), device_id_type=MESH)

    def begin(self):
        self.copy(0).start()

    def place(self, half):
        return self.kit.place[self.out](half, self.at)

    def final(self):
        kit = self.kit
        return pltpu.make_async_remote_copy(
            src_ref=kit.res[self.out].at[:, self.at], dst_ref=self.place(1 - self.layer),
            send_sem=kit.fsem.at[self.layer, self.num], recv_sem=kit.frsem.at[self.layer, self.num],
            device_id=(1 - kit.sec, kit.me), device_id_type=MESH)

    def advance(self):
        i = self.stage
        if i > self.last:
            return
        kit = self.kit
        self.copy(i).wait_recv()
        free = len(self.held) - 1 - i
        fixed = self.index(i, False)
        res = kit.res[self.out]

        def body(k, carry):
            sub = list(unpack_index(k, free))
            src = tuple(sub) + (slice(None), self.at)
            dst = tuple(sub.pop(0) if isinstance(f, slice) else f for f in fixed) + (slice(None), self.at)
            if i == self.last:
                val = self.buf[dst].astype(F32) + self.recvs[i][src].astype(F32)

                @pl.when(kit.sec == self.layer)
                def _():
                    self.place(self.layer)[...] = val

                @pl.when(kit.sec != self.layer)
                def _():
                    res[:, self.at] = val
            else:
                self.buf[dst] = self.buf[dst] + self.recvs[i][src]
            return carry

        if free:
            lax.fori_loop(0, 2**free, body, 0)
        else:
            body(0, 0)
        self.stage = i + 1
        if i < self.last:
            self.copy(i + 1).start()
        else:
            @pl.when(kit.sec != self.layer)
            def _():
                self.final().start()

    def finish(self):
        assert self.stage > self.last
        for i in range(self.last + 1):
            self.copy(i).wait_send()

        @pl.when(self.kit.sec != self.layer)
        def _():
            self.final().wait_send()

        @pl.when(self.kit.sec == self.layer)
        def _():
            self.final().wait_recv()


class VecSum:
    def __init__(self, kit, layer, n, acc, sib, msg, got, out):
        self.kit, self.layer, self.n = kit, layer, n
        self.acc, self.sib, self.msg, self.got, self.out = acc, sib, msg, got, out
        self.stage = 0

    def across(self):
        kit = self.kit
        return pltpu.make_async_remote_copy(
            src_ref=self.acc.at[self.layer], dst_ref=self.sib.at[self.layer],
            send_sem=kit.vsem.at[self.layer], recv_sem=kit.vrsem.at[self.layer],
            device_id=(1 - kit.sec, kit.me), device_id_type=MESH)

    def copy(self, k, dev, slot):
        kit = self.kit
        return pltpu.make_async_remote_copy(
            src_ref=self.msg.at[dev], dst_ref=self.got.at[slot],
            send_sem=kit.v2sem.at[self.layer, k], recv_sem=kit.v2rsem.at[self.layer, slot],
            device_id=(kit.sec, dev), device_id_type=MESH)

    def begin(self):
        @pl.when(self.kit.sec != self.layer)
        def _():
            self.across().start()

    def advance(self):
        kit, n = self.kit, self.n
        if self.stage > 1:
            return
        first = self.stage == 0
        self.stage += 1

        @pl.when(kit.sec == self.layer)
        def _():
            if first:
                self.across().wait_recv()
                total = self.acc[self.layer] + self.sib[self.layer]
                inner = total.shape[1]
                for j in range(n):
                    l0 = (j * (inner // n)) // LANES * LANES
                    g0 = (j * (kit.width // n)) // LANES * LANES
                    self.msg[j, 0:8, :] = total[:, l0 : l0 + LANES]
                    self.msg[j, 8:16, :] = total[:, g0 : g0 + LANES]
                for k in range(1, n):
                    self.copy(k, lax.rem(kit.me + k, n), kit.me).start()
                self.got[kit.me] = self.msg[kit.me]
            else:
                for k in range(1, n):
                    frm = lax.rem(kit.me + k, n)
                    self.copy(k, frm, frm).wait_recv()
                val = self.got[0]
                for j in range(1, n):
                    val = val + self.got[j]
                self.out[...] = val

    def drain(self):
        kit = self.kit
        while self.stage < 2:
            self.advance()

        @pl.when(kit.sec != self.layer)
        def _():
            self.across().wait_send()

        @pl.when(kit.sec == self.layer)
        def _():
            for k in range(1, self.n):
                self.copy(k, lax.rem(kit.me + k, self.n), kit.me).wait_send()


class Kit:
    pass


class Gather:
    def __init__(self, kit, kind, layer, src, dst):
        self.kit, self.kind, self.layer = kit, kind, layer
        self.src, self.dst = src, dst

    def peers(self):
        kit = self.kit
        x = kit.mybit[0]
        other = kit.me + 1 - 2 * x
        return [(1 - kit.sec, kit.me, x), (kit.sec, other, 1 - x), (1 - kit.sec, other, 1 - x)]

    def copy(self, k, slot):
        kit = self.kit
        sec, dev, bit = self.peers()[k]
        return pltpu.make_async_remote_copy(
            src_ref=self.src(sec, bit), dst_ref=self.dst(slot),
            send_sem=kit.osem.at[self.layer, self.kind, k], recv_sem=kit.orsem.at[self.layer, self.kind, slot],
            device_id=(sec, dev), device_id_type=MESH)

    def slot(self, sec, bit):
        return 2 * sec + bit

    def send(self, order=(1, 2, 0)):
        mine = self.slot(self.kit.sec, self.kit.mybit[0])
        for k in order:
            self.copy(k, mine).start()

    def wait(self):
        for k in range(3):
            sec, dev, bit = self.peers()[k]
            self.copy(k, self.slot(sec, bit)).wait_recv()

    def sent(self):
        mine = self.slot(self.kit.sec, self.kit.mybit[0])
        for k in range(3):
            self.copy(k, mine).wait_send()


LOADS = ("h", "xi", "z", "c", "proj", "beta", "ex", "us", "k2", "qb", "sb", "y", "dec")
BOTH = ("h", "proj", "dec", "sb")
BIG = ("go", "gz", "gx")


def lane_parts(lanes):
    unit = lanes // LANES
    a = max(1, (3 * unit) // 4)
    return [(0, a * LANES, 0), (a * LANES, lanes - a * LANES, 1)]


def two_parts(lanes):
    q = lanes // 4
    return [(0, q, 0), (q, q, 1), (2 * q, q, 0), (3 * q, q, 1)]


def bit_orders(bits):
    low = list(range(1, bits))
    return [low, [2, 1] + low[2:]]


def back_kernel(n, rank, shapes, *refs):
    refs = list(refs)

    def take(k):
        out = refs[:k]
        del refs[:k]
        return out

    tokens, cots, mask_ref, in_own, in_oth, out_own, out_oth = take(7)
    hbm = [dict(zip(LOADS + ("s", "ut4", "ot4"), take(len(LOADS) + 3))) for _ in range(2)]
    vec2, xp2, dtp2 = take(3)
    dh_out, gin_out, gout_out, gsm_out, vec_out = take(5)
    loc = {name: (take(2) if name in BOTH else take(1) * 2) for name in LOADS}
    (g_both, w_out, w_in, sbuf, qs2, ws2, bst, deps, dkq, dy_ref, dz_both, dx_both, gdt_ref, gtmp, rims, rimr) = take(16)
    dxc = loc["y"][0]
    ut4, ot4, dr4, dz4, dx4 = take(5)
    kit = Kit()
    bits, me, mybit = coords(n)
    bufs = [dict(zip(BIG + ("sm",), take(4))) for _ in range(2)]
    recvs = []
    for _ in range(2):
        got = {name: take(bits - 1) for name in BIG}
        got["sm"] = take(bits + 1)
        recvs.append(got)
    kit.res = dict(zip(BIG + ("sm",), take(4)))
    vacc, vsib, vmsg, vgot = take(4)
    c_src, c_recv, c_pre, c_dst = take(4)
    (ld_sem, g_sem, wo_sem, wi_sem, s_sem, rim_sem, rimr_sem, own_sem, kit.osem, kit.orsem, kit.ssem, kit.rsem,
     kit.fsem, kit.frsem, kit.vsem, kit.vrsem, kit.v2sem, kit.v2rsem, o_sem, o_rsem, c1, c2, c3, c4) = take(24)
    assert not refs
    sec = lax.axis_index("section")
    kit.sec, kit.me, kit.bits, kit.mybit = sec, me, bits, mybit
    t_len, width = dh_out.shape
    inner = w_out.shape[0]
    cb = 512
    lead = shapes["lead"]

    barrier = pltpu.get_barrier_semaphore()
    for k in range(1, n):
        pl.semaphore_signal(barrier, inc=1, device_id=(sec, lax.rem(me + k, n)), device_id_type=MESH)
    for to in (me, me + 1 - 2 * mybit[0]):
        pl.semaphore_signal(barrier, inc=1, device_id=(1 - sec, to), device_id_type=MESH)

    pos = {name: i for i, name in enumerate(LOADS)}

    def load(name, layer):
        src = tokens.at[sec] if (name, layer) == ("h", 0) else hbm[layer][name]
        return pltpu.make_async_copy(src, loc[name][layer], ld_sem.at[pos[name], layer])

    def out_chunk(k, src):
        at = pl.ds(k * cb, cb)
        return src.at[at, :], w_out.at[at, :], wo_sem.at[k]

    def in_chunk(k, slot, src):
        return src.at[:, pl.ds(k * cb, cb)], w_in.at[slot], wi_sem.at[slot]

    def fetch(layer, chunk, own, oth):
        a, b, s = chunk(own)
        a2 = chunk(oth)[0]

        @pl.when(sec == layer)
        def _():
            pltpu.make_async_copy(a, b, s).start()

        @pl.when(sec != layer)
        def _():
            pltpu.make_async_copy(a2, b, s).start()

    def arrive(chunk, own):
        a, b, s = chunk(own)
        pltpu.make_async_copy(a, b, s).wait()

    n_out = inner // cb
    n_in = 2 * inner // cb
    in_order = list(range(n_in // 2, n_in)) + list(range(n_in // 2))
    slots = w_in.shape[0]

    cot_hbm = cots.at[sec]
    pltpu.make_async_copy(cot_hbm, g_both.at[1], g_sem).start()
    for k in range(n_out):
        fetch(1, lambda src, k=k: out_chunk(k, src), out_own, out_oth)
    for name in ("z", "y", "c", "ex", "k2", "qb", "dec", "proj", "beta", "us", "sb", "xi", "h"):
        load(name, 1).start()
    for name in BOTH:
        load(name, 0).start()
    for i in range(slots):
        fetch(1, lambda src, i=i: in_chunk(in_order[i], i, src), in_own, in_oth)

    half_go = width // 2
    half_in = inner // 2
    kit.place = {
        "go": lambda hf, at: gout_out.at[:, pl.ds(hf * half_go + at.start, at.size)],
        "gz": lambda hf, at: gin_out.at[:, pl.ds(inner + hf * half_in + at.start, at.size)],
        "gx": lambda hf, at: gin_out.at[:, pl.ds(hf * half_in + at.start, at.size)],
        "sm": lambda hf, at: gsm_out.at[hf, :, at],
    }
    gx_parts = two_parts(half_in)
    subs = []
    for layer in range(2):
        mine = {}
        num = 0
        for name, parts in (("go", lane_parts(half_go)), ("gz", lane_parts(half_in)), ("gx", gx_parts)):
            mine[name] = []
            for l0, ln, which in parts:
                mine[name].append(
                    Sub(kit, num, layer, bufs[layer][name], recvs[layer][name], name, l0, ln, bit_orders(bits)[which],
                        list(range(bits - 1, 0, -1))))
                num += 1
        mine["sm"] = [Sub(kit, num, layer, bufs[layer]["sm"], recvs[layer]["sm"], "sm", 0, LANES,
                          ["s", 2, 1, 0] + list(range(3, bits)), ["s"] + list(range(bits - 1, -1, -1)))]
        subs.append(mine)

    def begin(layer, name):
        for s in subs[layer][name]:
            s.begin()

    def advance(layer, *names):
        for name in names:
            if name == "vec":
                vecs[layer].advance()
            else:
                for s in subs[layer][name]:
                    s.advance()

    rows_go = inner // n
    rows_in = width // n
    rows_sm = inner // n
    x = mybit[0]

    def owner(j, count):
        return tuple((j >> (count - 1 - d)) & 1 for d in range(count))

    my_slot = 2 * sec + x

    def operands(layer):
        half = n // 2

        def lanes_of(ref, size):
            return lambda sc, b: ref.at[:, pl.ds(pl.multiple_of(sc * size, LANES), size)]

        def rows_of(ref):
            return lambda slot: ref.at[layer, slot]

        quarter = half_in // 2

        def part_of(ref, p):
            return lambda sc, b: ref.at[:, pl.ds(pl.multiple_of(sc * half_in + p * quarter, LANES), quarter)]

        def part_to(ref, p):
            return lambda slot: ref.at[layer, slot, :, pl.ds(p * quarter, quarter)]

        return {
            "dr": Gather(kit, 0, layer, lanes_of(g_both.at[layer], half_go), rows_of(dr4)),
            "dz": Gather(kit, 1, layer, lanes_of(dz_both.at[layer], half_in), rows_of(dz4)),
            "dx0": Gather(kit, 2, layer, part_of(dx_both.at[layer], 0), part_to(dx4, 0)),
            "dx1": Gather(kit, 3, layer, part_of(dx_both.at[layer], 1), part_to(dx4, 1)),
        }

    ops = [operands(layer) for layer in range(2)]

    def part_load(layer, k):
        src, dst = (("ut4", ut4), ("ot4", ot4))[k]
        return pltpu.make_async_copy(hbm[layer][src], dst.at[layer], own_sem.at[layer, k])

    def own_half(ref, layer, size):
        return ref[layer, :, pl.ds(pl.multiple_of(sec * size, LANES), size)]

    pl.semaphore_wait(barrier, n + 1)
    kit.width = width
    vecs = [VecSum(kit, layer, n, vacc, vsib, vmsg, vgot, vec_out) for layer in range(2)]
    pltpu.make_async_copy(cot_hbm, g_both.at[1], g_sem).wait()
    def slot_at(i):
        return pl.ds(pl.multiple_of(i * t_len, LANES), t_len)

    o_hbm = hbm[1]["ot4"]
    o_own = pltpu.make_async_copy(o_hbm.at[:, x], ot4.at[1, :, :, slot_at(my_slot)], own_sem.at[1, 1])

    def o_copy(k):
        i = my_slot if k < 2 else 2 * sec + 1 - x
        dst = ot4.at[1, :, :, slot_at(i)]
        src = (o_hbm.at[:, 1 - x], o_hbm.at[:, x], dst)[k]
        return pltpu.make_async_remote_copy(
            src_ref=src, dst_ref=dst, send_sem=o_sem.at[k], recv_sem=o_rsem.at[i],
            device_id=(sec, me + 1 - 2 * x) if k == 0 else (1 - sec, me), device_id_type=MESH)

    def o_wait(i):
        dst = ot4.at[1, :, :, slot_at(i)]
        pltpu.make_async_remote_copy(
            src_ref=dst, dst_ref=dst, send_sem=o_sem.at[0], recv_sem=o_rsem.at[i],
            device_id=(1 - sec, me), device_id_type=MESH).wait_recv()

    o_copy(0).start()
    o_copy(1).start()
    o_own.start()
    ops[1]["dr"].send()
    for layer, k in ((1, 0), (0, 1), (0, 0)):
        part_load(layer, k).start()

    def grad_go(layer):
        ops[layer]["dr"].wait()
        if layer == 1:
            o_own.wait()
            o_wait(2 * (1 - sec) + x)
            o_wait(2 * (1 - sec) + 1 - x)
        else:
            part_load(layer, 1).wait()
        dr4[layer, my_slot] = own_half(g_both, layer, half_go)
        rhs = dr4[layer].reshape(4 * t_len, half_go)
        for j in range(n // 2):
            bufs[layer]["go"][owner(j, bits - 1)] = dot(ot4[layer, j], rhs).astype(BF)

    def grad_in(name, layer, four, l0):
        lhs = ut4[layer].reshape(n // 2 * rows_in, 4 * t_len)
        at = pl.ds(l0, cb)
        g = dot(lhs, four[layer, :, :, at].reshape(4 * t_len, cb)).astype(BF)
        for j in range(n // 2):
            bufs[layer][name][owner(j, bits - 1) + (slice(None), at)] = g[j * rows_in : (j + 1) * rows_in]

    def grad_gz(layer):
        ops[layer]["dz"].wait()
        part_load(layer, 0).wait()
        dz4[layer, my_slot] = own_half(dz_both, layer, half_in)
        for l0 in range(0, half_in, cb):
            grad_in("gz", layer, dz4, l0)
        begin(layer, "gz")

    def grad_gx(layer, p):
        if p == 0:
            dx4[layer, my_slot] = own_half(dx_both, layer, half_in)
        ops[layer]["dx0" if p == 0 else "dx1"].wait()
        for l0 in range(p * half_in // 2, (p + 1) * half_in // 2, cb):
            grad_in("gx", layer, dx4, l0)

    carries = []
    for layer in (1, 0):
        g_ref = g_both.at[layer]
        dz_ref = dz_both.at[layer]
        L = {name: loc[name][layer] for name in LOADS}
        vec, xp, dtp = vec2.at[layer], xp2.at[layer], dtp2.at[layer]
        vacc[layer] = jnp.zeros(vacc.shape[1:], F32)
        for name in ("z", "y", "c"):
            load(name, layer).wait()
        dr = g_ref[...]
        for k in range(n_out):
            at = pl.ds(k * cb, cb)
            arrive(lambda src, k=k: out_chunk(k, src), out_own)
            do = dot_nt(dr, w_out[at, :])
            act, der = silu_parts(L["z"][:, at])
            dy = do * act
            dy_ref[:, at] = dy
            dz_ref[:, at] = (do * L["y"][:, at] * der).astype(BF)
            c = L["c"][:, at]
            vacc[layer, 6:7, at] = jnp.sum(dy * (c * jax.nn.sigmoid(c)), axis=0, keepdims=True)
        if layer == 1:
            for k in range(n_out):
                fetch(0, lambda src, k=k: out_chunk(k, src), out_own, out_oth)
            load("z", 0).start()
        for name in ("ex", "k2", "qb"):
            load(name, layer).wait()
        k2_ref, qb_ref, ex_ref = L["k2"], L["qb"], L["ex"]
        ec = 512
        nt = ec // LANES
        un = 16

        def chunk(ci, carry, k2_ref=k2_ref, qb_ref=qb_ref, ex_ref=ex_ref, layer=layer):
            e0 = pl.multiple_of(ci * ec, ec)

            def body(i, b):
                b = list(b)
                g0 = pl.multiple_of((t_len // un - 1 - i) * un, un)
                for t in range(un - 1, -1, -1):
                    r = pl.multiple_of(g0 * N + t * N, N)
                    k2 = k2_ref[pl.ds(r, N), :]
                    qv = qb_ref[pl.ds(r, N), :]
                    for j in range(nt):
                        lane = pl.ds(e0 + LANES * j, LANES)
                        a = jnp.exp2(k2 * ex_ref.at[pl.ds(g0, un), lane][t : t + 1, :])
                        b[j] = a * (qv * dy_ref.at[pl.ds(g0, un), lane][t : t + 1, :] + b[j])
                return tuple(b)

            b = lax.fori_loop(0, t_len // un, body, tuple(jnp.zeros((N, LANES), F32) for _ in range(nt)))
            for j in range(nt):
                c_src[layer, :, pl.ds(e0 + LANES * j, LANES)] = b[j].astype(BF)
            return carry

        lax.fori_loop(0, inner // ec, chunk, 0)
        load("dec", layer).wait()
        cr = Carry(sec, me, n, c_src.at[layer], c_recv.at[layer], c_pre.at[layer], c_dst.at[layer],
                   [s.at[layer] for s in (c1, c2, c3, c4)], L["dec"], inner)
        carries.append(cr)
        cr.send()
        if layer == 1:
            o_wait(2 * sec + 1 - x)
            o_copy(2).start()
        else:
            grad_go(0)
        cr.combine()
        if layer == 0:
            grad_gx(1, 0)
            grad_gx(1, 1)
        steps = t_len // BT

        def s_copy(blk, slot, layer=layer):
            return pltpu.make_async_copy(
                hbm[layer]["s"].at[pl.ds(pl.multiple_of(blk * BT * N, BT * N), BT * N), :], sbuf.at[slot],
                s_sem.at[slot])

        s_copy(steps - 1, 0).start()
        for name in ("proj", "beta", "us", "sb"):
            load(name, layer).wait()
        cr.get()
        bst[...] = c_dst[layer].astype(F32)
        if layer == 0:
            begin(1, "gx")
            advance(1, "go", "gz", "vec", "sm")
        ops[layer]["dz"].send()
        if layer == 1:
            grad_go(1)
        begin(layer, "go")

        def block(i, carry, L=L, vec=vec, s_copy=s_copy, dy_ref=dy_ref):
            blk = steps - 1 - i
            slot = lax.rem(i, 2)
            base = pl.multiple_of(blk * BT, BT)
            rows = pl.ds(base, BT)
            rbase = pl.multiple_of(blk * BT * N, BT * N)

            @pl.when(i + 1 < steps)
            def _():
                s_copy(blk - 1, 1 - slot).start()

            s_copy(blk, slot).wait()
            projb = L["proj"][rows, :]
            pf = projb.astype(F32)
            cols = iota((BT, LANES), 1)
            is_k = (cols >= rank) & (cols < rank + N)
            ksum = jnp.sum(jnp.where(is_k, pf * pf, 0.0), axis=-1, keepdims=True)
            kbd = block_diag(projb, rank)
            k2bd = (kbd * kbd).astype(BF)
            kbd = kbd.astype(BF)
            r1 = jnp.zeros((BT, BT * N), F32)
            r2 = jnp.zeros((BT, BT * N), F32)
            r3 = jnp.zeros((BT, BT * N), F32)
            s_blk = sbuf.at[slot]
            for ci in range(inner // ec):
                e0 = ci * ec
                qs, ws = qs2.at[ci % 2], ws2.at[ci % 2]
                b = [bst[:, pl.ds(e0 + LANES * j, LANES)] for j in range(nt)]
                for t in range(BT - 1, -1, -1):
                    row = slice(t * N, (t + 1) * N)
                    krow = pl.ds(pl.multiple_of(rbase + t * N, N), N)
                    k2 = L["k2"][krow, :]
                    qv = L["qb"][krow, :]
                    for j in range(nt):
                        lane = pl.ds(e0 + LANES * j, LANES)
                        a = jnp.exp2(k2 * L["ex"].at[rows, lane][t : t + 1, :])
                        q = qv * dy_ref.at[rows, lane][t : t + 1, :] + b[j]
                        b[j] = a * q
                        prev = s_blk[(t - 1) * N : t * N, lane] if t > 0 else L["sb"][rows, lane]
                        qs[row, LANES * j : LANES * (j + 1)] = q.astype(BF)
                        ws[row, LANES * j : LANES * (j + 1)] = (b[j] * prev.astype(F32)).astype(BF)
                for j in range(nt):
                    bst[:, pl.ds(e0 + LANES * j, LANES)] = b[j]
                at = pl.ds(e0, ec)
                p1 = dot(kbd, qs[...])
                p2 = dot(k2bd, ws[...])
                c = L["c"][rows, at]
                beta = L["beta"][rows, at]
                eps = beta / (1.0 + beta * ksum)
                dy = dy_ref[rows, at]
                deps[rows, at] = (c * jax.nn.sigmoid(c)) * p1 - p2
                dxc[rows, at] = dy * vec[6:7, at] + eps * p1
                r1 = r1 + dot_nt(L["us"][rows, at].astype(BF), qs[...])
                r2 = r2 + dot_nt(eps.astype(BF), ws[...])
                r3 = r3 + dot_nt(dy.astype(BF), s_blk[:, at])
            same = iota((BT, BT * N), 0) == iota((BT, BT * N), 1) // N
            gather_k = (iota((BT * N, LANES), 1) == rank + iota((BT * N, LANES), 0) % N).astype(F32)
            gather_q = (iota((BT * N, LANES), 1) == rank + N + iota((BT * N, LANES), 0) % N).astype(F32)

            def pick(r, g):
                return jnp.dot(
                    jnp.where(same, r, 0.0), g, precision=lax.Precision.HIGHEST, preferred_element_type=F32)

            dkq[rows, :] = pick(r1, gather_k) - 2.0 * pf * pick(r2, gather_k) + pick(r3, gather_q)
            return carry

        def tick(k, layer=layer):
            if layer == 1:
                if k == 2:
                    grad_gz(1)
                return
            if k == 1:
                advance(1, "sm")
            if k == 2:
                grad_gz(0)
            if k == 3:
                advance(1, "gz", "gx", "sm", "vec")

        def block_and_tick(i, carry):
            block(i, carry)
            for k in range(4):
                @pl.when(i == (k + 1) * steps // 4 - 1)
                def _(k=k):
                    tick(k)

            return carry

        lax.fori_loop(0, steps, block_and_tick, 0)
        if layer == 1:
            for name in ("k2", "qb", "ex", "us"):
                load(name, 0).start()
        load("xi", layer).wait()
        projw = L["proj"][...]
        pw = projw.astype(F32)
        colw = iota((t_len, LANES), 1)
        kall = jnp.where((colw >= rank) & (colw < rank + N), pw, 0.0)
        ks = jnp.sum(kall * kall, axis=-1, keepdims=True)
        tc = 256
        def first(k, carry, L=L, dtp=dtp, layer=layer, projw=projw, ks=ks):
            dkc, ddt = carry
            at = pl.ds(pl.multiple_of(k * tc, tc), tc)
            beta = L["beta"][:, at]
            inv = 1.0 / (1.0 + beta * ks)
            dq = deps[:, at] * (inv * inv)
            dkc = dkc + jnp.sum(dq * beta * beta, axis=-1, keepdims=True)
            dp = (dq * beta * (1.0 - beta)).astype(BF)
            vacc[layer, 5:6, at] = jnp.sum(dp.astype(F32), axis=0, keepdims=True)
            gdt_ref[:, at] = dot_tn(projw, dp)[:rank]
            ddt = ddt + dot_nt(dp, dtp[:, at])
            return dkc, ddt

        dkc, ddt = lax.fori_loop(
            0, inner // tc, first, (jnp.zeros((t_len, 1), F32), jnp.zeros((t_len, LANES), F32)))
        dproj = (jnp.where(colw < rank, ddt, dkq[...]) - 2.0 * kall * dkc).astype(BF)
        mask = mask_ref[...]

        def rim_copy(to, layer=layer):
            return pltpu.make_async_remote_copy(
                src_ref=rims.at[layer], dst_ref=rimr.at[layer], send_sem=rim_sem.at[layer], recv_sem=rimr_sem.at[layer],
                device_id=(sec, to), device_id_type=MESH)

        for k in range(n_out):
            at = pl.ds(k * cb, cb)
            der = silu_parts(L["c"][0:BT, at])[1]
            dc = (dxc[0:BT, at] + dot(dproj[0:BT], xp[:, at])) * der
            rim = jnp.zeros((8, cb), F32)
            for j in range(3):
                m = dc[0:8] * mask[0:8, j : j + 1] * vec[j : j + 1, at]
                rim = rim + jnp.concatenate([jnp.zeros((8, cb), F32), m], axis=0)[8 - j : 16 - j]
            rims[layer, :, at] = jnp.where(iota((8, cb), 0) < 3, rim, 0.0)

        @pl.when(me > 0)
        def _():
            rim_copy(me - 1).start()

        @pl.when(me == n - 1)
        def _():
            rimr[layer] = jnp.zeros(rimr.shape[1:], F32)

        per_part = half_in // 2 // tc

        def add_rim(p, layer=layer):
            for hf in range(2):
                at = pl.ds(hf * half_in + p * half_in // 2, half_in // 2)
                rows = pl.ds(t_len - BT, BT)
                edge = jnp.concatenate([jnp.zeros((BT - 3, half_in // 2), F32), rimr[layer, 0:3, at]], axis=0)
                dx_both[layer, rows, at] = (deps[rows, at] + edge).astype(BF)
            ops[layer]["dx0" if p == 0 else "dx1"].send()

        def second(i, carry, L=L, xp=xp, layer=layer, dproj=dproj, ck_ref=vec):
            p, left = i // (2 * per_part), lax.rem(i, 2 * per_part)
            k = left // per_part * (half_in // tc) + p * per_part + lax.rem(left, per_part)
            at = pl.ds(pl.multiple_of(k * tc, tc), tc)
            c = L["c"][:, at]
            act, der = silu_parts(c)
            gxp = dot_tn(act.astype(BF), dproj).astype(BF)
            for r in range(tc // rows_sm):
                j = k * (tc // rows_sm) + r
                bufs[layer]["sm"][(0,) + unpack_index(j, bits)] = gxp[r * rows_sm : (r + 1) * rows_sm]
            dc = (dxc[:, at] + dot(dproj, xp[:, at])) * der
            vacc[layer, 4:5, at] = jnp.sum(dc, axis=0, keepdims=True)
            xi = L["xi"][:, at]
            pad = jnp.zeros((8, tc), F32)
            dxi = ck_ref[3:4, at] * dc
            vacc[layer, 3:4, at] = jnp.sum(dc * xi[lead:], axis=0, keepdims=True)
            for j in range(3):
                m = dc * mask[:, j : j + 1]
                vacc[layer, j : j + 1, at] = jnp.sum(m * xi[lead - 3 + j : lead - 3 + j + t_len], axis=0, keepdims=True)
                ext = jnp.concatenate([m * ck_ref[j : j + 1, at], pad], axis=0)
                dxi = dxi + ext[3 - j : 3 - j + t_len]
            dx_both[layer, :, at] = dxi.astype(BF)
            deps[pl.ds(t_len - BT, BT), at] = dxi[t_len - BT :]

            @pl.when(i == 2 * per_part - 1)
            def _():
                @pl.when(me < n - 1)
                def _():
                    rim_copy(me).wait_recv()

                add_rim(0)

            return carry

        lax.fori_loop(0, inner // tc, second, 0)
        add_rim(1)
        if layer == 1:
            for name in ("c", "beta", "xi", "y"):
                load(name, 0).start()
        prow = rank // n
        for j in range(n):
            for t in range(inner // LANES):
                gtmp[j, t * prow : (t + 1) * prow, :] = gdt_ref[j * prow : (j + 1) * prow, t * LANES : (t + 1) * LANES]
        drow = prow * (inner // LANES)
        for j in range(n):
            bufs[layer]["sm"][(1,) + owner(j, bits) + (slice(0, drow),)] = gtmp[j, 0:drow].astype(BF)
        begin(layer, "sm")
        advance(layer, "go")
        du = jnp.zeros((t_len, width), F32)

        def project(du, i, g, layer=layer):
            slot = i % slots
            arrive(lambda src: in_chunk(in_order[i], slot, src), in_own)
            du = du + dot_nt(g, w_in[slot])
            if i + slots < n_in:
                fetch(layer, lambda src: in_chunk(in_order[i + slots], slot, src), in_own, in_oth)
            elif layer == 1:
                fetch(0, lambda src: in_chunk(in_order[i + slots - n_in], slot, src), in_own, in_oth)
            return du

        for i in range(n_in // 2):
            du = project(du, i, dz_ref[:, pl.ds(i * cb, cb)])

        if layer == 0:
            advance(1, "gx", "sm")
        advance(layer, "gz", "sm")
        for i in range(n_in // 2, n_in):
            du = project(du, i, dx_both[layer, :, pl.ds((i - n_in // 2) * cb, cb)])
        advance(layer, "go")
        if layer == 0:
            advance(1, "gx")
            advance(0, "gz", "sm")
        load("h", layer).wait()
        hf = L["h"][...].astype(F32)
        inv = lax.rsqrt(jnp.mean(hf * hf, axis=-1, keepdims=True) + NORM_EPS)
        unit = hf * inv
        vacc[layer, 7:8, pl.ds(0, width)] = jnp.sum(du * unit, axis=0, keepdims=True)
        dn = du * vec[7:8, 0:width]
        dh = g_ref[...].astype(F32) + inv * (dn - unit * jnp.mean(dn * unit, axis=-1, keepdims=True))
        if layer == 1:
            g_both[0] = dh.astype(BF)
            ops[0]["dr"].send()
        else:
            dh_out[...] = dh.astype(BF)
        vecs[layer].begin()

    parts0 = subs[0]["gx"]
    half0 = len(parts0) // 2
    grad_gx(0, 0)
    for s in parts0[:half0]:
        s.begin()
    advance(0, "vec", "sm")
    grad_gx(0, 1)
    for s in parts0[half0:]:
        s.begin()
    advance(0, "go", "gz")
    for _ in range(bits - 1):
        for s in parts0[:half0]:
            s.advance()
        advance(0, "sm", "go", "gz")
        for s in parts0[half0:]:
            s.advance()
        advance(0, "vec")
    left = [s for layer in range(2) for v in subs[layer].values() for s in v]
    while any(s.stage <= s.last for s in left):
        for s in left[::-1]:
            s.advance()
    for k in range(3):
        o_copy(k).wait_send()
    for v in vecs:
        v.drain()
    for s in left:
        s.finish()
    for layer in range(2):
        for g in ops[layer].values():
            g.sent()

    @pl.when(me > 0)
    def _():
        for layer in range(2):
            pltpu.make_async_remote_copy(
                src_ref=rims.at[layer], dst_ref=rimr.at[layer], send_sem=rim_sem.at[layer], recv_sem=rimr_sem.at[layer],
                device_id=(sec, me - 1), device_id_type=MESH).wait_send()

    for cr in carries:
        cr.sent()


def backward(n, rank, cid, tokens, cot, mask, in_own, in_oth, out_own, out_oth, saved, vec2, xp2, dtp2):
    t_len, width = cot.shape[1:]
    inner = out_own.shape[0]
    bits = n.bit_length() - 1
    lead = saved[0]["xi"].shape[0] - t_len
    args = [tokens, cot, mask, in_own, in_oth, out_own, out_oth]
    specs = [ANYSPEC, ANYSPEC, VSPEC] + [ANYSPEC] * 4
    for layer in range(2):
        args += [saved[layer][name] for name in LOADS + ("s", "ut4", "ot4")]
        specs += [ANYSPEC] * (len(LOADS) + 3)
    args += [vec2, xp2, dtp2]
    specs += [VSPEC] * 3
    rows_go, rows_in, rows_sm = inner // n, width // n, inner // n

    def sd(t, *s):
        return jax.ShapeDtypeStruct(s, t)

    outs = [
        sd(BF, t_len, width), sd(F32, rows_in, 2 * inner), sd(F32, rows_go, width), sd(F32, 2, rows_sm, LANES),
        sd(F32, 16, LANES),
    ]
    scratch = []
    for name in LOADS:
        a = saved[0][name]
        scratch += [pltpu.VMEM(a.shape, a.dtype)] * (2 if name in BOTH else 1)
    slots = 4
    scratch += [
        pltpu.VMEM((2, t_len, width), BF), pltpu.VMEM((inner, width), BF), pltpu.VMEM((slots, width, 512), BF),
        pltpu.VMEM((2, BT * N, inner), BF), pltpu.VMEM((2, BT * N, 512), BF), pltpu.VMEM((2, BT * N, 512), BF),
        pltpu.VMEM((N, inner), F32), pltpu.VMEM((t_len, inner), F32),
        pltpu.VMEM((t_len, LANES), F32), pltpu.VMEM((t_len, inner), F32), pltpu.VMEM((2, t_len, inner), BF),
        pltpu.VMEM((2, t_len, inner), BF),
        pltpu.VMEM((rank, inner), F32), pltpu.VMEM((n, max(8, rank * inner // (LANES * n)), LANES), F32),
        pltpu.VMEM((2, 8, inner), F32), pltpu.VMEM((2, 8, inner), F32),
    ]
    scratch += [
        pltpu.VMEM((2, n // 2, rows_in, 4 * t_len), BF), pltpu.VMEM((2, n // 2, rows_go, 4 * t_len), BF),
        pltpu.VMEM((2, 4, t_len, width // 2), BF), pltpu.VMEM((2, 4, t_len, inner // 2), BF),
        pltpu.VMEM((2, 4, t_len, inner // 2), BF),
    ]
    dims = (("go", rows_go, width // 2), ("gz", rows_in, inner // 2), ("gx", rows_in, inner // 2), ("sm", rows_sm, LANES))
    for _ in range(2):
        for name, r, ln in dims:
            count = bits + 1 if name == "sm" else bits - 1
            scratch.append(pltpu.VMEM((2,) * count + (r, ln), BF))
    for _ in range(2):
        for name, r, ln in dims:
            count = bits + 1 if name == "sm" else bits - 1
            scratch += [pltpu.VMEM((2,) * (count - 1 - q) + (r, ln), BF) for q in range(count)]
    scratch += [pltpu.VMEM((r, ln), F32) for _, r, ln in dims]
    scratch += [pltpu.VMEM((2, 8, inner), F32)] * 2 + [pltpu.VMEM((n, 16, LANES), F32)] * 2
    scratch += [
        pltpu.VMEM((2, N, inner), BF), pltpu.VMEM((2, n, N, LANES), BF), pltpu.VMEM((2, n, N, LANES), BF),
        pltpu.VMEM((2, N, inner), BF),
    ]
    nsub = 1 + 2 + 2 + 4
    dma = pltpu.SemaphoreType.DMA
    scratch += [
        dma((len(LOADS), 2)), dma(()), dma((inner // 512,)), dma((slots,)), dma((2,)), dma((2,)), dma((2,)), dma((2, 2)),
        dma((2, 4, 3)), dma((2, 4, 4)), dma((2, nsub, bits + 1)), dma((2, nsub, bits + 1)),
        dma((2, nsub)), dma((2, nsub)), dma((2,)), dma((2,)), dma((2, n)), dma((2, n)), dma((3,)), dma((4,)),
        dma((2, n)), dma((2, n)), dma((2, n)), dma((2, n)),
    ]
    return pl.pallas_call(
        functools.partial(back_kernel, n, rank, {"lead": lead}),
        out_shape=outs,
        in_specs=specs,
        out_specs=[VSPEC] * len(outs),
        scratch_shapes=scratch,
        compiler_params=pltpu.CompilerParams(
            vmem_limit_bytes=63 * MIB, collective_id=cid, has_side_effects=True),
        name="backward",
    )(*args)


def finish_kernel(n, rank, used, hout, dh, g_in, g_out, g_sm, g_vec, *refs):
    o_h, o_dh, o_gain, o_in, o_ck, o_cb, o_xp, o_dt, o_dtb, o_skip, o_out, v0, v1, v2, v3, sems = refs
    moves = ((hout, v0, o_h), (dh, v1, o_dh), (g_in, v2, o_in), (g_out, v3, o_out))
    loads = [pltpu.make_async_copy(a, v, sems.at[i]) for i, (a, v, _) in enumerate(moves)]
    stores = [pltpu.make_async_copy(v, b.at[0], sems.at[i]) for i, (_, v, b) in enumerate(moves)]
    for cp in loads:
        cp.start()
    me = lax.axis_index("ctx")
    inner = o_dt.shape[2]
    o_xp[0] = g_sm[0].T[0:used]
    prow = rank // n
    for t in range(inner // LANES):
        o_dt[0, :, t * LANES : (t + 1) * LANES] = g_sm[1, t * prow : (t + 1) * prow, :]

    def pick(size, body):
        for l0 in range(0, LANES, size):
            @pl.when(lax.rem(me * size, LANES) == l0)
            def _():
                body(slice(l0, l0 + size))

    def vectors(at):
        o_ck[0] = g_vec[0:4, at]
        o_cb[...] = g_vec[4:5, at]
        o_dtb[...] = g_vec[5:6, at]
        o_skip[...] = g_vec[6:7, at]

    def gain(at):
        o_gain[...] = g_vec[15:16, at]

    pick(o_cb.shape[1], vectors)
    pick(o_gain.shape[1], gain)
    for a, b in zip(loads, stores):
        a.wait()
        b.start()
    for cp in stores:
        cp.wait()


def finish(n, rank, used, hout, dh, g_in, g_out, g_sm, g_vec):
    t_len, width = hout.shape
    inner = g_in.shape[1] // 2
    part = inner // n

    def f32(*s):
        return jax.ShapeDtypeStruct((1,) + s, F32)

    whole = jax.ShapeDtypeStruct((1, t_len, width), BF)
    return tuple(pl.pallas_call(
        functools.partial(finish_kernel, n, rank, used),
        out_shape=[
            whole, whole, f32(width // n), f32(*g_in.shape), f32(4, part), f32(part), f32(used, part),
            f32(rank // n, inner), f32(part), f32(part), f32(*g_out.shape),
        ],
        in_specs=[ANYSPEC] * 4 + [VSPEC] * 2,
        out_specs=[ANYSPEC, ANYSPEC, VSPEC, ANYSPEC] + [VSPEC] * 6 + [ANYSPEC],
        scratch_shapes=[pltpu.VMEM(a.shape, a.dtype) for a in (hout, dh, g_in, g_out)] + [pltpu.SemaphoreType.DMA((4,))],
        compiler_params=pltpu.CompilerParams(vmem_limit_bytes=60 * MIB),
        name="finish",
    )(hout, dh, g_in, g_out, g_sm, g_vec))


def on_device(
    tokens, cotangent, bounds, norm_gain, in_proj, conv_kernel, conv_bias, x_proj, dt_proj, dt_bias, skip_gain, out_proj
):
    sec = lax.axis_index("section")
    n = lax.axis_size("ctx")
    me = lax.axis_index("ctx")
    rank = dt_proj.shape[1]
    inner = out_proj.shape[1]
    used = x_proj.shape[2]
    in_own, out_own = in_proj[0], out_proj[0]
    smalls = (norm_gain, conv_kernel[0], conv_bias, dt_bias, skip_gain, x_proj[0].T, dt_proj[0])
    first, saved = forward(n, rank, 1, bounds, tokens, smalls, in_own, out_own)
    in_oth, out_oth, mask, xp2, dtp2, vec2, hmid, hout = first
    saved[0]["h"] = saved[1]["h"] = hmid
    dh, g_in, g_out, g_sm, g_vec = backward(
        n, rank, 2, tokens, cotangent, mask, in_own, in_oth, out_own, out_oth, saved, vec2, xp2, dtp2)
    outs = finish(n, rank, used, hout, dh, g_in, g_out, g_sm, g_vec)
    return outs[:6] + (outs[6].transpose(0, 2, 1),) + outs[7:]


def solution(mesh):
    placed = (
        P(None, "ctx", None), P(None, "ctx", None), P(), P("section", None), P("section"),
        P("section"), P("section", None), P("section"), P("section"),
        P("section", None), P("section", None), P("section"),
    )
    return jax.shard_map(
        on_device,
        mesh=mesh,
        in_specs=placed,
        out_specs=(
            P("section", "ctx", None), P("section", "ctx", None), P("section", "ctx"), P("section", "ctx", None),
            P("section", None, "ctx"), P("section", "ctx"), P("section", "ctx", None), P("section", "ctx", None),
            P("section", "ctx"), P("section", "ctx"), P("section", "ctx", None),
        ),
        check_vma=False,
    )
```
